32 devices in a mesh: dp: 8 (over z, y), seq: 4 (over x, core).
Axes of the slice: x: 2, y: 2, z: 4, core: 2. Of those that a mesh axis runs over, the one named last changes fastest.
Arguments:
- frames: bfloat16 [8, 640, 1024], P('dp', 'seq'), may hold values from -6 to 6
- cotangent: bfloat16 [8, 640, 1024], P('dp', 'seq'), may hold values from -6 to 6
- text_states: bfloat16 [8, 256, 768], P('dp'), may hold values from -6 to 6
- frame_start: int32 [8], P('dp'), may hold values from 0 to 319
- prompt_len: int32 [8], P('dp'), may hold values from 16 to 256, as said below
- w_query: bfloat16 [1024, 1024], P(('dp', 'seq')), may hold values from -0.1875 to 0.1875
- w_key: bfloat16 [1024, 1024], P(('dp', 'seq')), may hold values from -0.1875 to 0.1875
- w_value: bfloat16 [1024, 1024], P(('dp', 'seq')), may hold values from -0.1875 to 0.1875
- w_out: bfloat16 [1024, 1024], P(('dp', 'seq')), may hold values from -1.5 to 1.5
- c_query: bfloat16 [1024, 1024], P(('dp', 'seq')), may hold values from -0.1875 to 0.1875
- c_key: bfloat16 [1024, 1024], P(('dp', 'seq')), may hold values from -0.1875 to 0.1875
- c_value: bfloat16 [1024, 1024], P(('dp', 'seq')), may hold values from -0.1875 to 0.1875
- c_out: bfloat16 [1024, 1024], P(('dp', 'seq')), may hold values from -0.5 to 0.5
- w_text: bfloat16 [768, 1024], P(('dp', 'seq')), may hold values from -0.21875 to 0.21875
- w_up: bfloat16 [1024, 4096], P(('dp', 'seq')), may hold values from -0.1875 to 0.1875
- w_down: bfloat16 [4096, 1024], P(('dp', 'seq')), may hold values from -0.09375 to 0.09375
- gain_attn: bfloat16 [1024], P(('dp', 'seq')), may hold values from 0.25 to 1.75
- bias_attn: bfloat16 [1024], P(('dp', 'seq')), may hold values from -3 to 3
- gain_cross: bfloat16 [1024], P(('dp', 'seq')), may hold values from 0.25 to 1.75
- bias_cross: bfloat16 [1024], P(('dp', 'seq')), may hold values from -3 to 3
- gain_feed: bfloat16 [1024], P(('dp', 'seq')), may hold values from 0.25 to 1.75
- bias_feed: bfloat16 [1024], P(('dp', 'seq')), may hold values from -3 to 3
Outputs:
- block_out: bfloat16 [8, 640, 1024], P('dp', 'seq')
- frames_grad: bfloat16 [8, 640, 1024], P('dp', 'seq')
- text_grad: float32 [8, 256, 768], P('dp', 'seq')
- dw_query: float32 [1024, 1024], P(('dp', 'seq'))
- dw_key: float32 [1024, 1024], P(('dp', 'seq'))
- dw_value: float32 [1024, 1024], P(('dp', 'seq'))
- dw_out: float32 [1024, 1024], P(('dp', 'seq'))
- dc_query: float32 [1024, 1024], P(('dp', 'seq'))
- dc_key: float32 [1024, 1024], P(('dp', 'seq'))
- dc_value: float32 [1024, 1024], P(('dp', 'seq'))
- dc_out: float32 [1024, 1024], P(('dp', 'seq'))
- dw_text: float32 [768, 1024], P(('dp', 'seq'))
- dw_up: float32 [1024, 4096], P(('dp', 'seq'))
- dw_down: float32 [4096, 1024], P(('dp', 'seq'))
- dgain_attn: float32 [1024], P(('dp', 'seq'))
- dbias_attn: float32 [1024], P(('dp', 'seq'))
- dgain_cross: float32 [1024], P(('dp', 'seq'))
- dbias_cross: float32 [1024], P(('dp', 'seq'))
- dgain_feed: float32 [1024], P(('dp', 'seq'))
- dbias_feed: float32 [1024], P(('dp', 'seq'))
The draws below stay inside these ranges and needn't reach their ends.
Inputs may be any that keep to these rules, and one draw needn't show every extreme that they name: Each item's prompt holds prompt_len tokens at the front of its 256 slots; most hold 16 to 32, a few more, and some item holds exactly 256. frames before frame_start are padding: no other frame attends to them.
All inputs are finite; a program needn't handle non-finite values.
Results may differ from the reference program's by a relative error of at most 0.018.
Values may be sent and summed in bfloat16 or wider, within the bound.
A program may use at most 320 MiB of HBM per device.

```python
import jax
import jax.numpy as jnp
from jax import lax

D = 1024
HEADS = 16
FF = 4096
TD = 768
TEXT = 256
ITEMS_DEV = 1
FRAMES = 640
ITEMS = 8


def draw_prompt_len(key, part):
    key_short, key_long, key_pick, key_top = jax.random.split(jax.random.fold_in(key, 17), 4)
    short_len = jax.random.randint(key_short, (ITEMS,), 16, 33)
    long_len = jax.random.randint(key_long, (ITEMS,), 33, TEXT + 1)
    picked = jax.random.randint(key_pick, (ITEMS,), 0, 8) == 0
    lengths = jnp.where(picked, long_len, short_len)
    top_item = jax.random.randint(key_top, (), 0, ITEMS)
    return jnp.where(jnp.arange(ITEMS) == top_item, TEXT, lengths).astype(jnp.int32)


def touch_ends(entries, rng, smallest, high):
    extent = entries.shape
    spot = [jax.random.randint(jax.random.fold_in(rng, axis), (), 0, extent[axis]) for axis in range(len(extent))]
    entries = entries.at[tuple(spot)].set(smallest)
    longest = extent.index(max(extent))
    spot[longest] = (spot[longest] + 1) % extent[longest]
    return entries.at[tuple(spot)].set(high)


def strengthened(array, key, source, target, parts, factor):
    def block_of(dim):
        return (jnp.arange(array.shape[dim]) // (array.shape[dim] // parts)).reshape((-1,) + (1,) * (array.ndim - 1 - dim))

    first = jax.random.permutation(key, parts)[block_of(target)]
    second = (block_of(target) + parts // 2) % parts
    return jnp.where((block_of(source) == first) | (block_of(source) == second), factor * array, array)


def levels(stream_key, shape, pieces, smallest, high):
    def one(dim, parts):
        steps = jax.random.uniform(jax.random.fold_in(jax.random.fold_in(stream_key, 6), dim), (parts,), jnp.float32, smallest / len(pieces), high / len(pieces))
        return jnp.repeat(jnp.exp(steps), shape[dim] // parts).reshape((-1,) + (1,) * (len(shape) - dim - 1))

    loudness = one(*pieces[0])
    for cut in pieces[1:]:
        loudness = loudness * one(*cut)
    return loudness


def gaussian(stream_key, dims, deviation, most, cuts=(), dtype=jnp.bfloat16):
    values = jax.random.normal(stream_key, dims, jnp.float32) * deviation
    if len(cuts) > 0:
        values = levels(stream_key, dims, cuts, -0.22, 0.18) * values
    return jnp.clip(values, min=-most, max=most).astype(dtype)


def gaussian_with(stream_key, extent, deviation, limit, cuts, heavy, kind=jnp.bfloat16):
    array = deviation * jax.random.normal(stream_key, extent, jnp.float32)
    if cuts:
        array = array * levels(stream_key, extent, cuts, -0.22, 0.18)
    return jnp.clip(strengthened(array, jax.random.fold_in(stream_key, 3), *heavy), -limit, limit).astype(kind)


def setup_inputs(seed: int = 0) -> dict:
    seeds = jax.random.split(jax.random.key(seed), 23)
    return {
        "frames": gaussian_with(seeds[0], (ITEMS, FRAMES, D), 1.0, 6.0, ((0, 8), (1, 4)), (0, 2, 8, 2.0)),
        "cotangent": gaussian(seeds[1], (ITEMS, FRAMES, D), 1.0, 6.0, ((0, 8), (1, 4))),
        "text_states": gaussian(seeds[2], (ITEMS, TEXT, TD), 1.0, 6.0, ((0, 8),)),
        "frame_start": touch_ends(jax.random.randint(seeds[3], (ITEMS,), 0, FRAMES // 2), jax.random.fold_in(seeds[3], 1), 0, (FRAMES // 2) - 1).astype(jnp.int32),
        "prompt_len": draw_prompt_len(jax.random.fold_in(seeds[22], 71), 0),
        "w_query": gaussian(seeds[5], (D, D), D ** -0.5, 0.1875, ((0, 32),)),
        "w_key": gaussian(seeds[6], (D, D), D ** -0.5, 0.1875, ((0, 32),)),
        "w_value": gaussian(seeds[7], (D, D), D ** -0.5, 0.1875, ((0, 32),)),
        "w_out": gaussian(seeds[8], (D, D), (D // 64) ** -0.5, 1.5, ((0, 32),)),
        "c_query": gaussian(seeds[9], (D, D), D ** -0.5, 0.1875, ((0, 32),)),
        "c_key": gaussian(seeds[10], (D, D), D ** -0.5, 0.1875, ((0, 32),)),
        "c_value": gaussian(seeds[11], (D, D), D ** -0.5, 0.1875, ((0, 32),)),
        "c_out": gaussian(seeds[12], (D, D), (D // 8) ** -0.5, 0.5, ((0, 32),)),
        "w_text": gaussian(seeds[13], (TD, D), TD ** -0.5, 0.21875, ((0, 32),)),
        "w_up": gaussian(seeds[14], (D, FF), D ** -0.5, 0.1875, ((0, 32),)),
        "w_down": gaussian(seeds[15], (FF, D), FF ** -0.5, 0.09375, ((0, 32),)),
        "gain_attn": jnp.clip(1.0 + 0.15 * jax.random.normal(seeds[16], (D,), jnp.float32), 0.25, 1.75).astype(jnp.bfloat16),
        "bias_attn": gaussian(seeds[17], (D,), 0.3, 3.0, ((0, 32),)),
        "gain_cross": jnp.clip(1.0 + 0.15 * jax.random.normal(seeds[18], (D,), jnp.float32), 0.25, 1.75).astype(jnp.bfloat16),
        "bias_cross": gaussian(seeds[19], (D,), 0.3, 3.0, ((0, 32),)),
        "gain_feed": jnp.clip(1.0 + 0.15 * jax.random.normal(seeds[20], (D,), jnp.float32), 0.25, 1.75).astype(jnp.bfloat16),
        "bias_feed": gaussian(seeds[21], (D,), 0.3, 3.0, ((0, 32),)),
    }


@jax.custom_vjp
def low(v):
    return lax.optimization_barrier(v.astype(jnp.bfloat16)).astype(jnp.float32)

@jax.custom_vjp
def low_back(v):
    return v

def low_keep(v):
    return (low(v), None)

def low_pass(kept, grad):
    return (grad,)

def back_keep(v):
    return (v, None)

def back_low(kept, grad):
    return (low(grad),)
low.defvjp(low_keep, low_pass)
low_back.defvjp(back_keep, back_low)
eps_norm = 1e-05

def both_ways(values_in):
    return low(low_back(values_in))

def layer_norm(values_in, gain_vec, shift_vec):
    centre = values_in - lax.optimization_barrier(jnp.mean(values_in, axis=-1, keepdims=True))
    spread = lax.optimization_barrier(jnp.mean(centre * centre, axis=-1, keepdims=True))
    return centre * lax.rsqrt(spread + eps_norm) * gain_vec + shift_vec

def project(left, right):
    return jnp.einsum('gti,ij->gtj', left, right, precision=lax.Precision.HIGHEST)

def attend(query_rows, key_rows, value_rows, allowed):
    groups, row_count, model_width = query_rows.shape
    head_size = model_width // HEADS
    query_heads = query_rows.reshape(groups, row_count, HEADS, head_size)
    key_heads = key_rows.reshape(groups, key_rows.shape[1], HEADS, head_size)
    value_heads = value_rows.reshape(groups, value_rows.shape[1], HEADS, head_size)
    scores = jnp.einsum('gqhd,gkhd->ghqk', query_heads, key_heads, precision=lax.Precision.HIGHEST)
    scores = low_back(scores * head_size ** (-0.5))
    scores = jnp.where(allowed[:, None], scores, -1e+30)
    weights = low(jax.nn.softmax(scores, axis=-1))
    mixture = jnp.einsum('ghqk,gkhd->gqhd', weights, value_heads, precision=lax.Precision.HIGHEST)
    return both_ways(mixture.reshape(groups, row_count, model_width))

def forward(frames, text_rows, starts, lengths, params):
    w_query, w_key, w_value, w_out, c_query, c_key, c_value, c_out, w_text, w_up, w_down, gain_attn, bias_attn, gain_cross, bias_cross, gain_feed, bias_feed = params
    normed = low(layer_norm(frames, gain_attn, bias_attn))
    query_rows = both_ways(project(normed, w_query))
    key_rows = both_ways(project(normed, w_key))
    value_rows = both_ways(project(normed, w_value))
    position = jnp.arange(frames.shape[1])
    key_pos = position[None, None, :]
    query_pos = position[None, :, None]
    causal = (key_pos <= query_pos) & ((key_pos >= starts[:, None, None]) | (key_pos == query_pos))
    attended = attend(query_rows, key_rows, value_rows, causal)
    first = frames + low_back(project(attended, w_out))
    text_proj = both_ways(project(text_rows, w_text))
    normed_two = low(layer_norm(first, gain_cross, bias_cross))
    cross_query = both_ways(project(normed_two, c_query))
    cross_keys = both_ways(project(text_proj, c_key))
    cross_values = both_ways(project(text_proj, c_value))
    prompt_mask = jnp.arange(text_rows.shape[1])[None, None, :] < lengths[:, None, None]
    cross_mix = attend(cross_query, cross_keys, cross_values, prompt_mask)
    second = first + low_back(project(cross_mix, c_out))
    normed_three = low(layer_norm(second, gain_feed, bias_feed))
    hidden = low_back(project(normed_three, w_up))
    activated = low(jax.nn.gelu(hidden, approximate=False))
    return second + low_back(project(activated, w_down))

def reference(frames, cotangent, text_states, frame_start, prompt_len, w_query, w_key, w_value, w_out, c_query, c_key, c_value, c_out, w_text, w_up, w_down, gain_attn, bias_attn, gain_cross, bias_cross, gain_feed, bias_feed):
    params = tuple((weight.astype(jnp.float32) for weight in (w_query, w_key, w_value, w_out, c_query, c_key, c_value, c_out, w_text, w_up, w_down, gain_attn, bias_attn, gain_cross, bias_cross, gain_feed, bias_feed)))
    groups = ITEMS // ITEMS_DEV

    def regroup(array_in):
        return array_in.reshape((groups, ITEMS_DEV) + array_in.shape[1:])
    batches = (regroup(frames.astype(jnp.float32)), regroup(cotangent.astype(jnp.float32)), regroup(text_states.astype(jnp.float32)), regroup(frame_start), regroup(prompt_len))

    def step(totals, batch):
        frame_rows, cot_rows, text_rows, starts, lengths = batch

        def local(frame_in, text_in, param_in):
            return forward(frame_in, text_in, starts, lengths, param_in)
        result, pullback = jax.vjp(local, frame_rows, text_rows, params)
        grad_frames, grad_text, grad_params = pullback(cot_rows)
        totals = jax.tree.map(lambda left, right: left + right, totals, grad_params)
        return (totals, (result.astype(jnp.bfloat16), grad_frames.astype(jnp.bfloat16), grad_text))
    zeros_init = tuple((jnp.zeros_like(weight) for weight in params))
    totals, (results, grads_frames, grads_text) = lax.scan(step, zeros_init, batches)
    dw_query, dw_key, dw_value, dw_out, dc_query, dc_key, dc_value, dc_out, dw_text, dw_up, dw_down, dgain_attn, dbias_attn, dgain_cross, dbias_cross, dgain_feed, dbias_feed = totals
    block_out = results.reshape(frames.shape)
    frames_grad = grads_frames.reshape(frames.shape)
    text_grad = grads_text.reshape(text_states.shape)
    return (block_out, frames_grad, text_grad, dw_query, dw_key, dw_value, dw_out, dc_query, dc_key, dc_value, dc_out, dw_text, dw_up, dw_down, dgain_attn, dbias_attn, dgain_cross, dbias_cross, dgain_feed, dbias_feed)
```

```python
import functools
from typing import NamedTuple
import jax
import jax.numpy as jnp
from jax import lax
from jax.experimental import pallas as pl
from jax.experimental.pallas import tpu as pltpu
from jax.sharding import PartitionSpec as P

MESH = pl.DeviceIdType.MESH

LAG = 2
VMEM_LIMIT = 60 * 1024 * 1024

def unit_ops(perm, nz):
    rank = {a: i for i, a in enumerate(perm)}
    ops = {}

    def source(j, fy, fx):
        differs = [a for a, f in (("z", j > 0), ("y", fy), ("x", fx)) if f]
        if not differs:
            return None
        last = max(differs, key=lambda a: rank[a])
        if last == "z":
            return ("z", j - 1, fy, fx)
        if last == "y":
            return ("y", j, 0, fx)
        return ("x", j, fy, 0)

    for j in range(nz):
        for fy in range(2):
            for fx in range(2):
                for axis in "zyx":
                    flags = {"z": j > 0, "y": fy, "x": fx}
                    if axis != "z" and flags[axis]:
                        continue
                    if any(flags[a] and rank[a] > rank[axis] for a in "zyx" if a != axis):
                        continue
                    if axis == "z" and j == nz - 1:
                        continue
                    ops[(axis, j, fy, fx)] = source(j, fy, fx)
    return ops

def make_schedule(perms, nz, lag=LAG, window=None):
    ops = {}
    for u, perm in enumerate(perms):
        for key, dep in unit_ops(perm, nz).items():
            ops[(u,) + key] = None if dep is None else (u,) + dep
    children = {}
    for op, dep in ops.items():
        children.setdefault(dep, []).append(op)
    height = {}

    def tall(op):
        if op not in height:
            height[op] = 1 + max([tall(c) for c in children.get(op, [])], default=0)
        return height[op]

    for op in ops:
        tall(op)
    done, slots, left = {}, [], set(ops)
    while left:
        t = len(slots)
        slot = {}
        for axis in "zyx":
            ready = [op for op in left if op[1] == axis and (ops[op] is None or (ops[op] in done and done[ops[op]] + lag <= t))]
            if ready:
                slot[axis] = min(ready, key=lambda op: (op[0] // window if window else 0, -height[op], op[0], op))
        for axis, op in slot.items():
            done[op] = t
            left.discard(op)
        slots.append(slot)
    return slots

def nth_table(nz):
    rows = []
    for z in range(nz):
        offs = sorted((p - z for p in range(nz)), key=lambda o: (abs(o), o if z % 2 else -o))
        rows.append([z + o for o in offs])
    return rows

def pick(values, z):
    out = 0
    for i, v in enumerate(values):
        out = out + v * jnp.where(z == i, 1, 0)
    return out

UP, DOWN, YY, XX, CORE = range(5)
WAYS_OF = dict(z=(UP, DOWN), y=(YY,), x=(XX,))

class Place:
    def __init__(self, nz):
        d, s = lax.axis_index("dp"), lax.axis_index("seq")
        self.nz = nz
        self.z, self.y, self.x, self.c = d // 2, d % 2, s // 2, s % 2
        z, y, x, c = self.z, self.y, self.x, self.c
        self.device = [
            ((z + 1) * 2 + y, x * 2 + c),
            ((z - 1) * 2 + y, x * 2 + c),
            (z * 2 + 1 - y, x * 2 + c),
            (z * 2 + y, (1 - x) * 2 + c),
            (z * 2 + y, x * 2 + 1 - c),
        ]
        self.nth = [[row[j] for row in nth_table(nz)] for j in range(nz)]

    def greet(self):
        barrier = pltpu.get_barrier_semaphore()
        has_up, has_down = self.z + 1 < self.nz, self.z > 0
        for way in range(5):
            def hello(way=way):
                pl.semaphore_signal(barrier, inc=1, device_id=self.device[way], device_id_type=MESH)
            if way < YY:
                pl.when(has_up if way == UP else has_down)(hello)
            else:
                hello()
        edge = jnp.where(self.z == 0, 1, 0) + jnp.where(self.z == self.nz - 1, 1, 0)
        pl.semaphore_wait(barrier, 5 - edge)

    def gather_moves(self, axis, j, fy, fx):
        z, y, x, nz = self.z, self.y, self.x, self.nz
        py, px = (1 - y if fy else y), (1 - x if fx else x)
        if axis == "z":
            out = [(UP, (z - j >= 0) & (z + 1 < nz), (z - j, py, px)), (DOWN, (z + j < nz) & (z > 0), (z + j, py, px))]
            come = [(UP, z - 1 - j >= 0, (z - 1 - j, py, px)), (DOWN, z + 1 + j < nz, (z + 1 + j, py, px))]
        else:
            pz = pick(self.nth[j], z)
            there = (pz, 1 - y, px) if axis == "y" else (pz, py, 1 - x)
            way = YY if axis == "y" else XX
            out = [(way, None, (pz, py, px))]
            come = [(way, None, there)]
        return out, come

def when(cond, fn):
    if cond is None:
        fn()
    else:
        pl.when(cond)(fn)

def gather_body(nz, units, slots, n, depth, *refs):
    given, outs, rows_out = refs[:n + 1], refs[n + 1:2 * n + 1], refs[2 * n + 1]
    held = refs[2 * n + 2:3 * n + 3]
    ins, rows_in = held[:n], held[n]
    send_sem, recv_sem, core_send, core_recv, local_sem, rows_send, rows_recv = refs[3 * n + 3:]
    loads = [pltpu.make_async_copy(given[g], held[g], local_sem.at[g]) for g in range(n + 1)]
    for cp in loads:
        cp.start()
    here = Place(nz)
    z, y, x, c = here.z, here.y, here.x, here.c
    own = [pltpu.make_async_copy(ins[g], outs[g].at[z, y, x, c], local_sem.at[g]) for g in range(n)]
    own.append(pltpu.make_async_copy(rows_in, rows_out.at[x, c], local_sem.at[n]))
    here.greet()
    for cp in loads:
        cp.wait()
    for cp in own:
        cp.start()

    def rows_over(src, dst, way, i):
        return pltpu.make_async_remote_copy(
            src_ref=src, dst_ref=dst, send_sem=rows_send.at[i], recv_sem=rows_recv.at[i],
            device_id=here.device[way], device_id_type=MESH,
        )

    rows_moves = [
        rows_over(rows_in, rows_out.at[x, c], XX, 0),
        rows_over(rows_in, rows_out.at[x, c], CORE, 1),
        rows_over(rows_out.at[1 - x, c], rows_out.at[1 - x, c], CORE, 2),
    ]
    rows_moves[0].start()
    rows_moves[1].start()

    def piece(u, p):
        g, r0, rn, c0, cn = units[u]
        return outs[g].at[p[0], p[1], p[2], c, pl.ds(r0, rn), pl.ds(c0, cn)]

    def corner(u, fy, fx, which):
        g, r0, rn, c0, cn = units[u]
        return outs[g].at[:, 1 - y if fy else y, 1 - x if fx else x, which, pl.ds(r0, rn), pl.ds(c0, cn)]

    def remote(u, way, t, p, mine):
        i = way
        ref = piece(u, p)
        g, r0, rn, c0, cn = units[u]
        src = ins[g].at[pl.ds(r0, rn), pl.ds(c0, cn)] if mine else ref
        return pltpu.make_async_remote_copy(src_ref=src, dst_ref=ref, send_sem=send_sem.at[i, t], recv_sem=recv_sem.at[i, t], device_id=here.device[way], device_id_type=MESH)

    def across(u, fy, fx):
        ref = corner(u, fy, fx, c)
        i = fy * 2 + fx
        return pltpu.make_async_remote_copy(src_ref=ref, dst_ref=ref, send_sem=core_send.at[u, i], recv_sem=core_recv.at[u, i], device_id=here.device[CORE], device_id_type=MESH)

    last = {}
    for t, slot in enumerate(slots):
        for u, axis, j, fy, fx in slot.values():
            came = {"z": (u, fy, fx), "y": (u, 1, fx), "x": (u, fy, 1)}[axis]
            last[came] = t
    for t in range(len(slots) + depth):
        if t < len(slots):
            for axis, (u, _, j, fy, fx) in slots[t].items():
                for way, cond, p in here.gather_moves(axis, j, fy, fx)[0]:
                    when(cond, lambda u=u, way=way, p=p: remote(u, way, t, p, (j, fy, fx) == (0, 0, 0)).start())
        if t == depth - 1:
            for cp in own:
                cp.wait()
        if t == min(6, len(slots) - 1):
            arrived = rows_out.at[1 - x, c]
            pltpu.make_async_copy(arrived, arrived, rows_recv.at[0]).wait()
            rows_moves[2].start()
        if t >= depth:
            for axis, (u, _, j, fy, fx) in slots[t - depth].items():
                for way, cond, p in here.gather_moves(axis, j, fy, fx)[1]:
                    when(cond, lambda u=u, way=way, p=p: pltpu.make_async_copy(piece(u, p), piece(u, p), recv_sem.at[way, t - depth]).wait())
            for key in sorted(last):
                if last[key] == t - depth:
                    across(*key).start()
    for t, slot in enumerate(slots):
        for axis, (u, _, j, fy, fx) in slot.items():
            for way, cond, p in here.gather_moves(axis, j, fy, fx)[0]:
                when(cond, lambda u=u, way=way, p=p: remote(u, way, t, p, (j, fy, fx) == (0, 0, 0)).wait_send())
    for u, fy, fx in sorted(last):
        across(u, fy, fx).wait_send()
    for u, fy, fx in sorted(last):
        ref = corner(u, fy, fx, 1 - c)
        pltpu.make_async_copy(ref, ref, core_recv.at[u, fy * 2 + fx]).wait()
    for cp in rows_moves:
        cp.wait_send()
    for i, ref in ((1, rows_out.at[x, 1 - c]), (2, rows_out.at[1 - x, 1 - c])):
        pltpu.make_async_copy(ref, ref, rows_recv.at[i]).wait()

def gather_weights(arrays, frame_rows, units, perms, nz, window=None, depth=2):
    n = len(arrays)
    slots = make_schedule(perms, nz, lag=depth + 1, window=window)
    return pl.pallas_call(
        functools.partial(gather_body, nz, units, slots, n, depth),
        out_shape=[jax.ShapeDtypeStruct((nz, 2, 2, 2) + a.shape, a.dtype) for a in arrays]
        + [jax.ShapeDtypeStruct((2, 2) + frame_rows.shape, frame_rows.dtype)],
        in_specs=[pl.BlockSpec(memory_space=pl.ANY)] * (n + 1),
        out_specs=[pl.BlockSpec(memory_space=pl.ANY)] * (n + 1),
        scratch_shapes=[pltpu.VMEM(a.shape, a.dtype) for a in (*arrays, frame_rows)]
        + [
            pltpu.SemaphoreType.DMA((4, len(slots))),
            pltpu.SemaphoreType.DMA((4, len(slots))),
            pltpu.SemaphoreType.DMA((len(units), 4)),
            pltpu.SemaphoreType.DMA((len(units), 4)),
            pltpu.SemaphoreType.DMA((n + 1,)),
            pltpu.SemaphoreType.DMA((3,)),
            pltpu.SemaphoreType.DMA((3,)),
        ],
        compiler_params=pltpu.CompilerParams(collective_id=1, has_side_effects=True, vmem_limit_bytes=16 * 1024 * 1024),
        name="gather_weights",
    )(*arrays, frame_rows)


BACK = (DOWN, UP, YY, XX)


def scatter_body(nz, units, slots, n, depth, *refs):
    ins, out = refs[:n], refs[n]
    total, twin, landed, send_sem, recv_sem, core_send, core_recv, local_sem = refs[n + 1:]
    here = Place(nz)
    z, y, x, c = here.z, here.y, here.x, here.c
    steps = slots[::-1]
    numbers, order = {}, []
    for t, slot in enumerate(steps):
        for axis, op in slot.items():
            for way in WAYS_OF[axis]:
                numbers[way, t] = len(numbers)
            if op[0] not in order:
                order.append(op[0])

    def plane(u, which):
        g, r0, rn, c0, cn = units[u]
        return ins[g].at[:, :, :, which, pl.ds(r0, rn), pl.ds(c0, cn)]

    def local(u):
        return pltpu.make_async_copy(plane(u, c), total.at[u], local_sem.at[u])

    def across(u):
        return pltpu.make_async_remote_copy(
            src_ref=plane(u, 1 - c), dst_ref=twin.at[u], send_sem=core_send.at[u], recv_sem=core_recv.at[u],
            device_id=here.device[CORE], device_id_type=MESH,
        )

    def remote(u, way, t, p):
        i = numbers[way, t]
        return pltpu.make_async_remote_copy(
            src_ref=total.at[u, p[0], p[1], p[2]], dst_ref=landed.at[i], send_sem=send_sem.at[i], recv_sem=recv_sem.at[i],
            device_id=here.device[BACK[way]], device_id_type=MESH,
        )

    for u in order:
        local(u).start()
    here.greet()
    for u in order:
        across(u).start()

    def join(u):
        local(u).wait()
        across(u).wait_recv()

        @pl.loop(0, nz)
        def _(a):
            for b in range(2):
                for e in range(2):
                    total[u, a, b, e] = (
                        total[u, a, b, e].astype(jnp.float32) + twin[u, a, b, e].astype(jnp.float32)
                    ).astype(jnp.bfloat16)

    joined = set()
    for t in range(len(steps) + depth):
        if t < len(steps):
            for axis, (u, _, j, fy, fx) in steps[t].items():
                if u not in joined:
                    joined.add(u)
                    join(u)
                for way, cond, p in here.gather_moves(axis, j, fy, fx)[1]:
                    when(cond, lambda u=u, way=way, p=p: remote(u, way, t, p).start())
        if t >= depth:
            s = t - depth
            for axis, (u, _, j, fy, fx) in steps[s].items():
                for way, cond, p in here.gather_moves(axis, j, fy, fx)[0]:
                    def add(u=u, way=way, p=p):
                        i = numbers[way, s]
                        pltpu.make_async_copy(landed.at[i], landed.at[i], recv_sem.at[i]).wait()
                        total[u, p[0], p[1], p[2]] = (
                            total[u, p[0], p[1], p[2]].astype(jnp.float32) + landed[i].astype(jnp.float32)
                        ).astype(jnp.bfloat16)
                    when(cond, add)
    for u in range(len(units)):
        out[u] = total[u, z, y, x].astype(jnp.float32)
    for t, slot in enumerate(steps):
        for axis, (u, _, j, fy, fx) in slot.items():
            for way, cond, p in here.gather_moves(axis, j, fy, fx)[1]:
                when(cond, lambda u=u, way=way, p=p: remote(u, way, t, p).wait_send())
    for u in order:
        across(u).wait_send()


def scatter_grads(arrays, units, perms, nz, depth=2):
    n = len(arrays)
    slots = make_schedule(perms, nz, lag=depth + 1)
    count = sum(2 if axis == "z" else 1 for slot in slots for axis in slot)
    rows, columns = units[0][2], units[0][4]
    return pl.pallas_call(
        functools.partial(scatter_body, nz, units, slots, n, depth),
        out_shape=jax.ShapeDtypeStruct((len(units), rows, columns), jnp.float32),
        in_specs=[pl.BlockSpec(memory_space=pl.ANY)] * n,
        out_specs=pl.BlockSpec(memory_space=pltpu.VMEM),
        scratch_shapes=[
            pltpu.VMEM((len(units), nz, 2, 2, rows, columns), jnp.bfloat16),
            pltpu.VMEM((len(units), nz, 2, 2, rows, columns), jnp.bfloat16),
            pltpu.VMEM((count, rows, columns), jnp.bfloat16),
            pltpu.SemaphoreType.DMA((count,)),
            pltpu.SemaphoreType.DMA((count,)),
            pltpu.SemaphoreType.DMA((len(units),)),
            pltpu.SemaphoreType.DMA((len(units),)),
            pltpu.SemaphoreType.DMA((len(units),)),
        ],
        compiler_params=pltpu.CompilerParams(collective_id=2, has_side_effects=True, vmem_limit_bytes=VMEM_LIMIT),
        name="scatter_grads",
    )(*arrays)


def share_body(n, chunk, *refs):
    ins, outs = refs[:n], refs[n:2 * n]
    twins, sums, landed = refs[2 * n:3 * n], refs[3 * n:4 * n], refs[4 * n:5 * n]
    core_send, core_recv, x_send, x_recv = refs[5 * n:]
    d, s = lax.axis_index("dp"), lax.axis_index("seq")
    x, c = s // 2, s % 2
    core, over = (d, x * 2 + 1 - c), (d, (1 - x) * 2 + c)
    barrier = pltpu.get_barrier_semaphore()
    for other in (core, over):
        pl.semaphore_signal(barrier, inc=1, device_id=other, device_id_type=MESH)
    pl.semaphore_wait(barrier, 2)
    pieces = [(g, k, pl.ds(k * chunk, chunk)) for g in range(n) for k in range(ins[g].shape[2] // chunk)]

    def across(i, far):
        g, k, rows = pieces[i]
        part = 1 - x if far else x
        return pltpu.make_async_remote_copy(
            src_ref=ins[g].at[part, 1 - c, rows], dst_ref=twins[g].at[1 if far else 0, rows],
            send_sem=core_send.at[1 if far else 0, i], recv_sem=core_recv.at[1 if far else 0, i],
            device_id=core, device_id_type=MESH,
        )

    def beyond(i):
        g, k, rows = pieces[i]
        return pltpu.make_async_remote_copy(
            src_ref=sums[g].at[rows], dst_ref=landed[g].at[rows], send_sem=x_send.at[i], recv_sem=x_recv.at[i],
            device_id=over, device_id_type=MESH,
        )

    for far in (True, False):
        for i in range(len(pieces)):
            across(i, far).start()
    for i, (g, k, rows) in enumerate(pieces):
        across(i, True).wait_recv()
        sums[g][rows] = (ins[g][1 - x, c, rows].astype(jnp.float32) + twins[g][1, rows].astype(jnp.float32)).astype(jnp.bfloat16)
        beyond(i).start()
    for i, (g, k, rows) in enumerate(pieces):
        across(i, False).wait_recv()
        beyond(i).wait_recv()
        outs[g][rows] = (
            ins[g][x, c, rows].astype(jnp.float32) + twins[g][0, rows].astype(jnp.float32) + landed[g][rows].astype(jnp.float32)
        ).astype(jnp.bfloat16)
    for i in range(len(pieces)):
        across(i, True).wait_send()
        across(i, False).wait_send()
        beyond(i).wait_send()


def share_sums(arrays, number):
    n = len(arrays)
    chunk = 32
    count = sum(a.shape[2] // chunk for a in arrays)
    return pl.pallas_call(
        functools.partial(share_body, n, chunk),
        out_shape=[jax.ShapeDtypeStruct(a.shape[2:], a.dtype) for a in arrays],
        in_specs=[pl.BlockSpec(memory_space=pltpu.VMEM)] * n,
        out_specs=[pl.BlockSpec(memory_space=pltpu.VMEM)] * n,
        scratch_shapes=[pltpu.VMEM((2,) + a.shape[2:], a.dtype) for a in arrays]
        + [pltpu.VMEM(a.shape[2:], a.dtype) for a in arrays] * 2
        + [pltpu.SemaphoreType.DMA((2, count))] * 2
        + [pltpu.SemaphoreType.DMA((count,))] * 2,
        compiler_params=pltpu.CompilerParams(collective_id=number, has_side_effects=True, vmem_limit_bytes=32 * 1024 * 1024),
        name="share_sums",
    )(*arrays)


def deliver_body(units, text_rows, sums, *outs):
    for u, (g, r0, rn, c0, cn) in enumerate(units):
        if g == 8:
            outs[g][...] = sums[u, :text_rows]
            outs[-1][...] = sums[u, text_rows:text_rows + 8]
        else:
            outs[g][r0:r0 + rn, c0:c0 + cn] = sums[u]


def deliver(sums, units, text_rows, shapes):
    shapes = [(text_rows,) + s[1:] if g == 8 else s for g, s in enumerate(shapes)] + [(8, sums.shape[2])]
    return pl.pallas_call(
        functools.partial(deliver_body, units, text_rows),
        out_shape=[jax.ShapeDtypeStruct(s, sums.dtype) for s in shapes],
        compiler_params=pltpu.CompilerParams(vmem_limit_bytes=16 * 1024 * 1024),
        name="deliver",
    )(sums)


def pair_scores(bounds_ref, q, k, keep, causal):
    s = lax.dot_general(jnp.where(keep, q, 0), k, (((1,), (1,)), ((), ())), preferred_element_type=jnp.float32)
    col = lax.broadcasted_iota(jnp.int32, s.shape, 1)
    if causal:
        row = lax.broadcasted_iota(jnp.int32, s.shape, 0) + bounds_ref[0]
        seen = (col <= row) & ((col >= bounds_ref[1]) | (col == row))
    else:
        seen = col < bounds_ref[0]
    s = jnp.where(seen, s * 0.125, -1e30)
    e = jnp.exp(s - jnp.max(s, axis=1, keepdims=True))
    return e * (1.0 / jnp.sum(e, axis=1, keepdims=True))


def halves(width):
    lane = lax.broadcasted_iota(jnp.int32, (1, width), 1)
    return [(lane >= 64 * h) & (lane < 64 * h + 64) for h in range(width // 64)]


def attend_body(causal, bounds_ref, q_ref, k_ref, v_ref, out_ref):
    q, k, v = q_ref[...], k_ref[...], v_ref[...]
    out = None
    for keep in halves(q.shape[1]):
        p = pair_scores(bounds_ref, q, k, keep, causal)
        o = jnp.dot(p.astype(jnp.bfloat16), v, preferred_element_type=jnp.float32)
        out = o if out is None else jnp.where(keep, o, out)
    out_ref[...] = out.astype(jnp.bfloat16)


def attend_back_body(causal, bounds_ref, q_ref, k_ref, v_ref, g_ref, dq_ref, dk_ref, dv_ref):
    q, k, v, g = q_ref[...], k_ref[...], v_ref[...], g_ref[...]
    dq = dk = dv = None
    for keep in halves(q.shape[1]):
        p = pair_scores(bounds_ref, q, k, keep, causal)
        dp = lax.dot_general(jnp.where(keep, g, 0), v, (((1,), (1,)), ((), ())), preferred_element_type=jnp.float32)
        ds = (p * (dp - jnp.sum(p * dp, axis=1, keepdims=True))).astype(jnp.bfloat16)
        a = jnp.dot(ds, k, preferred_element_type=jnp.float32)
        b = lax.dot_general(ds, q, (((0,), (0,)), ((), ())), preferred_element_type=jnp.float32)
        e = lax.dot_general(p.astype(jnp.bfloat16), g, (((0,), (0,)), ((), ())), preferred_element_type=jnp.float32)
        if dq is None:
            dq, dk, dv = a, b, e
        else:
            dq, dk, dv = jnp.where(keep, a, dq), jnp.where(keep, b, dk), jnp.where(keep, e, dv)
    dq_ref[...] = (dq * 0.125).astype(jnp.bfloat16)
    dk_ref[...] = (dk * 0.125).astype(jnp.bfloat16)
    dv_ref[...] = dv.astype(jnp.bfloat16)


def attend_call(body, causal, bounds, operands, n_out_rows):
    width = operands[0].shape[1]
    spec = [pl.BlockSpec((a.shape[0], 128), lambda i: (0, i)) for a in operands]
    return pl.pallas_call(
        functools.partial(body, causal),
        grid=(width // 128,),
        out_shape=[jax.ShapeDtypeStruct((r, width), jnp.bfloat16) for r in n_out_rows],
        in_specs=[pl.BlockSpec(memory_space=pltpu.SMEM)] + spec,
        out_specs=[pl.BlockSpec((r, 128), lambda i: (0, i)) for r in n_out_rows],
        compiler_params=pltpu.CompilerParams(vmem_limit_bytes=32 * 1024 * 1024),
        name=("self_" if causal else "cross_") + body.__name__,
    )(bounds, *operands)


def attend(causal, bounds, q, k, v):
    return attend_call(attend_body, causal, bounds, (q, k, v), [q.shape[0]])[0]


def attend_grads(causal, bounds, q, k, v, g):
    return attend_call(attend_back_body, causal, bounds, (q, k, v, g), [q.shape[0], k.shape[0], k.shape[0]])


eps_norm = 1e-05


def layer_norm(values_in, gain_vec, shift_vec):
    centre = values_in - jnp.mean(values_in, axis=-1, keepdims=True)
    spread = jnp.mean(centre * centre, axis=-1, keepdims=True)
    return centre * lax.rsqrt(spread + eps_norm) * gain_vec + shift_vec


def gelu_exact(values_in):
    return jax.nn.gelu(values_in, approximate=False)


def project(left, right):
    return jnp.einsum("gti,ij->gtj", left, right, preferred_element_type=jnp.float32)


def project_back(left, right):
    return jnp.einsum("gtj,ij->gti", left, right, preferred_element_type=jnp.float32)


def outer_sum(left, right):
    return jnp.einsum("gti,gtj->ij", left, right, preferred_element_type=jnp.float32)


ORDERS = ("zyx", "zxy") * 4 + ("zyx", "yxz", "zxy", "zyx", "xyz", "zxy", "yxz", "zyx", "xyz")
SHORT_ORDERS = ("zyx", "zxy", "zyx", "zxy", "zyx", "zxy", "yxz", "zyx", "xyz")


class Params(NamedTuple):
    w_query: jax.Array
    w_key: jax.Array
    w_value: jax.Array
    w_out: jax.Array
    c_query: jax.Array
    c_key: jax.Array
    c_value: jax.Array
    c_out: jax.Array
    w_text: jax.Array
    w_up: jax.Array
    w_down: jax.Array
    gain_attn: jax.Array
    bias_attn: jax.Array
    gain_cross: jax.Array
    bias_cross: jax.Array
    gain_feed: jax.Array
    bias_feed: jax.Array


BLOCKS, GAINS = 11, 6


def all_axes():
    return ("dp", "seq")


class Wires:
    def __init__(self, own):
        self.nz = lax.axis_size("dp") // 2
        self.rows, self.width = own.w_query.shape
        self.text_rows = own.w_text.shape[0]
        rows, width = self.rows, self.width
        up, down = own.w_up.shape[1] // width, own.w_down.shape[0] // rows
        self.units = [(g, 0, rows, 0, width) for g in range(9)]
        self.units += [(9, 0, rows, k * width, width) for k in range(up)]
        self.units += [(10, k * rows, rows, 0, width) for k in range(down)]
        self.orders = [ORDERS[i % len(ORDERS)] for i in range(len(self.units))]

    @staticmethod
    def fits(own, frames, text):
        rows, width = own.w_query.shape
        return (
            lax.axis_size("seq") == 4 and lax.axis_size("dp") % 2 == 0 and rows == 32 and width % 128 == 0
            and own.w_text.shape[0] % 8 == 0 and own.w_text.shape[0] + 8 <= rows
            and own.w_up.shape[0] == rows and own.w_up.shape[1] % width == 0
            and own.w_down.shape[0] % rows == 0 and own.w_down.shape[1] == width
            and frames.shape[0] == 1 and frames.shape[1] % 32 == 0 and text.shape[0] == 1 and text.shape[1] % 128 == 0
        )

    def gather(self, own, frames):
        gains = jnp.stack(own[BLOCKS:])
        gains = jnp.pad(gains, ((0, self.rows - self.text_rows - GAINS), (0, self.width - gains.shape[1])))
        arrays = list(own[:BLOCKS])
        arrays[8] = jnp.concatenate([own.w_text, gains], axis=0)
        *full, all_rows = gather_weights(arrays[:9], frames[0], self.units[:9], SHORT_ORDERS, self.nz)
        full += [lax.all_gather(v, all_axes(), axis=0, tiled=True) for v in arrays[9:]]
        mixed = full[8].reshape((-1, self.rows, self.width))
        full = [f.reshape((-1, f.shape[-1])) for f in full]
        full[8] = mixed[:, : self.text_rows].reshape((-1, self.width))
        gains = [mixed[:, self.text_rows + i, : own[BLOCKS + i].shape[0]].reshape((-1,)) for i in range(GAINS)]
        return Params(*full, *gains), all_rows.reshape((1, -1, self.width))

    def scatter(self, grads):
        low = [v.astype(jnp.bfloat16) for v in grads]
        shards = self.nz * 8
        rest = jnp.stack([v.reshape((shards, -1)) for v in low[BLOCKS:]], axis=1)
        rest = jnp.pad(rest, ((0, 0), (0, self.rows - self.text_rows - GAINS), (0, self.width - rest.shape[2])))
        low[8] = jnp.concatenate([low[8].reshape((shards, self.text_rows, self.width)), rest], axis=1)
        arrays = [v.reshape((self.nz, 2, 2, 2, -1, v.shape[-1])) for v in low[:BLOCKS]]
        sums = scatter_grads(arrays, self.units, self.orders, self.nz)
        *blocks, mixed = deliver(sums, self.units, self.text_rows, [a.shape[4:] for a in arrays])
        gains = [mixed[i, : v.shape[0] // shards] for i, v in enumerate(grads[BLOCKS:])]
        return Params(*blocks, *gains)

    def share(self, arrays, number):
        return [v[None] for v in share_sums([a.reshape((2, 2, -1, self.width)) for a in arrays], number)]


class PlainWires:
    def gather(self, own, frames):
        full = Params(*[lax.all_gather(v, all_axes(), axis=0, tiled=True) for v in own])
        return full, lax.all_gather(frames, "seq", axis=1, tiled=True)

    def scatter(self, grads):
        return Params(*[lax.psum_scatter(v, all_axes(), scatter_dimension=0, tiled=True) for v in grads])

    def share(self, arrays, number):
        return [lax.psum_scatter(a, "seq", scatter_dimension=1, tiled=True) for a in arrays]


def attention(causal, bounds, q, k, v):
    return attend(causal, bounds[0], q[0], k[0], v[0])[None]


def attention_back(causal, bounds, *operands):
    return [r[None] for r in attend_grads(causal, bounds[0], *[a[0] for a in operands])]


def on_device(frames, cotangent, text_states, frame_start, prompt_len, *params):
    own = Params(*params)
    low = jnp.bfloat16
    wires = Wires(own) if Wires.fits(own, frames, text_states) else PlainWires()
    full, all_frames = wires.gather(own, frames)
    wide = [v.astype(jnp.float32) for v in full[BLOCKS:]]
    frames_f = frames.astype(jnp.float32)
    frame_count = frames.shape[1]
    normed, norm_one_back = jax.vjp(layer_norm, frames_f, wide[0], wide[1])
    normed_low = normed.astype(low)
    normed_all = layer_norm(all_frames.astype(jnp.float32), wide[0], wide[1]).astype(low)
    query_rows = project(normed_low, full.w_query).astype(low)
    key_all = project(normed_all, full.w_key).astype(low)
    value_all = project(normed_all, full.w_value).astype(low)
    rank = lax.axis_index("seq")
    self_bounds = jnp.stack([jnp.full_like(frame_start, rank * frame_count), frame_start], axis=1)
    attended = attention(True, self_bounds, query_rows, key_all, value_all)
    first = frames_f + project(attended, full.w_out)
    text_count = text_states.shape[1]
    quarter = text_count // lax.axis_size("seq")
    text_start = rank * quarter
    text_part = lax.dynamic_slice_in_dim(text_states, text_start, quarter, 1)
    proj_all = project(text_states, full.w_text).astype(low)
    cross_keys = project(proj_all, full.c_key).astype(low)
    cross_values = project(proj_all, full.c_value).astype(low)
    proj_part = lax.dynamic_slice_in_dim(proj_all, text_start, quarter, 1)
    normed_two, norm_two_back = jax.vjp(layer_norm, first, wide[2], wide[3])
    normed_two_low = normed_two.astype(low)
    cross_query = project(normed_two_low, full.c_query).astype(low)
    cross_bounds = jnp.stack([prompt_len, prompt_len], axis=1)
    cross_mix = attention(False, cross_bounds, cross_query, cross_keys, cross_values)
    second = first + project(cross_mix, full.c_out)
    normed_three, norm_three_back = jax.vjp(layer_norm, second, wide[4], wide[5])
    three_low = normed_three.astype(low)
    hidden = project(three_low, full.w_up)
    activated, gelu_back = jax.vjp(gelu_exact, hidden)
    act_low = activated.astype(low)
    block_out = (second + project(act_low, full.w_down)).astype(low)
    grad_act = project_back(cotangent, full.w_down)
    dw_down = outer_sum(act_low, cotangent)
    grad_hidden = gelu_back(grad_act)[0].astype(low)
    dw_up = outer_sum(three_low, grad_hidden)
    grad_second_ln, dgain_feed, dbias_feed = norm_three_back(project_back(grad_hidden, full.w_up))
    grad_second = cotangent.astype(jnp.float32) + grad_second_ln
    second_low = grad_second.astype(low)
    dc_out = outer_sum(cross_mix, second_low)
    grad_cross_mix = project_back(second_low, full.c_out).astype(low)
    cq_low, grad_ck, grad_cv = attention_back(
        False, cross_bounds, cross_query, cross_keys, cross_values, grad_cross_mix
    )
    ck_low, cv_low = wires.share([grad_ck, grad_cv], 3)
    dc_key = outer_sum(proj_part, ck_low)
    dc_value = outer_sum(proj_part, cv_low)
    grad_proj = (project_back(ck_low, full.c_key) + project_back(cv_low, full.c_value)).astype(low)
    dw_text = outer_sum(text_part, grad_proj)
    text_grad = project_back(grad_proj, full.w_text)
    dc_query = outer_sum(normed_two_low, cq_low)
    grad_first_ln, dgain_cross, dbias_cross = norm_two_back(project_back(cq_low, full.c_query))
    grad_first = grad_second + grad_first_ln
    first_low = grad_first.astype(low)
    dw_out = outer_sum(attended, first_low)
    grad_attended = project_back(first_low, full.w_out).astype(low)
    q_low, grad_k_all, grad_v_all = attention_back(
        True, self_bounds, query_rows, key_all, value_all, grad_attended
    )
    k_low, v_low = wires.share([grad_k_all, grad_v_all], 4)
    dw_query = outer_sum(normed_low, q_low)
    dw_key = outer_sum(normed_low, k_low)
    dw_value = outer_sum(normed_low, v_low)
    grad_normed = (
        project_back(q_low, full.w_query) + project_back(k_low, full.w_key) + project_back(v_low, full.w_value)
    )
    grad_frames_ln, dgain_attn, dbias_attn = norm_one_back(grad_normed)
    frames_grad = (grad_first + grad_frames_ln).astype(low)
    sums = wires.scatter(
        Params(
            dw_query, dw_key, dw_value, dw_out, dc_query, dc_key, dc_value, dc_out, dw_text, dw_up, dw_down,
            dgain_attn, dbias_attn, dgain_cross, dbias_cross, dgain_feed, dbias_feed,
        )
    )
    return (block_out, frames_grad, text_grad, *sums)


def solution(mesh):
    both = P(all_axes(), None)
    rows, vector = P(*all_axes(), None), P(all_axes())
    item, whole = P("dp"), P("dp", None, None)
    return jax.shard_map(
        on_device,
        mesh=mesh,
        in_specs=(rows, rows, whole, item, item) + (both,) * BLOCKS + (vector,) * GAINS,
        out_specs=(rows,) * 3 + (both,) * BLOCKS + (vector,) * GAINS,
        check_vma=False,
    )
```

```python
import functools
from typing import NamedTuple
import jax
import jax.numpy as jnp
from jax import lax
from jax.experimental import pallas as pl
from jax.experimental.pallas import tpu as pltpu
from jax.sharding import PartitionSpec as P

MESH = pl.DeviceIdType.MESH

LAG = 2
VMEM_LIMIT = 60 * 1024 * 1024

def unit_ops(perm, nz):
    rank = {a: i for i, a in enumerate(perm)}
    ops = {}

    def source(j, fy, fx):
        differs = [a for a, f in (("z", j > 0), ("y", fy), ("x", fx)) if f]
        if not differs:
            return None
        last = max(differs, key=lambda a: rank[a])
        if last == "z":
            return ("z", j - 1, fy, fx)
        if last == "y":
            return ("y", j, 0, fx)
        return ("x", j, fy, 0)

    for j in range(nz):
        for fy in range(2):
            for fx in range(2):
                for axis in "zyx":
                    flags = {"z": j > 0, "y": fy, "x": fx}
                    if axis != "z" and flags[axis]:
                        continue
                    if any(flags[a] and rank[a] > rank[axis] for a in "zyx" if a != axis):
                        continue
                    if axis == "z" and j == nz - 1:
                        continue
                    ops[(axis, j, fy, fx)] = source(j, fy, fx)
    return ops

def make_schedule(perms, nz, lag=LAG, window=None):
    ops = {}
    for u, perm in enumerate(perms):
        for key, dep in unit_ops(perm, nz).items():
            ops[(u,) + key] = None if dep is None else (u,) + dep
    children = {}
    for op, dep in ops.items():
        children.setdefault(dep, []).append(op)
    height = {}

    def tall(op):
        if op not in height:
            height[op] = 1 + max([tall(c) for c in children.get(op, [])], default=0)
        return height[op]

    for op in ops:
        tall(op)
    done, slots, left = {}, [], set(ops)
    while left:
        t = len(slots)
        slot = {}
        for axis in "zyx":
            ready = [op for op in left if op[1] == axis and (ops[op] is None or (ops[op] in done and done[ops[op]] + lag <= t))]
            if ready:
                slot[axis] = min(ready, key=lambda op: (op[0] // window if window else 0, -height[op], op[0], op))
        for axis, op in slot.items():
            done[op] = t
            left.discard(op)
        slots.append(slot)
    return slots

def nth_table(nz):
    rows = []
    for z in range(nz):
        offs = sorted((p - z for p in range(nz)), key=lambda o: (abs(o), o if z % 2 else -o))
        rows.append([z + o for o in offs])
    return rows

def pick(values, z):
    out = 0
    for i, v in enumerate(values):
        out = out + v * jnp.where(z == i, 1, 0)
    return out

UP, DOWN, YY, XX, CORE = range(5)
WAYS_OF = dict(z=(UP, DOWN), y=(YY,), x=(XX,))

class Place:
    def __init__(self, nz):
        d, s = lax.axis_index("dp"), lax.axis_index("seq")
        self.nz = nz
        self.z, self.y, self.x, self.c = d // 2, d % 2, s // 2, s % 2
        z, y, x, c = self.z, self.y, self.x, self.c
        self.device = [
            ((z + 1) * 2 + y, x * 2 + c),
            ((z - 1) * 2 + y, x * 2 + c),
            (z * 2 + 1 - y, x * 2 + c),
            (z * 2 + y, (1 - x) * 2 + c),
            (z * 2 + y, x * 2 + 1 - c),
        ]
        self.nth = [[row[j] for row in nth_table(nz)] for j in range(nz)]

    def greet(self):
        barrier = pltpu.get_barrier_semaphore()
        has_up, has_down = self.z + 1 < self.nz, self.z > 0
        for way in range(5):
            def hello(way=way):
                pl.semaphore_signal(barrier, inc=1, device_id=self.device[way], device_id_type=MESH)
            if way < YY:
                pl.when(has_up if way == UP else has_down)(hello)
            else:
                hello()
        edge = jnp.where(self.z == 0, 1, 0) + jnp.where(self.z == self.nz - 1, 1, 0)
        pl.semaphore_wait(barrier, 5 - edge)

    def gather_moves(self, axis, j, fy, fx):
        z, y, x, nz = self.z, self.y, self.x, self.nz
        py, px = (1 - y if fy else y), (1 - x if fx else x)
        if axis == "z":
            out = [(UP, (z - j >= 0) & (z + 1 < nz), (z - j, py, px)), (DOWN, (z + j < nz) & (z > 0), (z + j, py, px))]
            come = [(UP, z - 1 - j >= 0, (z - 1 - j, py, px)), (DOWN, z + 1 + j < nz, (z + 1 + j, py, px))]
        else:
            pz = pick(self.nth[j], z)
            there = (pz, 1 - y, px) if axis == "y" else (pz, py, 1 - x)
            way = YY if axis == "y" else XX
            out = [(way, None, (pz, py, px))]
            come = [(way, None, there)]
        return out, come

def when(cond, fn):
    if cond is None:
        fn()
    else:
        pl.when(cond)(fn)

def gather_body(nz, units, slots, n, depth, *refs):
    given, outs, rows_out = refs[:n + 1], refs[n + 1:2 * n + 1], refs[2 * n + 1]
    held = refs[2 * n + 2:3 * n + 3]
    ins, rows_in = held[:n], held[n]
    send_sem, recv_sem, core_send, core_recv, local_sem, rows_send, rows_recv = refs[3 * n + 3:]
    loads = [pltpu.make_async_copy(given[g], held[g], local_sem.at[g]) for g in range(n + 1)]
    for cp in loads:
        cp.start()
    here = Place(nz)
    z, y, x, c = here.z, here.y, here.x, here.c
    own = [pltpu.make_async_copy(ins[g], outs[g].at[z, y, x, c], local_sem.at[g]) for g in range(n)]
    own.append(pltpu.make_async_copy(rows_in, rows_out.at[x, c], local_sem.at[n]))
    here.greet()
    for cp in loads:
        cp.wait()
    for cp in own:
        cp.start()

    def rows_over(src, dst, way, i):
        return pltpu.make_async_remote_copy(
            src_ref=src, dst_ref=dst, send_sem=rows_send.at[i], recv_sem=rows_recv.at[i],
            device_id=here.device[way], device_id_type=MESH,
        )

    rows_moves = [
        rows_over(rows_in, rows_out.at[x, c], XX, 0),
        rows_over(rows_in, rows_out.at[x, c], CORE, 1),
        rows_over(rows_out.at[1 - x, c], rows_out.at[1 - x, c], CORE, 2),
    ]
    rows_moves[0].start()
    rows_moves[1].start()

    def piece(u, p):
        g, r0, rn, c0, cn = units[u]
        return outs[g].at[p[0], p[1], p[2], c, pl.ds(r0, rn), pl.ds(c0, cn)]

    def corner(u, fy, fx, which):
        g, r0, rn, c0, cn = units[u]
        return outs[g].at[:, 1 - y if fy else y, 1 - x if fx else x, which, pl.ds(r0, rn), pl.ds(c0, cn)]

    def remote(u, way, t, p, mine):
        i = way
        ref = piece(u, p)
        g, r0, rn, c0, cn = units[u]
        src = ins[g].at[pl.ds(r0, rn), pl.ds(c0, cn)] if mine else ref
        return pltpu.make_async_remote_copy(src_ref=src, dst_ref=ref, send_sem=send_sem.at[i, t], recv_sem=recv_sem.at[i, t], device_id=here.device[way], device_id_type=MESH)

    def across(u, fy, fx):
        ref = corner(u, fy, fx, c)
        i = fy * 2 + fx
        return pltpu.make_async_remote_copy(src_ref=ref, dst_ref=ref, send_sem=core_send.at[u, i], recv_sem=core_recv.at[u, i], device_id=here.device[CORE], device_id_type=MESH)

    last = {}
    for t, slot in enumerate(slots):
        for u, axis, j, fy, fx in slot.values():
            came = {"z": (u, fy, fx), "y": (u, 1, fx), "x": (u, fy, 1)}[axis]
            last[came] = t
    for t in range(len(slots) + depth):
        if t < len(slots):
            for axis, (u, _, j, fy, fx) in slots[t].items():
                for way, cond, p in here.gather_moves(axis, j, fy, fx)[0]:
                    when(cond, lambda u=u, way=way, p=p: remote(u, way, t, p, (j, fy, fx) == (0, 0, 0)).start())
        if t == depth - 1:
            for cp in own:
                cp.wait()
        if t == min(6, len(slots) - 1):
            arrived = rows_out.at[1 - x, c]
            pltpu.make_async_copy(arrived, arrived, rows_recv.at[0]).wait()
            rows_moves[2].start()
        if t >= depth:
            for axis, (u, _, j, fy, fx) in slots[t - depth].items():
                for way, cond, p in here.gather_moves(axis, j, fy, fx)[1]:
                    when(cond, lambda u=u, way=way, p=p: pltpu.make_async_copy(piece(u, p), piece(u, p), recv_sem.at[way, t - depth]).wait())
            for key in sorted(last):
                if last[key] == t - depth:
                    across(*key).start()
    for t, slot in enumerate(slots):
        for axis, (u, _, j, fy, fx) in slot.items():
            for way, cond, p in here.gather_moves(axis, j, fy, fx)[0]:
                when(cond, lambda u=u, way=way, p=p: remote(u, way, t, p, (j, fy, fx) == (0, 0, 0)).wait_send())
    for u, fy, fx in sorted(last):
        across(u, fy, fx).wait_send()
    for u, fy, fx in sorted(last):
        ref = corner(u, fy, fx, 1 - c)
        pltpu.make_async_copy(ref, ref, core_recv.at[u, fy * 2 + fx]).wait()
    for cp in rows_moves:
        cp.wait_send()
    for i, ref in ((1, rows_out.at[x, 1 - c]), (2, rows_out.at[1 - x, 1 - c])):
        pltpu.make_async_copy(ref, ref, rows_recv.at[i]).wait()

def gather_weights(arrays, frame_rows, units, perms, nz, window=None, depth=2):
    n = len(arrays)
    slots = make_schedule(perms, nz, lag=depth + 1, window=window)
    return pl.pallas_call(
        functools.partial(gather_body, nz, units, slots, n, depth),
        out_shape=[jax.ShapeDtypeStruct((nz, 2, 2, 2) + a.shape, a.dtype) for a in arrays]
        + [jax.ShapeDtypeStruct((2, 2) + frame_rows.shape, frame_rows.dtype)],
        in_specs=[pl.BlockSpec(memory_space=pl.ANY)] * (n + 1),
        out_specs=[pl.BlockSpec(memory_space=pl.ANY)] * (n + 1),
        scratch_shapes=[pltpu.VMEM(a.shape, a.dtype) for a in (*arrays, frame_rows)]
        + [
            pltpu.SemaphoreType.DMA((4, len(slots))),
            pltpu.SemaphoreType.DMA((4, len(slots))),
            pltpu.SemaphoreType.DMA((len(units), 4)),
            pltpu.SemaphoreType.DMA((len(units), 4)),
            pltpu.SemaphoreType.DMA((n + 1,)),
            pltpu.SemaphoreType.DMA((3,)),
            pltpu.SemaphoreType.DMA((3,)),
        ],
        compiler_params=pltpu.CompilerParams(collective_id=1, has_side_effects=True, vmem_limit_bytes=VMEM_LIMIT),
        name="gather_weights",
    )(*arrays, frame_rows)


BACK = (DOWN, UP, YY, XX)


def scatter_steps(here, units, slots, depth, ins, total, twin, landed, send_sem, recv_sem, core_send, core_recv, local_sem):
    nz = here.nz
    z, y, x, c = here.z, here.y, here.x, here.c
    steps = slots[::-1]
    numbers, order = {}, []
    for t, slot in enumerate(steps):
        for axis, op in slot.items():
            for way in WAYS_OF[axis]:
                numbers[way, t] = len(numbers)
            if op[0] not in order:
                order.append(op[0])

    def plane(u, b, which):
        g, r0, rn, c0, cn = units[u][b]
        return ins[g].at[:, :, :, which, pl.ds(r0, rn), pl.ds(c0, cn)]

    def rows_of(buffer, u, b):
        rn = units[u][b][2]
        return buffer.at[u, :, :, :, pl.ds(b * rn, rn)]

    def local(u, b):
        return pltpu.make_async_copy(plane(u, b, c), rows_of(total, u, b), local_sem.at[u, b])

    def across(u, b):
        return pltpu.make_async_remote_copy(
            src_ref=plane(u, b, 1 - c), dst_ref=rows_of(twin, u, b), send_sem=core_send.at[u, b],
            recv_sem=core_recv.at[u, b], device_id=here.device[CORE], device_id_type=MESH,
        )

    def remote(u, way, t, p):
        i = numbers[way, t]
        return pltpu.make_async_remote_copy(
            src_ref=total.at[u, p[0], p[1], p[2]], dst_ref=landed.at[i], send_sem=send_sem.at[i], recv_sem=recv_sem.at[i],
            device_id=here.device[BACK[way]], device_id_type=MESH,
        )

    ahead = 3
    blocks = range(len(units[0]))
    for u in order[:ahead]:
        for b in blocks:
            local(u, b).start()
    here.greet()
    for u in order[:ahead]:
        for b in blocks:
            across(u, b).start()

    def join(u):
        later = order.index(u) + ahead
        if later < len(order):
            for b in blocks:
                local(order[later], b).start()
                across(order[later], b).start()
        for b in blocks:
            local(u, b).wait()
            across(u, b).wait_recv()

        @pl.loop(0, nz)
        def _(a):
            for b in range(2):
                for e in range(2):
                    total[u, a, b, e] = (
                        total[u, a, b, e].astype(jnp.float32) + twin[u, a, b, e].astype(jnp.float32)
                    ).astype(jnp.bfloat16)

    joined = set()
    for t in range(len(steps) + depth):
        if t < len(steps):
            for axis, (u, _, j, fy, fx) in steps[t].items():
                if u not in joined:
                    joined.add(u)
                    join(u)
                for way, cond, p in here.gather_moves(axis, j, fy, fx)[1]:
                    when(cond, lambda u=u, way=way, p=p: remote(u, way, t, p).start())
        if t >= depth:
            s = t - depth
            for axis, (u, _, j, fy, fx) in steps[s].items():
                for way, cond, p in here.gather_moves(axis, j, fy, fx)[0]:
                    def add(u=u, way=way, p=p):
                        i = numbers[way, s]
                        pltpu.make_async_copy(landed.at[i], landed.at[i], recv_sem.at[i]).wait()
                        total[u, p[0], p[1], p[2]] = (
                            total[u, p[0], p[1], p[2]].astype(jnp.float32) + landed[i].astype(jnp.float32)
                        ).astype(jnp.bfloat16)
                    when(cond, add)
        yield t
    for t, slot in enumerate(steps):
        for axis, (u, _, j, fy, fx) in slot.items():
            for way, cond, p in here.gather_moves(axis, j, fy, fx)[1]:
                when(cond, lambda u=u, way=way, p=p: remote(u, way, t, p).wait_send())
    for u in order:
        for b in blocks:
            across(u, b).wait_send()


def unit_shape(units):
    return sum(block[2] for block in units[0]), units[0][0][4]


def scatter_scratch(units, slots, nz):
    rows, columns = unit_shape(units)
    count = sum(len(WAYS_OF[axis]) for slot in slots for axis in slot)
    plane = (len(units), nz, 2, 2, rows, columns)
    return [
        pltpu.VMEM(plane, jnp.bfloat16),
        pltpu.VMEM(plane, jnp.bfloat16),
        pltpu.VMEM((count, rows, columns), jnp.bfloat16),
        pltpu.SemaphoreType.DMA((count,)),
        pltpu.SemaphoreType.DMA((count,)),
        pltpu.SemaphoreType.DMA((len(units), len(units[0]))),
        pltpu.SemaphoreType.DMA((len(units), len(units[0]))),
        pltpu.SemaphoreType.DMA((len(units), len(units[0]))),
    ]


def scatter_body(nz, units, slots, n, depth, *refs):
    ins, out = refs[:n], refs[n]
    here = Place(nz)
    for _ in scatter_steps(here, units, slots, depth, ins, *refs[n + 1:]):
        pass
    total = refs[n + 1]
    for u in range(len(units)):
        out[u] = total[u, here.z, here.y, here.x].astype(jnp.float32)


def scatter_grads(arrays, units, perms, nz, depth=2):
    n = len(arrays)
    slots = make_schedule(perms, nz, lag=depth + 1)
    rows, columns = unit_shape(units)
    return pl.pallas_call(
        functools.partial(scatter_body, nz, units, slots, n, depth),
        out_shape=jax.ShapeDtypeStruct((len(units), rows, columns), jnp.float32),
        in_specs=[pl.BlockSpec(memory_space=pl.ANY)] * n,
        out_specs=pl.BlockSpec(memory_space=pltpu.VMEM),
        scratch_shapes=scatter_scratch(units, slots, nz),
        compiler_params=pltpu.CompilerParams(collective_id=2, has_side_effects=True, vmem_limit_bytes=VMEM_LIMIT),
        name="scatter_grads",
    )(*arrays)


def share_body(n, chunk, *refs):
    ins, outs = refs[:n], refs[n:2 * n]
    twins, sums, landed = refs[2 * n:3 * n], refs[3 * n:4 * n], refs[4 * n:5 * n]
    core_send, core_recv, x_send, x_recv = refs[5 * n:]
    d, s = lax.axis_index("dp"), lax.axis_index("seq")
    x, c = s // 2, s % 2
    core, over = (d, x * 2 + 1 - c), (d, (1 - x) * 2 + c)
    barrier = pltpu.get_barrier_semaphore()
    for other in (core, over):
        pl.semaphore_signal(barrier, inc=1, device_id=other, device_id_type=MESH)
    pl.semaphore_wait(barrier, 2)
    pieces = [(g, k, pl.ds(k * chunk, chunk)) for g in range(n) for k in range(ins[g].shape[2] // chunk)]

    def across(i, far):
        g, k, rows = pieces[i]
        part = 1 - x if far else x
        return pltpu.make_async_remote_copy(
            src_ref=ins[g].at[part, 1 - c, rows], dst_ref=twins[g].at[1 if far else 0, rows],
            send_sem=core_send.at[1 if far else 0, i], recv_sem=core_recv.at[1 if far else 0, i],
            device_id=core, device_id_type=MESH,
        )

    def beyond(i):
        g, k, rows = pieces[i]
        return pltpu.make_async_remote_copy(
            src_ref=sums[g].at[rows], dst_ref=landed[g].at[rows], send_sem=x_send.at[i], recv_sem=x_recv.at[i],
            device_id=over, device_id_type=MESH,
        )

    for far in (True, False):
        for i in range(len(pieces)):
            across(i, far).start()
    for i, (g, k, rows) in enumerate(pieces):
        across(i, True).wait_recv()
        sums[g][rows] = (ins[g][1 - x, c, rows].astype(jnp.float32) + twins[g][1, rows].astype(jnp.float32)).astype(jnp.bfloat16)
        beyond(i).start()
    for i, (g, k, rows) in enumerate(pieces):
        across(i, False).wait_recv()
        beyond(i).wait_recv()
        outs[g][rows] = (
            ins[g][x, c, rows].astype(jnp.float32) + twins[g][0, rows].astype(jnp.float32) + landed[g][rows].astype(jnp.float32)
        ).astype(jnp.bfloat16)
    for i in range(len(pieces)):
        across(i, True).wait_send()
        across(i, False).wait_send()
        beyond(i).wait_send()


def share_sums(arrays, number):
    n = len(arrays)
    chunk = 32
    count = sum(a.shape[2] // chunk for a in arrays)
    return pl.pallas_call(
        functools.partial(share_body, n, chunk),
        out_shape=[jax.ShapeDtypeStruct(a.shape[2:], a.dtype) for a in arrays],
        in_specs=[pl.BlockSpec(memory_space=pltpu.VMEM)] * n,
        out_specs=[pl.BlockSpec(memory_space=pltpu.VMEM)] * n,
        scratch_shapes=[pltpu.VMEM((2,) + a.shape[2:], a.dtype) for a in arrays]
        + [pltpu.VMEM(a.shape[2:], a.dtype) for a in arrays] * 2
        + [pltpu.SemaphoreType.DMA((2, count))] * 2
        + [pltpu.SemaphoreType.DMA((count,))] * 2,
        compiler_params=pltpu.CompilerParams(collective_id=number, has_side_effects=True, vmem_limit_bytes=32 * 1024 * 1024),
        name="share_sums",
    )(*arrays)


def deliver_body(parts, text_rows, n, *refs):
    ins, outs = refs[:n], refs[n:]
    for sums, units in zip(ins, parts):
        for u, unit in enumerate(units):
            for b, (g, r0, rn, c0, cn) in enumerate(unit):
                if g == 8:
                    outs[g][...] = sums[u, :text_rows]
                    outs[-1][...] = sums[u, text_rows:text_rows + 8]
                else:
                    outs[g][r0:r0 + rn, c0:c0 + cn] = sums[u, b * rn:(b + 1) * rn]


def deliver(sums, parts, text_rows, shapes):
    shapes = [(text_rows,) + s[1:] if g == 8 else s for g, s in enumerate(shapes)] + [(8, sums[0].shape[2])]
    return pl.pallas_call(
        functools.partial(deliver_body, parts, text_rows, len(sums)),
        out_shape=[jax.ShapeDtypeStruct(s, jnp.float32) for s in shapes],
        compiler_params=pltpu.CompilerParams(vmem_limit_bytes=16 * 1024 * 1024),
        name="deliver",
    )(*sums)


def pair_scores(bounds_ref, q, k, keep, causal):
    s = lax.dot_general(jnp.where(keep, q, 0), k, (((1,), (1,)), ((), ())), preferred_element_type=jnp.float32)
    col = lax.broadcasted_iota(jnp.int32, s.shape, 1)
    if causal:
        row = lax.broadcasted_iota(jnp.int32, s.shape, 0) + bounds_ref[0]
        seen = (col <= row) & ((col >= bounds_ref[1]) | (col == row))
    else:
        seen = col < bounds_ref[0]
    s = jnp.where(seen, s * 0.125, -1e30)
    e = jnp.exp(s - jnp.max(s, axis=1, keepdims=True))
    return e * (1.0 / jnp.sum(e, axis=1, keepdims=True))


def halves(width):
    lane = lax.broadcasted_iota(jnp.int32, (1, width), 1)
    return [(lane >= 64 * h) & (lane < 64 * h + 64) for h in range(width // 64)]


def attend_body(causal, bounds_ref, q_ref, k_ref, v_ref, out_ref):
    q, k, v = q_ref[...], k_ref[...], v_ref[...]
    out = None
    for keep in halves(q.shape[1]):
        p = pair_scores(bounds_ref, q, k, keep, causal)
        o = jnp.dot(p.astype(jnp.bfloat16), v, preferred_element_type=jnp.float32)
        out = o if out is None else jnp.where(keep, o, out)
    out_ref[...] = out.astype(jnp.bfloat16)


def attend_back_body(causal, bounds_ref, q_ref, k_ref, v_ref, g_ref, dq_ref, dk_ref, dv_ref):
    q, k, v, g = q_ref[...], k_ref[...], v_ref[...], g_ref[...]
    dq = dk = dv = None
    for keep in halves(q.shape[1]):
        p = pair_scores(bounds_ref, q, k, keep, causal)
        dp = lax.dot_general(jnp.where(keep, g, 0), v, (((1,), (1,)), ((), ())), preferred_element_type=jnp.float32)
        ds = (p * (dp - jnp.sum(p * dp, axis=1, keepdims=True))).astype(jnp.bfloat16)
        a = jnp.dot(ds, k, preferred_element_type=jnp.float32)
        b = lax.dot_general(ds, q, (((0,), (0,)), ((), ())), preferred_element_type=jnp.float32)
        e = lax.dot_general(p.astype(jnp.bfloat16), g, (((0,), (0,)), ((), ())), preferred_element_type=jnp.float32)
        if dq is None:
            dq, dk, dv = a, b, e
        else:
            dq, dk, dv = jnp.where(keep, a, dq), jnp.where(keep, b, dk), jnp.where(keep, e, dv)
    dq_ref[...] = (dq * 0.125).astype(jnp.bfloat16)
    dk_ref[...] = (dk * 0.125).astype(jnp.bfloat16)
    dv_ref[...] = dv.astype(jnp.bfloat16)


def attend_call(body, causal, bounds, operands, n_out_rows):
    width = operands[0].shape[1]
    spec = [pl.BlockSpec((a.shape[0], 128), lambda i: (0, i)) for a in operands]
    return pl.pallas_call(
        functools.partial(body, causal),
        grid=(width // 128,),
        out_shape=[jax.ShapeDtypeStruct((r, width), jnp.bfloat16) for r in n_out_rows],
        in_specs=[pl.BlockSpec(memory_space=pltpu.SMEM)] + spec,
        out_specs=[pl.BlockSpec((r, 128), lambda i: (0, i)) for r in n_out_rows],
        compiler_params=pltpu.CompilerParams(vmem_limit_bytes=32 * 1024 * 1024),
        name=("self_" if causal else "cross_") + body.__name__,
    )(bounds, *operands)


def attend(causal, bounds, q, k, v):
    return attend_call(attend_body, causal, bounds, (q, k, v), [q.shape[0]])[0]


def attend_grads(causal, bounds, q, k, v, g):
    return attend_call(attend_back_body, causal, bounds, (q, k, v, g), [q.shape[0], k.shape[0], k.shape[0]])


def dot_tt(a, b):
    return lax.dot_general(a, b, (((0,), (0,)), ((), ())), preferred_element_type=jnp.float32)


def dot_nt(a, b):
    return lax.dot_general(a, b, (((1,), (1,)), ((), ())), preferred_element_type=jnp.float32)


def norm_parts(v):
    centre = v - jnp.mean(v, axis=1, keepdims=True)
    rate = lax.rsqrt(jnp.mean(centre * centre, axis=1, keepdims=True) + eps_norm)
    return centre * rate, rate


def norm_grads(v, gain, h):
    xh, rate = norm_parts(v)
    hg = h * gain
    dv = (hg - jnp.mean(hg, axis=1, keepdims=True) - xh * jnp.mean(hg * xh, axis=1, keepdims=True)) * rate
    return dv, jnp.sum(h * xh, axis=0, keepdims=True), jnp.sum(h, axis=0, keepdims=True)


class Share:
    def __init__(self, here, mine, twins, sums, landed, core_send, core_recv, x_send, x_recv, chunk):
        self.here, self.mine, self.twins, self.sums, self.landed = here, mine, twins, sums, landed
        self.sems, self.chunk = (core_send, core_recv, x_send, x_recv), chunk

    def columns(self, k):
        return pl.ds(k * self.chunk, self.chunk)

    def across(self, g, k, far):
        here, f = self.here, 1 if far else 0
        part = (1 - here.x if far else here.x) * 2 + 1 - here.c
        return pltpu.make_async_remote_copy(
            src_ref=self.mine[g].at[part, :, self.columns(k)], dst_ref=self.twins[g].at[f, :, self.columns(k)],
            send_sem=self.sems[0].at[f, g, k], recv_sem=self.sems[1].at[f, g, k],
            device_id=here.device[CORE], device_id_type=MESH,
        )

    def beyond(self, g, k):
        return pltpu.make_async_remote_copy(
            src_ref=self.sums[g].at[:, self.columns(k)], dst_ref=self.landed[g].at[:, self.columns(k)],
            send_sem=self.sems[2].at[g, k], recv_sem=self.sems[3].at[g, k],
            device_id=self.here.device[XX], device_id_type=MESH,
        )

    def send(self, k):
        for far in (True, False):
            for g in range(len(self.mine)):
                self.across(g, k, far).start()

    def forward(self, k):
        here, cols = self.here, slice(k * self.chunk, (k + 1) * self.chunk)
        for g, mine in enumerate(self.mine):
            self.across(g, k, True).wait_recv()
            part = (1 - here.x) * 2 + here.c
            self.sums[g][:, cols] = (
                mine[part, :, cols].astype(jnp.float32) + self.twins[g][1, :, cols].astype(jnp.float32)
            ).astype(jnp.bfloat16)
            self.beyond(g, k).start()

    def collect(self, g, k):
        here, cols = self.here, slice(k * self.chunk, (k + 1) * self.chunk)
        self.across(g, k, False).wait_recv()
        self.beyond(g, k).wait_recv()
        return (
            self.mine[g][here.x * 2 + here.c, :, cols].astype(jnp.float32) + self.twins[g][0, :, cols].astype(jnp.float32)
            + self.landed[g][:, cols].astype(jnp.float32)
        ).astype(jnp.bfloat16)

    def finish(self, chunks):
        for g in range(len(self.mine)):
            for k in range(chunks):
                self.across(g, k, True).wait_send()
                self.across(g, k, False).wait_send()
                self.beyond(g, k).wait_send()


class Pace:
    def __init__(self, steps, every):
        self.steps, self.every, self.owed = steps, every, 0.0

    def spend(self, time):
        self.owed += time
        while self.owed >= self.every:
            self.owed -= self.every
            next(self.steps, None)


def pair_grads(bounds_ref, causal, q, k, v, g, between):
    dq = dk = dv = None
    for keep in halves(q.shape[1]):
        p = pair_scores(bounds_ref, q, k, keep, causal)
        dp = dot_nt(jnp.where(keep, g, 0), v)
        ds = (p * (dp - jnp.sum(p * dp, axis=1, keepdims=True))).astype(jnp.bfloat16)
        a = jnp.dot(ds, k, preferred_element_type=jnp.float32)
        b = dot_tt(ds, q)
        e = dot_tt(p.astype(jnp.bfloat16), g)
        if dq is None:
            dq, dk, dv = a, b, e
        else:
            dq, dk, dv = jnp.where(keep, a, dq), jnp.where(keep, b, dk), jnp.where(keep, e, dv)
        between()
    return [(r * s).astype(jnp.bfloat16) for r, s in ((dq, 0.125), (dk, 0.125), (dv, 1.0))]


def middle_body(nz, units, slots, depth, *refs):
    (bounds, second_low, grad_second, cross_mix, cross_query, cross_keys, cross_values, two_low, first, text_part,
     proj_part, attended, gain) = refs[:13]
    weights, feed = refs[13:19], refs[19:21]
    placed = refs[21:27]
    text_grad, grad_first, grad_attended, dgain, dbias, sums = refs[27:33]
    held, (weight_sem, mixed, first_low, grad_ck, grad_cv, twin_k, twin_v, sum_k, sum_v, land_k, land_v) = refs[33:39], refs[39:50]
    share_sems, stage, stage_sem, scatter = refs[50:54], refs[54], refs[55], refs[56:]
    here = Place(nz)
    loads = [pltpu.make_async_copy(w, h, weight_sem.at[i]) for i, (w, h) in enumerate(zip(weights, held))]
    for cp in loads:
        cp.start()
    c_out, c_query, c_key, c_value, w_text, w_out = held
    steps = scatter_steps(here, units, slots, depth, feed, *scatter)
    low = jnp.bfloat16
    width = second_low.shape[1]
    rows = text_part.shape[0]
    tiles = [slice(i, i + 256) for i in range(0, width, 256)]
    share = Share(here, (grad_ck, grad_cv), (twin_k, twin_v), (sum_k, sum_v), (land_k, land_v), *share_sems, width // 2)

    pace = Pace(steps, 32.0 / (len(slots) + depth))
    spend = pace.spend

    def stored(i):
        src = stage.at[i % 3, pl.ds(0, placed[i].shape[0])]
        return pltpu.make_async_copy(src, placed[i], stage_sem.at[i])

    next(steps)
    loads[0].wait()
    for n in tiles:
        mixed[:, n] = dot_nt(second_low[...], c_out[n, :]).astype(low)
        spend(0.4)
    for n in tiles:
        stage[0, n, :] = dot_tt(cross_mix[:, n], second_low[...]).astype(low)
        spend(0.55)
    stored(0).start()
    pairs = width // 128
    for i in range(pairs):
        n = slice(i * 128, i * 128 + 128)
        dq, dk, dv = pair_grads(bounds, False, cross_query[:, n], cross_keys[:, n], cross_values[:, n], mixed[:, n], lambda: spend(0.72))
        mixed[:, n] = dq
        grad_ck[:, :, n] = dk.reshape(4, rows, 128)
        grad_cv[:, :, n] = dv.reshape(4, rows, 128)
        if i == pairs // 2 - 1:
            share.send(0)
    share.send(1)
    share.forward(0)
    loads[1].wait()
    for n in tiles:
        grad_first[:, n] = dot_nt(mixed[...], c_query[n, :])
        spend(0.4)
    share.forward(1)
    dv, dg, db = norm_grads(first[...], gain[...], grad_first[...])
    dgain[...] = dg
    dbias[...] = db
    dv = grad_second[...] + dv
    grad_first[...] = dv
    first_low[...] = dv.astype(low)
    spend(2.0)
    loads[5].wait()
    for n in tiles:
        grad_attended[:, n] = dot_nt(first_low[...], w_out[n, :]).astype(low)
        spend(0.4)
    for n in tiles:
        stage[1, n, :] = dot_tt(two_low[:, n], mixed[...]).astype(low)
        spend(0.55)
    stored(1).start()
    for n in tiles:
        stage[2, n, :] = dot_tt(attended[:, n], first_low[...]).astype(low)
        spend(0.55)
    stored(2).start()
    ck = jnp.concatenate([share.collect(0, k) for k in range(2)], axis=1)
    cv = jnp.concatenate([share.collect(1, k) for k in range(2)], axis=1)
    for i in (2, 3, 4):
        loads[i].wait()
    stored(0).wait()
    stored(1).wait()
    for n in tiles:
        stage[0, n, :] = dot_tt(proj_part[:, n], ck).astype(low)
        stage[1, n, :] = dot_tt(proj_part[:, n], cv).astype(low)
        spend(0.7)
    stored(3).start()
    stored(4).start()
    proj = []
    for n in tiles:
        proj.append((dot_nt(ck, c_key[n, :]) + dot_nt(cv, c_value[n, :])).astype(low))
        spend(0.5)
    proj = jnp.concatenate(proj, axis=1)
    stored(2).wait()
    for i in range(0, text_part.shape[1], 256):
        n = slice(i, i + 256)
        stage[2, n, :] = dot_tt(text_part[:, n], proj).astype(low)
        text_grad[:, n] = dot_nt(proj, w_text[n, :])
        spend(0.7)
    stored(5).start()
    for _ in steps:
        pass
    share.finish(2)
    for i in (3, 4, 5):
        stored(i).wait()
    total = scatter[0]
    for u in range(len(units)):
        sums[u] = total[u, here.z, here.y, here.x].astype(jnp.float32)


def middle_back(bounds, near, weights, feed, units, perms, nz, depth=3):
    slots = make_schedule(perms, nz, lag=depth + 1)
    second_low, text_part = near[0], near[8]
    width, rows, text_width = second_low.shape[1], text_part.shape[0], text_part.shape[1]
    low, wide = jnp.bfloat16, jnp.float32
    square = jax.ShapeDtypeStruct((width, width), low)
    outs = [square] * 5 + [jax.ShapeDtypeStruct((text_width, width), low)]
    outs += [jax.ShapeDtypeStruct(text_part.shape, wide), jax.ShapeDtypeStruct(second_low.shape, wide)]
    outs += [jax.ShapeDtypeStruct(second_low.shape, low)] + [jax.ShapeDtypeStruct((1, width), wide)] * 2
    outs += [jax.ShapeDtypeStruct((len(units),) + unit_shape(units), wide)]
    vmem, any_ = pl.BlockSpec(memory_space=pltpu.VMEM), pl.BlockSpec(memory_space=pl.ANY)
    part = pltpu.VMEM((rows, width), low)
    return pl.pallas_call(
        functools.partial(middle_body, nz, units, slots, depth),
        out_shape=outs,
        in_specs=[pl.BlockSpec(memory_space=pltpu.SMEM)] + [vmem] * len(near) + [any_] * 8,
        out_specs=[any_] * 6 + [vmem] * (len(outs) - 6),
        scratch_shapes=[pltpu.VMEM(w.shape, low) for w in weights]
        + [pltpu.SemaphoreType.DMA((6,)), pltpu.VMEM(second_low.shape, low), pltpu.VMEM(second_low.shape, low)]
        + [pltpu.VMEM((4, rows, width), low)] * 2 + [pltpu.VMEM((2, rows, width), low)] * 2 + [part] * 4
        + [pltpu.SemaphoreType.DMA((2, 2, 2))] * 2 + [pltpu.SemaphoreType.DMA((2, 2))] * 2
        + [pltpu.VMEM((3, width, width), low), pltpu.SemaphoreType.DMA((6,))]
        + scatter_scratch(units, slots, nz),
        compiler_params=pltpu.CompilerParams(collective_id=5, has_side_effects=True, vmem_limit_bytes=VMEM_LIMIT),
        name="middle_back",
    )(bounds, *near, *weights, *feed)


eps_norm = 1e-05


def layer_norm(values_in, gain_vec, shift_vec):
    centre = values_in - jnp.mean(values_in, axis=-1, keepdims=True)
    spread = jnp.mean(centre * centre, axis=-1, keepdims=True)
    return centre * lax.rsqrt(spread + eps_norm) * gain_vec + shift_vec


def gelu_exact(values_in):
    return jax.nn.gelu(values_in, approximate=False)


def project(left, right):
    return jnp.einsum("gti,ij->gtj", left, right, preferred_element_type=jnp.float32)


def project_back(left, right):
    return jnp.einsum("gtj,ij->gti", left, right, preferred_element_type=jnp.float32)


def outer_sum(left, right):
    return jnp.einsum("gti,gtj->ij", left, right, preferred_element_type=jnp.float32)


ORDERS = ("zyx", "zxy") * 4 + ("zyx", "yxz", "zxy", "zyx", "xyz", "zxy", "yxz", "zyx", "xyz")
FEED_ORDERS = ("zyx", "zxy", "zyx", "yxz", "zxy", "zyx", "xyz", "zxy")
SHORT_ORDERS = ("zyx", "zxy", "zyx", "zxy", "zyx", "zxy", "yxz", "zyx", "xyz")


class Params(NamedTuple):
    w_query: jax.Array
    w_key: jax.Array
    w_value: jax.Array
    w_out: jax.Array
    c_query: jax.Array
    c_key: jax.Array
    c_value: jax.Array
    c_out: jax.Array
    w_text: jax.Array
    w_up: jax.Array
    w_down: jax.Array
    gain_attn: jax.Array
    bias_attn: jax.Array
    gain_cross: jax.Array
    bias_cross: jax.Array
    gain_feed: jax.Array
    bias_feed: jax.Array


BLOCKS, GAINS = 11, 6


def all_axes():
    return ("dp", "seq")


class Wires:
    def __init__(self, own):
        self.nz = lax.axis_size("dp") // 2
        self.rows, self.width = own.w_query.shape
        self.text_rows = own.w_text.shape[0]
        rows, width = self.rows, self.width
        up, down = own.w_up.shape[1] // width, own.w_down.shape[0] // rows
        self.units = [(g, 0, rows, 0, width) for g in range(9)]
        self.units += [(9, 0, rows, k * width, width) for k in range(up)]
        self.units += [(10, k * rows, rows, 0, width) for k in range(down)]
        feed = self.units[9:]
        self.feed_units = [(u,) for u in feed]
        self.near_units = [(u,) for u in self.units[:9]]
        self.orders = [ORDERS[i % len(ORDERS)] for i in range(len(self.units))]

    @staticmethod
    def fits(own, frames, text):
        rows, width = own.w_query.shape
        return (
            lax.axis_size("seq") == 4 and lax.axis_size("dp") % 2 == 0 and rows == 32 and width % 128 == 0
            and own.w_text.shape[0] % 8 == 0 and own.w_text.shape[0] + 8 <= rows
            and own.w_up.shape[0] == rows and own.w_up.shape[1] % width == 0
            and own.w_down.shape[0] % rows == 0 and own.w_down.shape[1] == width
            and frames.shape[0] == 1 and frames.shape[1] % 32 == 0 and text.shape[0] == 1 and text.shape[1] % 128 == 0
        )

    def gather(self, own, frames):
        gains = jnp.stack(own[BLOCKS:])
        gains = jnp.pad(gains, ((0, self.rows - self.text_rows - GAINS), (0, self.width - gains.shape[1])))
        arrays = list(own[:BLOCKS])
        arrays[8] = jnp.concatenate([own.w_text, gains], axis=0)
        *full, all_rows = gather_weights(arrays[:9], frames[0], self.units[:9], SHORT_ORDERS, self.nz)
        full += [lax.all_gather(v, all_axes(), axis=0, tiled=True) for v in arrays[9:]]
        mixed = full[8].reshape((-1, self.rows, self.width))
        full = [f.reshape((-1, f.shape[-1])) for f in full]
        full[8] = mixed[:, : self.text_rows].reshape((-1, self.width))
        gains = [mixed[:, self.text_rows + i, : own[BLOCKS + i].shape[0]].reshape((-1,)) for i in range(GAINS)]
        return Params(*full, *gains), all_rows.reshape((1, -1, self.width))

    def middle(self, cross, full, gain, feed):
        bounds, grad_second, *rest = cross
        near = [grad_second[0].astype(jnp.bfloat16), grad_second[0]] + [v[0] for v in rest] + [gain[None]]
        weights = (full.c_out, full.c_query, full.c_key, full.c_value, full.w_text, full.w_out)
        feed = [v.astype(jnp.bfloat16).reshape((self.nz, 2, 2, 2, -1, v.shape[-1])) for v in feed]
        units = [tuple((g - 9, *rest) for g, *rest in unit) for unit in self.feed_units]
        outs = middle_back(bounds[0], near, weights, feed, units, [FEED_ORDERS[i % len(FEED_ORDERS)] for i in range(len(units))], self.nz)
        dc_out, dc_query, dw_out, dc_key, dc_value, dw_text = outs[:6]
        return (dc_query, dc_key, dc_value, dc_out, dw_text, dw_out, *[v[None] for v in outs[6:9]], outs[9][0], outs[10][0], outs[11])

    def scatter(self, feed_sums, grads):
        low = [v.astype(jnp.bfloat16) for v in grads]
        shards = self.nz * 8
        rest = jnp.stack([v.reshape((shards, -1)) for v in low[BLOCKS:]], axis=1)
        rest = jnp.pad(rest, ((0, 0), (0, self.rows - self.text_rows - GAINS), (0, self.width - rest.shape[2])))
        low[8] = jnp.concatenate([low[8].reshape((shards, self.text_rows, self.width)), rest], axis=1)
        arrays = [v.reshape((self.nz, 2, 2, 2, -1, v.shape[-1])) for v in low[:BLOCKS]]
        sums = scatter_grads(arrays[:9], self.near_units, SHORT_ORDERS, self.nz)
        parts = (self.near_units, self.feed_units)
        *blocks, mixed = deliver((sums, feed_sums), parts, self.text_rows, [a.shape[4:] for a in arrays])
        gains = [mixed[i, : v.shape[0] // shards] for i, v in enumerate(grads[BLOCKS:])]
        return Params(*blocks, *gains)

    def share(self, arrays, number):
        return [v[None] for v in share_sums([a.reshape((2, 2, -1, self.width)) for a in arrays], number)]


class PlainWires:
    def gather(self, own, frames):
        full = Params(*[lax.all_gather(v, all_axes(), axis=0, tiled=True) for v in own])
        return full, lax.all_gather(frames, "seq", axis=1, tiled=True)

    def middle(self, cross, full, gain, feed):
        bounds, grad_second, cross_mix, cross_query, cross_keys, cross_values, two_low, first, text_part, proj_part, attended = cross
        low = jnp.bfloat16
        second_low = grad_second.astype(low)
        dc_out = outer_sum(cross_mix, second_low)
        grad_cross_mix = project_back(second_low, full.c_out).astype(low)
        cq_low, grad_ck, grad_cv = attention_back(False, bounds, cross_query, cross_keys, cross_values, grad_cross_mix)
        ck_low, cv_low = self.share([grad_ck, grad_cv], 3)
        dc_key = outer_sum(proj_part, ck_low)
        dc_value = outer_sum(proj_part, cv_low)
        grad_proj = (project_back(ck_low, full.c_key) + project_back(cv_low, full.c_value)).astype(low)
        dw_text = outer_sum(text_part, grad_proj)
        text_grad = project_back(grad_proj, full.w_text)
        dc_query = outer_sum(two_low, cq_low)
        back = jax.vjp(lambda v, s: layer_norm(v, s, jnp.zeros_like(s)), first, gain)[1]
        two_grad = project_back(cq_low, full.c_query)
        grad_first_ln, dgain = back(two_grad)
        grad_first = grad_second + grad_first_ln
        first_low = grad_first.astype(low)
        dw_out = outer_sum(attended, first_low)
        grad_attended = project_back(first_low, full.w_out).astype(low)
        return (
            dc_query, dc_key, dc_value, dc_out, dw_text, dw_out, text_grad, grad_first, grad_attended, dgain,
            jnp.sum(two_grad, axis=(0, 1)), None,
        )

    def scatter(self, feed_sums, grads):
        return Params(*[lax.psum_scatter(v, all_axes(), scatter_dimension=0, tiled=True) for v in grads])

    def share(self, arrays, number):
        return [lax.psum_scatter(a, "seq", scatter_dimension=1, tiled=True) for a in arrays]


def attention(causal, bounds, q, k, v):
    return attend(causal, bounds[0], q[0], k[0], v[0])[None]


def attention_back(causal, bounds, *operands):
    return [r[None] for r in attend_grads(causal, bounds[0], *[a[0] for a in operands])]


def on_device(frames, cotangent, text_states, frame_start, prompt_len, *params):
    own = Params(*params)
    low = jnp.bfloat16
    wires = Wires(own) if Wires.fits(own, frames, text_states) else PlainWires()
    full, all_frames = wires.gather(own, frames)
    wide = [v.astype(jnp.float32) for v in full[BLOCKS:]]
    frames_f = frames.astype(jnp.float32)
    frame_count = frames.shape[1]
    normed, norm_one_back = jax.vjp(layer_norm, frames_f, wide[0], wide[1])
    normed_low = normed.astype(low)
    normed_all = layer_norm(all_frames.astype(jnp.float32), wide[0], wide[1]).astype(low)
    query_rows = project(normed_low, full.w_query).astype(low)
    key_all = project(normed_all, full.w_key).astype(low)
    value_all = project(normed_all, full.w_value).astype(low)
    rank = lax.axis_index("seq")
    self_bounds = jnp.stack([jnp.full_like(frame_start, rank * frame_count), frame_start], axis=1)
    attended = attention(True, self_bounds, query_rows, key_all, value_all)
    first = frames_f + project(attended, full.w_out)
    text_count = text_states.shape[1]
    quarter = text_count // lax.axis_size("seq")
    text_start = rank * quarter
    text_part = lax.dynamic_slice_in_dim(text_states, text_start, quarter, 1)
    proj_all = project(text_states, full.w_text).astype(low)
    cross_keys = project(proj_all, full.c_key).astype(low)
    cross_values = project(proj_all, full.c_value).astype(low)
    proj_part = lax.dynamic_slice_in_dim(proj_all, text_start, quarter, 1)
    normed_two, norm_two_back = jax.vjp(layer_norm, first, wide[2], wide[3])
    normed_two_low = normed_two.astype(low)
    cross_query = project(normed_two_low, full.c_query).astype(low)
    cross_bounds = jnp.stack([prompt_len, prompt_len], axis=1)
    cross_mix = attention(False, cross_bounds, cross_query, cross_keys, cross_values)
    second = first + project(cross_mix, full.c_out)
    normed_three, norm_three_back = jax.vjp(layer_norm, second, wide[4], wide[5])
    three_low = normed_three.astype(low)
    hidden = project(three_low, full.w_up)
    activated, gelu_back = jax.vjp(gelu_exact, hidden)
    act_low = activated.astype(low)
    block_out = (second + project(act_low, full.w_down)).astype(low)
    grad_act = project_back(cotangent, full.w_down)
    dw_down = outer_sum(act_low, cotangent)
    grad_hidden = gelu_back(grad_act)[0].astype(low)
    dw_up = outer_sum(three_low, grad_hidden)
    grad_second_ln, dgain_feed, dbias_feed = norm_three_back(project_back(grad_hidden, full.w_up))
    grad_second = cotangent.astype(jnp.float32) + grad_second_ln
    cross = (cross_bounds, grad_second, cross_mix, cross_query, cross_keys, cross_values, normed_two_low, first, text_part, proj_part, attended)
    middle = wires.middle(cross, full, wide[2], (dw_up, dw_down))
    (
        dc_query, dc_key, dc_value, dc_out, dw_text, dw_out, text_grad, grad_first, grad_attended, dgain_cross,
        dbias_cross, feed_sums,
    ) = middle
    q_low, grad_k_all, grad_v_all = attention_back(
        True, self_bounds, query_rows, key_all, value_all, grad_attended
    )
    k_low, v_low = wires.share([grad_k_all, grad_v_all], 4)
    dw_query = outer_sum(normed_low, q_low)
    dw_key = outer_sum(normed_low, k_low)
    dw_value = outer_sum(normed_low, v_low)
    grad_normed = (
        project_back(q_low, full.w_query) + project_back(k_low, full.w_key) + project_back(v_low, full.w_value)
    )
    grad_frames_ln, dgain_attn, dbias_attn = norm_one_back(grad_normed)
    frames_grad = (grad_first + grad_frames_ln).astype(low)
    sums = wires.scatter(
        feed_sums,
        Params(
            dw_query, dw_key, dw_value, dw_out, dc_query, dc_key, dc_value, dc_out, dw_text, dw_up, dw_down,
            dgain_attn, dbias_attn, dgain_cross, dbias_cross, dgain_feed, dbias_feed,
        ),
    )
    return (block_out, frames_grad, text_grad, *sums)


def solution(mesh):
    both = P(all_axes(), None)
    rows, vector = P(*all_axes(), None), P(all_axes())
    item, whole = P("dp"), P("dp", None, None)
    return jax.shard_map(
        on_device,
        mesh=mesh,
        in_specs=(rows, rows, whole, item, item) + (both,) * BLOCKS + (vector,) * GAINS,
        out_specs=(rows,) * 3 + (both,) * BLOCKS + (vector,) * GAINS,
        check_vma=False,
    )
```

```python
import functools
from typing import NamedTuple
import jax
import jax.numpy as jnp
from jax import lax
from jax.experimental import pallas as pl
from jax.experimental.pallas import tpu as pltpu
from jax.sharding import PartitionSpec as P

MESH = pl.DeviceIdType.MESH

LAG = 2
VMEM_LIMIT = 60 * 1024 * 1024

def unit_ops(perm, nz):
    rank = {a: i for i, a in enumerate(perm)}
    ops = {}

    def source(j, fy, fx):
        differs = [a for a, f in (("z", j > 0), ("y", fy), ("x", fx)) if f]
        if not differs:
            return None
        last = max(differs, key=lambda a: rank[a])
        if last == "z":
            return ("z", j - 1, fy, fx)
        if last == "y":
            return ("y", j, 0, fx)
        return ("x", j, fy, 0)

    for j in range(nz):
        for fy in range(2):
            for fx in range(2):
                for axis in "zyx":
                    flags = {"z": j > 0, "y": fy, "x": fx}
                    if axis != "z" and flags[axis]:
                        continue
                    if any(flags[a] and rank[a] > rank[axis] for a in "zyx" if a != axis):
                        continue
                    if axis == "z" and j == nz - 1:
                        continue
                    ops[(axis, j, fy, fx)] = source(j, fy, fx)
    return ops

def make_schedule(perms, nz, lag=LAG, window=None):
    ops = {}
    for u, perm in enumerate(perms):
        for key, dep in unit_ops(perm, nz).items():
            ops[(u,) + key] = None if dep is None else (u,) + dep
    children = {}
    for op, dep in ops.items():
        children.setdefault(dep, []).append(op)
    height = {}

    def tall(op):
        if op not in height:
            height[op] = 1 + max([tall(c) for c in children.get(op, [])], default=0)
        return height[op]

    for op in ops:
        tall(op)
    done, slots, left = {}, [], set(ops)
    while left:
        t = len(slots)
        slot = {}
        for axis in "zyx":
            ready = [op for op in left if op[1] == axis and (ops[op] is None or (ops[op] in done and done[ops[op]] + lag <= t))]
            if ready:
                slot[axis] = min(ready, key=lambda op: (op[0] // window if window else 0, -height[op], op[0], op))
        for axis, op in slot.items():
            done[op] = t
            left.discard(op)
        slots.append(slot)
    return slots

def nth_table(nz):
    rows = []
    for z in range(nz):
        offs = sorted((p - z for p in range(nz)), key=lambda o: (abs(o), o if z % 2 else -o))
        rows.append([z + o for o in offs])
    return rows

def pick(values, z):
    out = 0
    for i, v in enumerate(values):
        out = out + v * jnp.where(z == i, 1, 0)
    return out

UP, DOWN, YY, XX, CORE = range(5)
WAYS_OF = dict(z=(UP, DOWN), y=(YY,), x=(XX,))

class Place:
    def __init__(self, nz):
        d, s = lax.axis_index("dp"), lax.axis_index("seq")
        self.nz = nz
        self.z, self.y, self.x, self.c = d // 2, d % 2, s // 2, s % 2
        z, y, x, c = self.z, self.y, self.x, self.c
        self.device = [
            ((z + 1) * 2 + y, x * 2 + c),
            ((z - 1) * 2 + y, x * 2 + c),
            (z * 2 + 1 - y, x * 2 + c),
            (z * 2 + y, (1 - x) * 2 + c),
            (z * 2 + y, x * 2 + 1 - c),
        ]
        self.nth = [[row[j] for row in nth_table(nz)] for j in range(nz)]

    def greet(self):
        barrier = pltpu.get_barrier_semaphore()
        has_up, has_down = self.z + 1 < self.nz, self.z > 0
        for way in range(5):
            def hello(way=way):
                pl.semaphore_signal(barrier, inc=1, device_id=self.device[way], device_id_type=MESH)
            if way < YY:
                pl.when(has_up if way == UP else has_down)(hello)
            else:
                hello()
        edge = jnp.where(self.z == 0, 1, 0) + jnp.where(self.z == self.nz - 1, 1, 0)
        pl.semaphore_wait(barrier, 5 - edge)

    def gather_moves(self, axis, j, fy, fx):
        z, y, x, nz = self.z, self.y, self.x, self.nz
        py, px = (1 - y if fy else y), (1 - x if fx else x)
        if axis == "z":
            out = [(UP, (z - j >= 0) & (z + 1 < nz), (z - j, py, px)), (DOWN, (z + j < nz) & (z > 0), (z + j, py, px))]
            come = [(UP, z - 1 - j >= 0, (z - 1 - j, py, px)), (DOWN, z + 1 + j < nz, (z + 1 + j, py, px))]
        else:
            pz = pick(self.nth[j], z)
            there = (pz, 1 - y, px) if axis == "y" else (pz, py, 1 - x)
            way = YY if axis == "y" else XX
            out = [(way, None, (pz, py, px))]
            come = [(way, None, there)]
        return out, come

def when(cond, fn):
    if cond is None:
        fn()
    else:
        pl.when(cond)(fn)

BACK = (DOWN, UP, YY, XX)


def scatter_steps(here, units, slots, depth, ins, total, twin, landed, send_sem, recv_sem, core_send, core_recv, local_sem):
    nz = here.nz
    z, y, x, c = here.z, here.y, here.x, here.c
    steps = slots[::-1]
    numbers, order = {}, []
    for t, slot in enumerate(steps):
        for axis, op in slot.items():
            for way in WAYS_OF[axis]:
                numbers[way, t] = len(numbers)
            if op[0] not in order:
                order.append(op[0])

    def plane(u, b, which):
        g, r0, rn, c0, cn = units[u][b]
        return ins[g].at[:, :, :, which, pl.ds(r0, rn), pl.ds(c0, cn)]

    def rows_of(buffer, u, b):
        rn = units[u][b][2]
        return buffer.at[u, :, :, :, pl.ds(b * rn, rn)]

    def local(u, b):
        return pltpu.make_async_copy(plane(u, b, c), rows_of(total, u, b), local_sem.at[u, b])

    def across(u, b):
        return pltpu.make_async_remote_copy(
            src_ref=plane(u, b, 1 - c), dst_ref=rows_of(twin, u, b), send_sem=core_send.at[u, b],
            recv_sem=core_recv.at[u, b], device_id=here.device[CORE], device_id_type=MESH,
        )

    def remote(u, way, t, p):
        i = numbers[way, t]
        return pltpu.make_async_remote_copy(
            src_ref=total.at[u, p[0], p[1], p[2]], dst_ref=landed.at[i], send_sem=send_sem.at[i], recv_sem=recv_sem.at[i],
            device_id=here.device[BACK[way]], device_id_type=MESH,
        )

    ahead = 3
    blocks = range(len(units[0]))
    for u in order[:ahead]:
        for b in blocks:
            local(u, b).start()
    here.greet()
    for u in order[:ahead]:
        for b in blocks:
            across(u, b).start()

    def join(u):
        later = order.index(u) + ahead
        if later < len(order):
            for b in blocks:
                local(order[later], b).start()
                across(order[later], b).start()
        for b in blocks:
            local(u, b).wait()
            across(u, b).wait_recv()

        @pl.loop(0, nz)
        def _(a):
            for b in range(2):
                for e in range(2):
                    total[u, a, b, e] = (
                        total[u, a, b, e].astype(jnp.float32) + twin[u, a, b, e].astype(jnp.float32)
                    ).astype(jnp.bfloat16)

    joined = set()
    for t in range(len(steps) + depth):
        if t < len(steps):
            for axis, (u, _, j, fy, fx) in steps[t].items():
                if u not in joined:
                    joined.add(u)
                    join(u)
                for way, cond, p in here.gather_moves(axis, j, fy, fx)[1]:
                    when(cond, lambda u=u, way=way, p=p: remote(u, way, t, p).start())
        if t >= depth:
            s = t - depth
            for axis, (u, _, j, fy, fx) in steps[s].items():
                for way, cond, p in here.gather_moves(axis, j, fy, fx)[0]:
                    def add(u=u, way=way, p=p):
                        i = numbers[way, s]
                        pltpu.make_async_copy(landed.at[i], landed.at[i], recv_sem.at[i]).wait()
                        total[u, p[0], p[1], p[2]] = (
                            total[u, p[0], p[1], p[2]].astype(jnp.float32) + landed[i].astype(jnp.float32)
                        ).astype(jnp.bfloat16)
                    when(cond, add)
        yield t
    for t, slot in enumerate(steps):
        for axis, (u, _, j, fy, fx) in slot.items():
            for way, cond, p in here.gather_moves(axis, j, fy, fx)[1]:
                when(cond, lambda u=u, way=way, p=p: remote(u, way, t, p).wait_send())
    for u in order:
        for b in blocks:
            across(u, b).wait_send()


def unit_shape(units):
    return sum(block[2] for block in units[0]), units[0][0][4]


def scatter_scratch(units, slots, nz):
    rows, columns = unit_shape(units)
    count = sum(len(WAYS_OF[axis]) for slot in slots for axis in slot)
    plane = (len(units), nz, 2, 2, rows, columns)
    return [
        pltpu.VMEM(plane, jnp.bfloat16),
        pltpu.VMEM(plane, jnp.bfloat16),
        pltpu.VMEM((count, rows, columns), jnp.bfloat16),
        pltpu.SemaphoreType.DMA((count,)),
        pltpu.SemaphoreType.DMA((count,)),
        pltpu.SemaphoreType.DMA((len(units), len(units[0]))),
        pltpu.SemaphoreType.DMA((len(units), len(units[0]))),
        pltpu.SemaphoreType.DMA((len(units), len(units[0]))),
    ]


def scatter_body(nz, units, slots, n, depth, *refs):
    ins, out = refs[:n], refs[n]
    here = Place(nz)
    for _ in scatter_steps(here, units, slots, depth, ins, *refs[n + 1:]):
        pass
    total = refs[n + 1]
    for u in range(len(units)):
        out[u] = total[u, here.z, here.y, here.x].astype(jnp.float32)


def scatter_grads(arrays, units, perms, nz, depth=2):
    n = len(arrays)
    slots = make_schedule(perms, nz, lag=depth + 1)
    rows, columns = unit_shape(units)
    return pl.pallas_call(
        functools.partial(scatter_body, nz, units, slots, n, depth),
        out_shape=jax.ShapeDtypeStruct((len(units), rows, columns), jnp.float32),
        in_specs=[pl.BlockSpec(memory_space=pl.ANY)] * n,
        out_specs=pl.BlockSpec(memory_space=pltpu.VMEM),
        scratch_shapes=scatter_scratch(units, slots, nz),
        compiler_params=pltpu.CompilerParams(collective_id=2, has_side_effects=True, vmem_limit_bytes=VMEM_LIMIT),
        name="scatter_grads",
    )(*arrays)


def share_body(n, chunk, *refs):
    ins, outs = refs[:n], refs[n:2 * n]
    twins, sums, landed = refs[2 * n:3 * n], refs[3 * n:4 * n], refs[4 * n:5 * n]
    core_send, core_recv, x_send, x_recv = refs[5 * n:]
    d, s = lax.axis_index("dp"), lax.axis_index("seq")
    x, c = s // 2, s % 2
    core, over = (d, x * 2 + 1 - c), (d, (1 - x) * 2 + c)
    barrier = pltpu.get_barrier_semaphore()
    for other in (core, over):
        pl.semaphore_signal(barrier, inc=1, device_id=other, device_id_type=MESH)
    pl.semaphore_wait(barrier, 2)
    pieces = [(g, k, pl.ds(k * chunk, chunk)) for g in range(n) for k in range(ins[g].shape[2] // chunk)]

    def across(i, far):
        g, k, rows = pieces[i]
        part = 1 - x if far else x
        return pltpu.make_async_remote_copy(
            src_ref=ins[g].at[part, 1 - c, rows], dst_ref=twins[g].at[1 if far else 0, rows],
            send_sem=core_send.at[1 if far else 0, i], recv_sem=core_recv.at[1 if far else 0, i],
            device_id=core, device_id_type=MESH,
        )

    def beyond(i):
        g, k, rows = pieces[i]
        return pltpu.make_async_remote_copy(
            src_ref=sums[g].at[rows], dst_ref=landed[g].at[rows], send_sem=x_send.at[i], recv_sem=x_recv.at[i],
            device_id=over, device_id_type=MESH,
        )

    for far in (True, False):
        for i in range(len(pieces)):
            across(i, far).start()
    for i, (g, k, rows) in enumerate(pieces):
        across(i, True).wait_recv()
        sums[g][rows] = (ins[g][1 - x, c, rows].astype(jnp.float32) + twins[g][1, rows].astype(jnp.float32)).astype(jnp.bfloat16)
        beyond(i).start()
    for i, (g, k, rows) in enumerate(pieces):
        across(i, False).wait_recv()
        beyond(i).wait_recv()
        outs[g][rows] = (
            ins[g][x, c, rows].astype(jnp.float32) + twins[g][0, rows].astype(jnp.float32) + landed[g][rows].astype(jnp.float32)
        ).astype(jnp.bfloat16)
    for i in range(len(pieces)):
        across(i, True).wait_send()
        across(i, False).wait_send()
        beyond(i).wait_send()


def share_sums(arrays, number):
    n = len(arrays)
    chunk = 32
    count = sum(a.shape[2] // chunk for a in arrays)
    return pl.pallas_call(
        functools.partial(share_body, n, chunk),
        out_shape=[jax.ShapeDtypeStruct(a.shape[2:], a.dtype) for a in arrays],
        in_specs=[pl.BlockSpec(memory_space=pltpu.VMEM)] * n,
        out_specs=[pl.BlockSpec(memory_space=pltpu.VMEM)] * n,
        scratch_shapes=[pltpu.VMEM((2,) + a.shape[2:], a.dtype) for a in arrays]
        + [pltpu.VMEM(a.shape[2:], a.dtype) for a in arrays] * 2
        + [pltpu.SemaphoreType.DMA((2, count))] * 2
        + [pltpu.SemaphoreType.DMA((count,))] * 2,
        compiler_params=pltpu.CompilerParams(collective_id=number, has_side_effects=True, vmem_limit_bytes=32 * 1024 * 1024),
        name="share_sums",
    )(*arrays)


def deliver_body(parts, text_rows, n, *refs):
    ins, outs = refs[:n], refs[n:]
    for sums, units in zip(ins, parts):
        for u, unit in enumerate(units):
            for b, (g, r0, rn, c0, cn) in enumerate(unit):
                if g == 8:
                    outs[g][...] = sums[u, :text_rows]
                    outs[-1][...] = sums[u, text_rows:text_rows + 8]
                else:
                    outs[g][r0:r0 + rn, c0:c0 + cn] = sums[u, b * rn:(b + 1) * rn]


def deliver(sums, parts, text_rows, shapes):
    shapes = [(text_rows,) + s[1:] if g == 8 else s for g, s in enumerate(shapes)] + [(8, sums[0].shape[2])]
    return pl.pallas_call(
        functools.partial(deliver_body, parts, text_rows, len(sums)),
        out_shape=[jax.ShapeDtypeStruct(s, jnp.float32) for s in shapes],
        compiler_params=pltpu.CompilerParams(vmem_limit_bytes=16 * 1024 * 1024),
        name="deliver",
    )(*sums)


def pair_scores(bounds_ref, q, k, keep, causal):
    s = lax.dot_general(jnp.where(keep, q, 0), k, (((1,), (1,)), ((), ())), preferred_element_type=jnp.float32)
    col = lax.broadcasted_iota(jnp.int32, s.shape, 1)
    if causal:
        row = lax.broadcasted_iota(jnp.int32, s.shape, 0) + bounds_ref[0]
        seen = (col <= row) & ((col >= bounds_ref[1]) | (col == row))
    else:
        seen = col < bounds_ref[0]
    s = jnp.where(seen, s * 0.125, -1e30)
    e = jnp.exp(s - jnp.max(s, axis=1, keepdims=True))
    return e * (1.0 / jnp.sum(e, axis=1, keepdims=True))


def halves(width):
    lane = lax.broadcasted_iota(jnp.int32, (1, width), 1)
    return [(lane >= 64 * h) & (lane < 64 * h + 64) for h in range(width // 64)]


def attend_body(causal, bounds_ref, q_ref, k_ref, v_ref, out_ref):
    q, k, v = q_ref[...], k_ref[...], v_ref[...]
    out = None
    for keep in halves(q.shape[1]):
        p = pair_scores(bounds_ref, q, k, keep, causal)
        o = jnp.dot(p.astype(jnp.bfloat16), v, preferred_element_type=jnp.float32)
        out = o if out is None else jnp.where(keep, o, out)
    out_ref[...] = out.astype(jnp.bfloat16)


def attend_back_body(causal, bounds_ref, q_ref, k_ref, v_ref, g_ref, dq_ref, dk_ref, dv_ref):
    q, k, v, g = q_ref[...], k_ref[...], v_ref[...], g_ref[...]
    dq = dk = dv = None
    for keep in halves(q.shape[1]):
        p = pair_scores(bounds_ref, q, k, keep, causal)
        dp = lax.dot_general(jnp.where(keep, g, 0), v, (((1,), (1,)), ((), ())), preferred_element_type=jnp.float32)
        ds = (p * (dp - jnp.sum(p * dp, axis=1, keepdims=True))).astype(jnp.bfloat16)
        a = jnp.dot(ds, k, preferred_element_type=jnp.float32)
        b = lax.dot_general(ds, q, (((0,), (0,)), ((), ())), preferred_element_type=jnp.float32)
        e = lax.dot_general(p.astype(jnp.bfloat16), g, (((0,), (0,)), ((), ())), preferred_element_type=jnp.float32)
        if dq is None:
            dq, dk, dv = a, b, e
        else:
            dq, dk, dv = jnp.where(keep, a, dq), jnp.where(keep, b, dk), jnp.where(keep, e, dv)
    dq_ref[...] = (dq * 0.125).astype(jnp.bfloat16)
    dk_ref[...] = (dk * 0.125).astype(jnp.bfloat16)
    dv_ref[...] = dv.astype(jnp.bfloat16)


def attend_call(body, causal, bounds, operands, n_out_rows):
    width = operands[0].shape[1]
    spec = [pl.BlockSpec((a.shape[0], 128), lambda i: (0, i)) for a in operands]
    return pl.pallas_call(
        functools.partial(body, causal),
        grid=(width // 128,),
        out_shape=[jax.ShapeDtypeStruct((r, width), jnp.bfloat16) for r in n_out_rows],
        in_specs=[pl.BlockSpec(memory_space=pltpu.SMEM)] + spec,
        out_specs=[pl.BlockSpec((r, 128), lambda i: (0, i)) for r in n_out_rows],
        compiler_params=pltpu.CompilerParams(vmem_limit_bytes=32 * 1024 * 1024),
        name=("self_" if causal else "cross_") + body.__name__,
    )(bounds, *operands)


def attend(causal, bounds, q, k, v):
    return attend_call(attend_body, causal, bounds, (q, k, v), [q.shape[0]])[0]


def attend_grads(causal, bounds, q, k, v, g):
    return attend_call(attend_back_body, causal, bounds, (q, k, v, g), [q.shape[0], k.shape[0], k.shape[0]])


def dot_tt(a, b):
    return lax.dot_general(a, b, (((0,), (0,)), ((), ())), preferred_element_type=jnp.float32)


def dot_nt(a, b):
    return lax.dot_general(a, b, (((1,), (1,)), ((), ())), preferred_element_type=jnp.float32)


def norm_parts(v):
    centre = v - jnp.mean(v, axis=1, keepdims=True)
    rate = lax.rsqrt(jnp.mean(centre * centre, axis=1, keepdims=True) + eps_norm)
    return centre * rate, rate


def norm_grads(v, gain, h):
    xh, rate = norm_parts(v)
    hg = h * gain
    dv = (hg - jnp.mean(hg, axis=1, keepdims=True) - xh * jnp.mean(hg * xh, axis=1, keepdims=True)) * rate
    return dv, jnp.sum(h * xh, axis=0, keepdims=True), jnp.sum(h, axis=0, keepdims=True)


class Share:
    def __init__(self, here, mine, twins, sums, landed, core_send, core_recv, x_send, x_recv, chunk):
        self.here, self.mine, self.twins, self.sums, self.landed = here, mine, twins, sums, landed
        self.sems, self.chunk = (core_send, core_recv, x_send, x_recv), chunk

    def columns(self, k):
        return pl.ds(k * self.chunk, self.chunk)

    def across(self, g, k, far):
        here, f = self.here, 1 if far else 0
        part = (1 - here.x if far else here.x) * 2 + 1 - here.c
        return pltpu.make_async_remote_copy(
            src_ref=self.mine[g].at[part, :, self.columns(k)], dst_ref=self.twins[g].at[f, :, self.columns(k)],
            send_sem=self.sems[0].at[f, g, k], recv_sem=self.sems[1].at[f, g, k],
            device_id=here.device[CORE], device_id_type=MESH,
        )

    def beyond(self, g, k):
        return pltpu.make_async_remote_copy(
            src_ref=self.sums[g].at[:, self.columns(k)], dst_ref=self.landed[g].at[:, self.columns(k)],
            send_sem=self.sems[2].at[g, k], recv_sem=self.sems[3].at[g, k],
            device_id=self.here.device[XX], device_id_type=MESH,
        )

    def send(self, k):
        for far in (True, False):
            for g in range(len(self.mine)):
                self.across(g, k, far).start()

    def forward(self, k):
        here, cols = self.here, slice(k * self.chunk, (k + 1) * self.chunk)
        for g, mine in enumerate(self.mine):
            self.across(g, k, True).wait_recv()
            part = (1 - here.x) * 2 + here.c
            self.sums[g][:, cols] = (
                mine[part, :, cols].astype(jnp.float32) + self.twins[g][1, :, cols].astype(jnp.float32)
            ).astype(jnp.bfloat16)
            self.beyond(g, k).start()

    def collect(self, g, k):
        here, cols = self.here, slice(k * self.chunk, (k + 1) * self.chunk)
        self.across(g, k, False).wait_recv()
        self.beyond(g, k).wait_recv()
        return (
            self.mine[g][here.x * 2 + here.c, :, cols].astype(jnp.float32) + self.twins[g][0, :, cols].astype(jnp.float32)
            + self.landed[g][:, cols].astype(jnp.float32)
        ).astype(jnp.bfloat16)

    def finish(self, chunks):
        for g in range(len(self.mine)):
            for k in range(chunks):
                self.across(g, k, True).wait_send()
                self.across(g, k, False).wait_send()
                self.beyond(g, k).wait_send()


class Pace:
    def __init__(self, steps, every):
        self.steps, self.every, self.owed = steps, every, 0.0

    def spend(self, time):
        self.owed += time
        while self.owed >= self.every:
            self.owed -= self.every
            next(self.steps, None)


def pair_grads(bounds_ref, causal, q, k, v, g, between):
    dq = dk = dv = None
    for keep in halves(q.shape[1]):
        p = pair_scores(bounds_ref, q, k, keep, causal)
        dp = dot_nt(jnp.where(keep, g, 0), v)
        ds = (p * (dp - jnp.sum(p * dp, axis=1, keepdims=True))).astype(jnp.bfloat16)
        a = jnp.dot(ds, k, preferred_element_type=jnp.float32)
        b = dot_tt(ds, q)
        e = dot_tt(p.astype(jnp.bfloat16), g)
        if dq is None:
            dq, dk, dv = a, b, e
        else:
            dq, dk, dv = jnp.where(keep, a, dq), jnp.where(keep, b, dk), jnp.where(keep, e, dv)
        between()
    return [(r * s).astype(jnp.bfloat16) for r, s in ((dq, 0.125), (dk, 0.125), (dv, 1.0))]


def middle_body(nz, units, slots, depth, *refs):
    (bounds, second_low, grad_second, cross_mix, cross_query, cross_keys, cross_values, two_low, first, text_part,
     proj_part, attended, gain) = refs[:13]
    weights, feed = refs[13:19], refs[19:21]
    placed = refs[21:27]
    text_grad, grad_first, grad_attended, dgain, dbias, sums = refs[27:33]
    held, (weight_sem, mixed, first_low, grad_ck, grad_cv, twin_k, twin_v, sum_k, sum_v, land_k, land_v) = refs[33:39], refs[39:50]
    share_sems, stage, stage_sem, scatter = refs[50:54], refs[54], refs[55], refs[56:]
    here = Place(nz)
    loads = [pltpu.make_async_copy(w, h, weight_sem.at[i]) for i, (w, h) in enumerate(zip(weights, held))]
    for cp in loads:
        cp.start()
    c_out, c_query, c_key, c_value, w_text, w_out = held
    steps = scatter_steps(here, units, slots, depth, feed, *scatter)
    low = jnp.bfloat16
    width = second_low.shape[1]
    rows = text_part.shape[0]
    tiles = [slice(i, i + 256) for i in range(0, width, 256)]
    share = Share(here, (grad_ck, grad_cv), (twin_k, twin_v), (sum_k, sum_v), (land_k, land_v), *share_sems, width // 2)

    pace = Pace(steps, 32.0 / (len(slots) + depth))
    spend = pace.spend

    def stored(i):
        src = stage.at[i % 3, pl.ds(0, placed[i].shape[0])]
        return pltpu.make_async_copy(src, placed[i], stage_sem.at[i])

    next(steps)
    loads[0].wait()
    for n in tiles:
        mixed[:, n] = dot_nt(second_low[...], c_out[n, :]).astype(low)
        spend(0.4)
    for n in tiles:
        stage[0, n, :] = dot_tt(cross_mix[:, n], second_low[...]).astype(low)
        spend(0.55)
    stored(0).start()
    pairs = width // 128
    for i in range(pairs):
        n = slice(i * 128, i * 128 + 128)
        dq, dk, dv = pair_grads(bounds, False, cross_query[:, n], cross_keys[:, n], cross_values[:, n], mixed[:, n], lambda: spend(0.72))
        mixed[:, n] = dq
        grad_ck[:, :, n] = dk.reshape(4, rows, 128)
        grad_cv[:, :, n] = dv.reshape(4, rows, 128)
        if i == pairs // 2 - 1:
            share.send(0)
    share.send(1)
    share.forward(0)
    loads[1].wait()
    for n in tiles:
        grad_first[:, n] = dot_nt(mixed[...], c_query[n, :])
        spend(0.4)
    share.forward(1)
    dv, dg, db = norm_grads(first[...], gain[...], grad_first[...])
    dgain[...] = dg
    dbias[...] = db
    dv = grad_second[...] + dv
    grad_first[...] = dv
    first_low[...] = dv.astype(low)
    spend(2.0)
    loads[5].wait()
    for n in tiles:
        grad_attended[:, n] = dot_nt(first_low[...], w_out[n, :]).astype(low)
        spend(0.4)
    for n in tiles:
        stage[1, n, :] = dot_tt(two_low[:, n], mixed[...]).astype(low)
        spend(0.55)
    stored(1).start()
    for n in tiles:
        stage[2, n, :] = dot_tt(attended[:, n], first_low[...]).astype(low)
        spend(0.55)
    stored(2).start()
    ck = jnp.concatenate([share.collect(0, k) for k in range(2)], axis=1)
    cv = jnp.concatenate([share.collect(1, k) for k in range(2)], axis=1)
    for i in (2, 3, 4):
        loads[i].wait()
    stored(0).wait()
    stored(1).wait()
    for n in tiles:
        stage[0, n, :] = dot_tt(proj_part[:, n], ck).astype(low)
        stage[1, n, :] = dot_tt(proj_part[:, n], cv).astype(low)
        spend(0.7)
    stored(3).start()
    stored(4).start()
    proj = []
    for n in tiles:
        proj.append((dot_nt(ck, c_key[n, :]) + dot_nt(cv, c_value[n, :])).astype(low))
        spend(0.5)
    proj = jnp.concatenate(proj, axis=1)
    stored(2).wait()
    for i in range(0, text_part.shape[1], 256):
        n = slice(i, i + 256)
        stage[2, n, :] = dot_tt(text_part[:, n], proj).astype(low)
        text_grad[:, n] = dot_nt(proj, w_text[n, :])
        spend(0.7)
    stored(5).start()
    for _ in steps:
        pass
    share.finish(2)
    for i in (3, 4, 5):
        stored(i).wait()
    total = scatter[0]
    for u in range(len(units)):
        sums[u] = total[u, here.z, here.y, here.x].astype(jnp.float32)


def middle_back(bounds, near, weights, feed, units, perms, nz, depth=3):
    slots = make_schedule(perms, nz, lag=depth + 1)
    second_low, text_part = near[0], near[8]
    width, rows, text_width = second_low.shape[1], text_part.shape[0], text_part.shape[1]
    low, wide = jnp.bfloat16, jnp.float32
    square = jax.ShapeDtypeStruct((width, width), low)
    outs = [square] * 5 + [jax.ShapeDtypeStruct((text_width, width), low)]
    outs += [jax.ShapeDtypeStruct(text_part.shape, wide), jax.ShapeDtypeStruct(second_low.shape, wide)]
    outs += [jax.ShapeDtypeStruct(second_low.shape, low)] + [jax.ShapeDtypeStruct((1, width), wide)] * 2
    outs += [jax.ShapeDtypeStruct((len(units),) + unit_shape(units), wide)]
    vmem, any_ = pl.BlockSpec(memory_space=pltpu.VMEM), pl.BlockSpec(memory_space=pl.ANY)
    part = pltpu.VMEM((rows, width), low)
    return pl.pallas_call(
        functools.partial(middle_body, nz, units, slots, depth),
        out_shape=outs,
        in_specs=[pl.BlockSpec(memory_space=pltpu.SMEM)] + [vmem] * len(near) + [any_] * 8,
        out_specs=[any_] * 6 + [vmem] * (len(outs) - 6),
        scratch_shapes=[pltpu.VMEM(w.shape, low) for w in weights]
        + [pltpu.SemaphoreType.DMA((6,)), pltpu.VMEM(second_low.shape, low), pltpu.VMEM(second_low.shape, low)]
        + [pltpu.VMEM((4, rows, width), low)] * 2 + [pltpu.VMEM((2, rows, width), low)] * 2 + [part] * 4
        + [pltpu.SemaphoreType.DMA((2, 2, 2))] * 2 + [pltpu.SemaphoreType.DMA((2, 2))] * 2
        + [pltpu.VMEM((3, width, width), low), pltpu.SemaphoreType.DMA((6,))]
        + scatter_scratch(units, slots, nz),
        compiler_params=pltpu.CompilerParams(collective_id=5, has_side_effects=True, vmem_limit_bytes=VMEM_LIMIT),
        name="middle_back",
    )(bounds, *near, *weights, *feed)


class Gather:
    def __init__(self, here, units, slots, depth, given, held, outs, rows_out, sems):
        self.here, self.units, self.slots, self.depth = here, units, slots, depth
        self.outs, self.rows_out = outs, rows_out
        self.ins, self.rows_in = held[:-1], held[-1]
        (self.send_sem, self.recv_sem, self.core_send, self.core_recv, self.local_sem, self.rows_send,
         self.rows_recv) = sems
        self.last = {}
        for t, slot in enumerate(slots):
            for u, axis, j, fy, fx in slot.values():
                self.last[dict(z=(u, fy, fx), y=(u, 1, fx), x=(u, fy, 1))[axis]] = t
        self.done = -1
        self.loads = [pltpu.make_async_copy(given[g], held[g], self.local_sem.at[g]) for g in range(len(held))]
        self.steps = self.run()

    def piece(self, u, p):
        g, r0, rn, c0, cn = self.units[u]
        return self.outs[g].at[p[0], p[1], p[2], self.here.c, pl.ds(r0, rn), pl.ds(c0, cn)]

    def corner(self, u, fy, fx, which):
        g, r0, rn, c0, cn = self.units[u]
        here = self.here
        return self.outs[g].at[
            :, 1 - here.y if fy else here.y, 1 - here.x if fx else here.x, which, pl.ds(r0, rn), pl.ds(c0, cn)
        ]

    def remote(self, u, way, t, p, mine):
        ref = self.piece(u, p)
        g, r0, rn, c0, cn = self.units[u]
        return pltpu.make_async_remote_copy(
            src_ref=self.ins[g].at[pl.ds(r0, rn), pl.ds(c0, cn)] if mine else ref, dst_ref=ref,
            send_sem=self.send_sem.at[way, t], recv_sem=self.recv_sem.at[way, t],
            device_id=self.here.device[way], device_id_type=MESH,
        )

    def across(self, u, fy, fx):
        ref = self.corner(u, fy, fx, self.here.c)
        i = fy * 2 + fx
        return pltpu.make_async_remote_copy(
            src_ref=ref, dst_ref=ref, send_sem=self.core_send.at[u, i], recv_sem=self.core_recv.at[u, i],
            device_id=self.here.device[CORE], device_id_type=MESH,
        )

    def rows_over(self, src, dst, way, i):
        return pltpu.make_async_remote_copy(
            src_ref=src, dst_ref=dst, send_sem=self.rows_send.at[i], recv_sem=self.rows_recv.at[i],
            device_id=self.here.device[way], device_id_type=MESH,
        )

    def run(self):
        here, slots, depth, n = self.here, self.slots, self.depth, len(self.outs)
        z, y, x, c = here.z, here.y, here.x, here.c
        own = [pltpu.make_async_copy(self.ins[g], self.outs[g].at[z, y, x, c], self.local_sem.at[g]) for g in range(n)]
        own.append(pltpu.make_async_copy(self.rows_in, self.rows_out.at[x, c], self.local_sem.at[n]))
        for cp in self.loads:
            cp.start()
        here.greet()
        for cp in self.loads:
            cp.wait()
        for cp in own:
            cp.start()
        beside = self.rows_out.at[1 - x, c]
        self.rows_moves = [
            self.rows_over(self.rows_in, self.rows_out.at[x, c], XX, 0),
            self.rows_over(self.rows_in, self.rows_out.at[x, c], CORE, 1),
            self.rows_over(beside, beside, CORE, 2),
        ]
        self.rows_moves[0].start()
        self.rows_moves[1].start()
        for t in range(len(slots) + depth):
            if t < len(slots):
                for axis, (u, _, j, fy, fx) in slots[t].items():
                    for way, cond, p in here.gather_moves(axis, j, fy, fx)[0]:
                        when(cond, lambda u=u, way=way, p=p: self.remote(u, way, t, p, (j, fy, fx) == (0, 0, 0)).start())
            if t == depth - 1:
                for cp in own:
                    cp.wait()
            if t == 6:
                pltpu.make_async_copy(beside, beside, self.rows_recv.at[0]).wait()
                self.rows_moves[2].start()
            if t >= depth:
                for axis, (u, _, j, fy, fx) in slots[t - depth].items():
                    for way, cond, p in here.gather_moves(axis, j, fy, fx)[1]:
                        def got(u=u, way=way, p=p):
                            ref = self.piece(u, p)
                            pltpu.make_async_copy(ref, ref, self.recv_sem.at[way, t - depth]).wait()
                        when(cond, got)
                for key in sorted(self.last):
                    if self.last[key] == t - depth:
                        self.across(*key).start()
            self.done = t
            yield t
        for t, slot in enumerate(slots):
            for axis, (u, _, j, fy, fx) in slot.items():
                for way, cond, p in here.gather_moves(axis, j, fy, fx)[0]:
                    when(cond, lambda u=u, way=way, p=p: self.remote(u, way, t, p, (j, fy, fx) == (0, 0, 0)).wait_send())
        for u, fy, fx in sorted(self.last):
            self.across(u, fy, fx).wait_send()
        for cp in self.rows_moves:
            cp.wait_send()

    def advance(self, t):
        while self.done < min(t, len(self.slots) + self.depth - 1):
            next(self.steps)

    def frames(self):
        here = self.here
        self.advance(8)
        for i, ref in ((1, self.rows_out.at[here.x, 1 - here.c]), (2, self.rows_out.at[1 - here.x, 1 - here.c])):
            pltpu.make_async_copy(ref, ref, self.rows_recv.at[i]).wait()

    def arrived(self, u):
        self.advance(max(t for key, t in self.last.items() if key[0] == u) + self.depth + 1)
        for fy in range(2):
            for fx in range(2):
                ref = self.corner(u, fy, fx, 1 - self.here.c)
                pltpu.make_async_copy(ref, ref, self.core_recv.at[u, fy * 2 + fx]).wait()


def ahead_body(nz, units, slots, depth, every, *refs):
    bounds, frames, text, cot = refs[:4]
    given = refs[4:16]
    full, rows_out, dw_up, dw_down = refs[16:27], refs[27], refs[28], refs[29]
    (gains, own_low, q_out, k_out, v_out, attended, first, two_low, cross_query, cross_keys, cross_values, cross_mix,
     proj, block_out, grad_second, second_low, dgain, dbias) = refs[30:48]
    held, sems = refs[48:60], refs[60:67]
    (near, near_sem, down, down_sem, up, up_sem, rows_all, rows_sem, normed, grad_act, three_low, second, fed, grad_three,
     stage_down, stage_up, stage_sem) = refs[67:]
    here = Place(nz)
    low, wide = jnp.bfloat16, jnp.float32
    width, count = cot.shape[1], frames.shape[0]
    per = held[0].shape[0]
    gather = Gather(here, units, slots, depth, given, held, full, rows_out, sems)
    pace = Pace(gather.steps, every)
    spend = pace.spend
    tiles = [slice(i, i + 256) for i in range(0, width, 256)]
    depth_slots = near.shape[0]
    loads = {}

    def fetch(u):
        gather.arrived(u)
        slot = u % depth_slots
        loads[u] = pltpu.make_async_copy(full[units[u][0]], near.at[slot], near_sem.at[slot])
        loads[u].start()

    def weight(u, n):
        return near[u % depth_slots, :, :, :, :, :, n].reshape(width, -1)

    def apply(a, u, write, cost):
        if u > 0:
            loads[u].wait()
        for n in tiles:
            write(n, jnp.dot(a[...], weight(u, n), preferred_element_type=wide))
            spend(cost)

    def norm(v, i):
        xh, _ = norm_parts(v)
        return xh * gains[8 + i:9 + i] + gains[9 + i:10 + i]

    def put(ref):
        def write(n, r):
            ref[:, n] = r.astype(low)
        return write

    gather.frames()
    rows_load = pltpu.make_async_copy(rows_out, rows_all, rows_sem)
    rows_load.start()
    fetch(0)
    rows_load.wait()
    loads[0].wait()
    lane = lax.broadcasted_iota(jnp.int32, (128, width), 1)
    spread = jnp.where(lax.broadcasted_iota(jnp.int32, (128, width), 0) == lane % per, 1.0, 0.0).astype(low)
    corner = near[0, :, :, :, :, 16:32, 0:128].astype(wide).reshape(-1, 128).astype(low)
    wider = jnp.dot(corner, spread, preferred_element_type=wide)
    row = lax.broadcasted_iota(jnp.int32, wider.shape, 0)
    wider = jnp.where(row // 16 == lax.broadcasted_iota(jnp.int32, wider.shape, 1) // per, wider, 0.0)
    gains[...] = jnp.sum(wider.reshape(-1, 16, width), axis=0)
    spend(1.5)
    for i in range(2):
        for j in range(2):
            part = i * 2 + j
            normed[part * count:(part + 1) * count] = norm(rows_all[i, j].astype(wide), 0).astype(low)
            spend(0.7)
    own_low[...] = norm(frames[...].astype(wide), 0).astype(low)
    spend(0.7)
    apply(text, 0, put(proj), 0.4)
    fetch(1)
    fetch(2)
    apply(normed, 1, put(k_out), 0.8)
    fetch(3)
    apply(normed, 2, put(v_out), 0.8)
    fetch(4)
    apply(own_low, 3, put(q_out), 0.4)
    fetch(5)
    for i in range(0, width, 128):
        n = slice(i, i + 128)
        out = None
        for keep in halves(128):
            p = pair_scores((bounds[0], bounds[1]), q_out[:, n], k_out[:, n], keep, True).astype(low)
            o = jnp.dot(p, v_out[:, n], preferred_element_type=wide)
            out = o if out is None else jnp.where(keep, o, out)
            spend(0.65)
        attended[:, n] = out.astype(low)
    apply(proj, 4, put(cross_keys), 0.4)
    fetch(6)
    apply(proj, 5, put(cross_values), 0.4)
    fetch(7)

    def add_first(n, r):
        first[:, n] = frames[:, n].astype(wide) + r

    apply(attended, 6, add_first, 0.4)
    two_low[...] = norm(first[...], 2).astype(low)
    spend(0.7)
    fetch(8)
    apply(two_low, 7, put(cross_query), 0.4)
    for i in range(0, width, 128):
        n = slice(i, i + 128)
        out = None
        for keep in halves(128):
            p = pair_scores((bounds[2],), cross_query[:, n], cross_keys[:, n], keep, False).astype(low)
            o = jnp.dot(p, cross_values[:, n], preferred_element_type=wide)
            out = o if out is None else jnp.where(keep, o, out)
            spend(0.35)
        cross_mix[:, n] = out.astype(low)

    def add_second(n, r):
        second[:, n] = first[:, n] + r

    apply(cross_mix, 8, add_second, 0.4)
    three_low[...] = norm(second[...], 4).astype(low)
    grad_three[...] = jnp.zeros_like(grad_three)
    fed[...] = jnp.zeros_like(fed)
    spend(0.7)
    n_near = 9
    n_down = len([u for u in units if u[0] == 10])
    n_up = len(units) - n_near - n_down
    for u in range(n_near, n_near + n_down):
        gather.arrived(u)
    load = pltpu.make_async_copy(full[10], down, down_sem)
    load.start()
    ups = []

    def fetch_up(k):
        gather.arrived(n_near + n_down + k)
        slot = k % 2
        ups.append(pltpu.make_async_copy(
            full[9].at[:, :, :, :, :, pl.ds(k * width, width)], up.at[slot], up_sem.at[slot]))
        ups[k].start()

    fetch_up(0)
    load.wait()

    def down_rows(at):
        s = at // down.shape[4]
        return down[s // 8, s // 4 % 2, s // 2 % 2].reshape(-1, width)

    for at in range(0, n_up * width, 256):
        grad_act[:, at:at + 256] = dot_nt(cot[...], down_rows(at))
        spend(0.4)
    def stored(k):
        slot = k % 2
        rows = pl.ds(k * width, width)
        return [
            pltpu.make_async_copy(stage_down.at[slot], dw_down.at[rows], stage_sem.at[0, slot]),
            pltpu.make_async_copy(stage_up.at[slot], dw_up.at[:, rows], stage_sem.at[1, slot]),
        ]

    for k in range(n_up):
        slot = k % 2
        ups[k].wait()
        if k >= 2:
            for cp in stored(k - 2):
                cp.wait()
        for n in tiles:
            at = slice(k * width + n.start, k * width + n.stop)
            w = up[slot, :, :, :, :, :, n].reshape(width, -1)
            hidden = jnp.dot(three_low[...], w, preferred_element_type=wide)
            phi = 0.5 + 0.5 * lax.erf(hidden * (0.5 ** 0.5))
            act = (hidden * phi).astype(low)
            slope = phi + hidden * jnp.exp(-0.5 * hidden * hidden) * 0.3989422804014327
            grad = (grad_act[:, at] * slope).astype(low)
            spend(0.9)
            fed[...] += jnp.dot(act, down_rows(at.start), preferred_element_type=wide)
            grad_three[...] += dot_nt(grad, w)
            spend(0.8)
            stage_down[slot, n, :] = dot_tt(act, cot[...]).astype(low)
            stage_up[slot, :, n] = dot_tt(three_low[...], grad).astype(low)
            spend(1.1)
            if n.start == 256 and k + 1 < n_up:
                fetch_up(k + 1)
        for cp in stored(k):
            cp.start()
    for _ in gather.steps:
        pass
    block_out[...] = (second[...] + fed[...]).astype(low)
    dv, dgain[...], dbias[...] = norm_grads(second[...], gains[12:13], grad_three[...])
    dv = cot[...].astype(wide) + dv
    grad_second[...] = dv
    second_low[...] = dv.astype(low)
    for k in range(max(n_up - 2, 0), n_up):
        for cp in stored(k):
            cp.wait()


def ahead(bounds, frames, text, cot, arrays, units, perms, nz, depth=3, every=1.3):
    slots = make_schedule(perms, nz, lag=depth + 1)
    low, wide = jnp.bfloat16, jnp.float32
    count, width = frames.shape
    tokens, rows = text.shape[0], arrays[0].shape[0]
    hidden = arrays[9].shape[1]
    any_, vmem = pl.BlockSpec(memory_space=pl.ANY), pl.BlockSpec(memory_space=pltpu.VMEM)

    def like(n, kind):
        return jax.ShapeDtypeStruct((n, width), kind)

    given = [*arrays, frames]
    outs = [jax.ShapeDtypeStruct((nz, 2, 2, 2) + a.shape, a.dtype) for a in arrays]
    outs += [jax.ShapeDtypeStruct((2, 2) + frames.shape, low), jax.ShapeDtypeStruct((width, hidden), low), like(hidden, low)]
    far = len(outs)
    outs += [like(16, wide), like(count, low), like(count, low), like(4 * count, low), like(4 * count, low), like(count, low)]
    outs += [like(count, wide), like(count, low), like(count, low), like(tokens, low), like(tokens, low), like(count, low)]
    outs += [like(tokens, low), like(count, low), like(count, wide), like(count, low), like(1, wide), like(1, wide)]
    block = (nz, 2, 2, 2, rows, width)
    dma = pltpu.SemaphoreType.DMA
    return pl.pallas_call(
        functools.partial(ahead_body, nz, units, slots, depth, every),
        out_shape=outs,
        in_specs=[pl.BlockSpec(memory_space=pltpu.SMEM)] + [vmem] * 3 + [any_] * len(given),
        out_specs=[any_] * far + [vmem] * (len(outs) - far),
        scratch_shapes=[pltpu.VMEM(a.shape, a.dtype) for a in given]
        + [dma((4, len(slots)))] * 2 + [dma((len(units), 4))] * 2 + [dma((len(given),)), dma((3,)), dma((3,))]
        + [pltpu.VMEM((5,) + block, low), dma((5,))]
        + [pltpu.VMEM((nz, 2, 2, 2) + arrays[10].shape, low), dma]
        + [pltpu.VMEM((2,) + block, low), dma((2,))]
        + [pltpu.VMEM((2, 2) + frames.shape, low), dma, pltpu.VMEM((4 * count, width), low)]
        + [pltpu.VMEM((count, hidden), wide), pltpu.VMEM((count, width), low)] + [pltpu.VMEM((count, width), wide)] * 3
        + [pltpu.VMEM((2, width, width), low)] * 2 + [dma((2, 2))],
        compiler_params=pltpu.CompilerParams(collective_id=1, has_side_effects=True, vmem_limit_bytes=VMEM_LIMIT),
        name="ahead",
    )(bounds, frames, text, cot, *given)


eps_norm = 1e-05


def layer_norm(values_in, gain_vec, shift_vec):
    centre = values_in - jnp.mean(values_in, axis=-1, keepdims=True)
    spread = jnp.mean(centre * centre, axis=-1, keepdims=True)
    return centre * lax.rsqrt(spread + eps_norm) * gain_vec + shift_vec


def gelu_exact(values_in):
    return jax.nn.gelu(values_in, approximate=False)


def project(left, right):
    return jnp.einsum("gti,ij->gtj", left, right, preferred_element_type=jnp.float32)


def project_back(left, right):
    return jnp.einsum("gtj,ij->gti", left, right, preferred_element_type=jnp.float32)


def outer_sum(left, right):
    return jnp.einsum("gti,gtj->ij", left, right, preferred_element_type=jnp.float32)


class Params(NamedTuple):
    w_query: jax.Array
    w_key: jax.Array
    w_value: jax.Array
    w_out: jax.Array
    c_query: jax.Array
    c_key: jax.Array
    c_value: jax.Array
    c_out: jax.Array
    w_text: jax.Array
    w_up: jax.Array
    w_down: jax.Array
    gain_attn: jax.Array
    bias_attn: jax.Array
    gain_cross: jax.Array
    bias_cross: jax.Array
    gain_feed: jax.Array
    bias_feed: jax.Array


BLOCKS, GAINS = 11, 6


def all_axes():
    return ("dp", "seq")


def fits(own, frames, text):
    rows, width = own.w_query.shape
    return (
        lax.axis_size("seq") == 4 and lax.axis_size("dp") % 2 == 0 and rows == 32 and width % 128 == 0
        and own.w_text.shape[0] % 8 == 0 and own.w_text.shape[0] + 8 == rows
        and own.w_up.shape[0] == rows and own.w_up.shape[1] % width == 0
        and own.w_down.shape == (own.w_up.shape[1] // width * rows, width) and own.w_down.shape[0] == 128
        and width == rows * lax.axis_size("dp") * 4
        and frames.shape[0] == 1 and frames.shape[1] % 32 == 0 and text.shape[0] == 1 and text.shape[1] % 128 == 0
    )


class PlainWires:
    def gather(self, own, frames):
        full = Params(*[lax.all_gather(v, all_axes(), axis=0, tiled=True) for v in own])
        return full, lax.all_gather(frames, "seq", axis=1, tiled=True)

    def scatter(self, grads):
        return Params(*[lax.psum_scatter(v, all_axes(), scatter_dimension=0, tiled=True) for v in grads])

    def share(self, arrays, number):
        return [lax.psum_scatter(a, "seq", scatter_dimension=1, tiled=True) for a in arrays]


def attention(causal, bounds, q, k, v):
    return attend(causal, bounds[0], q[0], k[0], v[0])[None]


def attention_back(causal, bounds, *operands):
    return [r[None] for r in attend_grads(causal, bounds[0], *[a[0] for a in operands])]


def plain_layer(own, frames, cotangent, text_states, frame_start, prompt_len):
    low = jnp.bfloat16
    wires = PlainWires()
    full, all_frames = wires.gather(own, frames)
    wide = [v.astype(jnp.float32) for v in full[BLOCKS:]]
    frames_f = frames.astype(jnp.float32)
    frame_count = frames.shape[1]
    normed, norm_one_back = jax.vjp(layer_norm, frames_f, wide[0], wide[1])
    normed_low = normed.astype(low)
    normed_all = layer_norm(all_frames.astype(jnp.float32), wide[0], wide[1]).astype(low)
    query_rows = project(normed_low, full.w_query).astype(low)
    key_all = project(normed_all, full.w_key).astype(low)
    value_all = project(normed_all, full.w_value).astype(low)
    rank = lax.axis_index("seq")
    self_bounds = jnp.stack([jnp.full_like(frame_start, rank * frame_count), frame_start], axis=1)
    attended = attention(True, self_bounds, query_rows, key_all, value_all)
    first = frames_f + project(attended, full.w_out)
    text_count = text_states.shape[1]
    quarter = text_count // lax.axis_size("seq")
    text_start = rank * quarter
    text_part = lax.dynamic_slice_in_dim(text_states, text_start, quarter, 1)
    proj_all = project(text_states, full.w_text).astype(low)
    cross_keys = project(proj_all, full.c_key).astype(low)
    cross_values = project(proj_all, full.c_value).astype(low)
    proj_part = lax.dynamic_slice_in_dim(proj_all, text_start, quarter, 1)
    normed_two, norm_two_back = jax.vjp(layer_norm, first, wide[2], wide[3])
    normed_two_low = normed_two.astype(low)
    cross_query = project(normed_two_low, full.c_query).astype(low)
    cross_bounds = jnp.stack([prompt_len, prompt_len], axis=1)
    cross_mix = attention(False, cross_bounds, cross_query, cross_keys, cross_values)
    second = first + project(cross_mix, full.c_out)
    normed_three, norm_three_back = jax.vjp(layer_norm, second, wide[4], wide[5])
    three_low = normed_three.astype(low)
    hidden = project(three_low, full.w_up)
    activated, gelu_back = jax.vjp(gelu_exact, hidden)
    act_low = activated.astype(low)
    block_out = (second + project(act_low, full.w_down)).astype(low)
    grad_act = project_back(cotangent, full.w_down)
    dw_down = outer_sum(act_low, cotangent)
    grad_hidden = gelu_back(grad_act)[0].astype(low)
    dw_up = outer_sum(three_low, grad_hidden)
    grad_second_ln, dgain_feed, dbias_feed = norm_three_back(project_back(grad_hidden, full.w_up))
    grad_second = cotangent.astype(jnp.float32) + grad_second_ln
    second_low = grad_second.astype(low)
    dc_out = outer_sum(cross_mix, second_low)
    grad_cross_mix = project_back(second_low, full.c_out).astype(low)
    cq_low, grad_ck, grad_cv = attention_back(
        False, cross_bounds, cross_query, cross_keys, cross_values, grad_cross_mix
    )
    ck_low, cv_low = wires.share([grad_ck, grad_cv], 3)
    dc_key = outer_sum(proj_part, ck_low)
    dc_value = outer_sum(proj_part, cv_low)
    grad_proj = (project_back(ck_low, full.c_key) + project_back(cv_low, full.c_value)).astype(low)
    dw_text = outer_sum(text_part, grad_proj)
    text_grad = project_back(grad_proj, full.w_text)
    dc_query = outer_sum(normed_two_low, cq_low)
    grad_first_ln, dgain_cross, dbias_cross = norm_two_back(project_back(cq_low, full.c_query))
    grad_first = grad_second + grad_first_ln
    first_low = grad_first.astype(low)
    dw_out = outer_sum(attended, first_low)
    grad_attended = project_back(first_low, full.w_out).astype(low)
    q_low, grad_k_all, grad_v_all = attention_back(
        True, self_bounds, query_rows, key_all, value_all, grad_attended
    )
    k_low, v_low = wires.share([grad_k_all, grad_v_all], 4)
    dw_query = outer_sum(normed_low, q_low)
    dw_key = outer_sum(normed_low, k_low)
    dw_value = outer_sum(normed_low, v_low)
    grad_normed = (
        project_back(q_low, full.w_query) + project_back(k_low, full.w_key) + project_back(v_low, full.w_value)
    )
    grad_frames_ln, dgain_attn, dbias_attn = norm_one_back(grad_normed)
    frames_grad = (grad_first + grad_frames_ln).astype(low)
    sums = wires.scatter(
        Params(
            dw_query, dw_key, dw_value, dw_out, dc_query, dc_key, dc_value, dc_out, dw_text, dw_up, dw_down,
            dgain_attn, dbias_attn, dgain_cross, dbias_cross, dgain_feed, dbias_feed,
        )
    )
    return (block_out, frames_grad, text_grad, *sums)


NEAR_ORDERS = ("zyx", "zxy", "zyx", "zxy", "zyx", "zxy", "zyx", "zxy", "zyx")
LATE_ORDERS = ("zxy", "yxz", "zyx", "xyz", "zxy", "zyx", "yxz", "xyz")
SHORT_ORDERS = ("zyx", "zxy", "zyx", "zxy", "zyx", "zxy", "yxz", "zyx", "xyz")
FEED_ORDERS = ("zyx", "zxy", "zyx", "yxz", "zxy", "zyx", "xyz", "zxy")


def cycle(orders, n):
    return [orders[i % len(orders)] for i in range(n)]


def fast_layer(own, frames, cotangent, text_states, frame_start, prompt_len):
    low, wide = jnp.bfloat16, jnp.float32
    nz = lax.axis_size("dp") // 2
    shards = nz * 8
    rows, width = own.w_query.shape
    text_rows = own.w_text.shape[0]
    count = frames.shape[1]
    rank = lax.axis_index("seq")
    up, down = own.w_up.shape[1] // width, own.w_down.shape[0] // rows
    near_units = [(g, 0, rows, 0, width) for g in range(9)]
    up_units = [(9, 0, rows, k * width, width) for k in range(up)]
    down_units = [(10, k * rows, rows, 0, width) for k in range(down)]
    units = [near_units[i] for i in (8, 1, 2, 0, 5, 6, 3, 4, 7)] + down_units + up_units
    gains = jnp.stack(own[BLOCKS:])
    gains = jnp.pad(gains, ((0, rows - text_rows - GAINS), (0, width - gains.shape[1])))
    arrays = list(own[:BLOCKS])
    arrays[8] = jnp.concatenate([own.w_text, gains], axis=0)
    tokens = text_states.shape[1]
    text = jnp.pad(text_states.reshape((tokens, shards, text_rows)), ((0, 0), (0, 0), (0, rows - text_rows))).reshape((tokens, width))
    bounds = jnp.concatenate([jnp.full_like(frame_start, rank * count), frame_start, prompt_len])
    cot = cotangent[0]
    orders = cycle(NEAR_ORDERS, 9) + cycle(LATE_ORDERS, up + down)
    outs = ahead(bounds, frames[0], text, cot, arrays, units, orders, nz)
    full, (_, dw_up, dw_down) = [f.reshape((-1, f.shape[-1])) for f in outs[:BLOCKS]], outs[BLOCKS:BLOCKS + 3]
    (gains, normed_low, query_rows, key_all, value_all, attended, first, two_low, cross_query, cross_keys, cross_values,
     cross_mix, proj, block_out, grad_second, second_low, dgain_feed, dbias_feed) = outs[BLOCKS + 3:]
    quarter = tokens // 4
    text_part = lax.dynamic_slice_in_dim(text, rank * quarter, quarter, 0)
    proj_part = lax.dynamic_slice_in_dim(proj, rank * quarter, quarter, 0)
    near = [second_low, grad_second, cross_mix, cross_query, cross_keys, cross_values, two_low, first, text_part, proj_part, attended, gains[10:11]]
    weights = [full[i] for i in (7, 4, 5, 6, 8, 3)]
    lead = (nz, 2, 2, 2)
    feed = [v.reshape(lead + (-1, v.shape[-1])) for v in (dw_up, dw_down)]
    feed_units = [((g - 9, *rest),) for g, *rest in up_units + down_units]
    (dc_out, dc_query, dw_out, dc_key, dc_value, dw_text, text_grad, grad_first, grad_attended, dgain_cross, dbias_cross,
     feed_sums) = middle_back(bounds[2:], near, weights, feed, feed_units, cycle(FEED_ORDERS, up + down), nz)
    q_low, grad_k, grad_v = attend_grads(True, bounds[:2], query_rows, key_all, value_all, grad_attended)
    k_low, v_low = share_sums([v.reshape((2, 2, -1, width)) for v in (grad_k, grad_v)], 4)
    dw_query, dw_key, dw_value = [outer_sum(normed_low[None], v[None]).astype(low) for v in (q_low, k_low, v_low)]
    grad_normed = sum(project_back(v[None], full[i]) for i, v in enumerate((q_low, k_low, v_low)))
    frames_f = frames.astype(wide)
    back = jax.vjp(layer_norm, frames_f, gains[8], gains[9])[1]
    grad_ln, dgain_attn, dbias_attn = back(grad_normed)
    frames_grad = (grad_first[None] + grad_ln).astype(low)
    rest = [dgain_attn, dbias_attn, dgain_cross[0], dbias_cross[0], dgain_feed[0], dbias_feed[0]]
    rest = jnp.stack([v.astype(low).reshape((shards, -1)) for v in rest], axis=1)
    rest = jnp.pad(rest, ((0, 0), (0, rows - text_rows - GAINS), (0, width - rest.shape[2])))
    mixed = jnp.concatenate([dw_text.reshape((shards, rows, width))[:, :text_rows], rest], axis=1)
    grads = [dw_query, dw_key, dw_value, dw_out, dc_query, dc_key, dc_value, dc_out, mixed]
    grads = [v.reshape(lead + (rows, width)) for v in grads]
    near_units = [(u,) for u in near_units]
    sums = scatter_grads(grads, near_units, cycle(SHORT_ORDERS, 9), nz)
    shapes = [(rows, width)] * 9 + [own.w_up.shape, own.w_down.shape]
    feed_units = [((g + 9, *rest),) for ((g, *rest),) in feed_units]
    *blocks, tail = deliver((sums, feed_sums), (near_units, feed_units), text_rows, shapes)
    text_grad = text_grad.reshape((quarter, shards, rows))[:, :, :text_rows].reshape((1, quarter, -1))
    return (block_out[None], frames_grad, text_grad, *blocks, *[tail[i, : width // shards] for i in range(GAINS)])


def on_device(frames, cotangent, text_states, frame_start, prompt_len, *params):
    own = Params(*params)
    layer = fast_layer if fits(own, frames, text_states) else plain_layer
    return layer(own, frames, cotangent, text_states, frame_start, prompt_len)


def solution(mesh):
    both = P(all_axes(), None)
    rows, vector = P(*all_axes(), None), P(all_axes())
    item, whole = P("dp"), P("dp", None, None)
    return jax.shard_map(
        on_device,
        mesh=mesh,
        in_specs=(rows, rows, whole, item, item) + (both,) * BLOCKS + (vector,) * GAINS,
        out_specs=(rows,) * 3 + (both,) * BLOCKS + (vector,) * GAINS,
        check_vma=False,
    )
```

```python
import functools
from typing import NamedTuple
import jax
import jax.numpy as jnp
from jax import lax
from jax.experimental import pallas as pl
from jax.experimental.pallas import tpu as pltpu
from jax.sharding import PartitionSpec as P

MESH = pl.DeviceIdType.MESH

LAG = 2
VMEM_LIMIT = 60 * 1024 * 1024

def unit_ops(perm, nz):
    rank = {a: i for i, a in enumerate(perm)}
    ops = {}

    def source(j, fy, fx):
        differs = [a for a, f in (("z", j > 0), ("y", fy), ("x", fx)) if f]
        if not differs:
            return None
        last = max(differs, key=lambda a: rank[a])
        if last == "z":
            return ("z", j - 1, fy, fx)
        if last == "y":
            return ("y", j, 0, fx)
        return ("x", j, fy, 0)

    for j in range(nz):
        for fy in range(2):
            for fx in range(2):
                for axis in "zyx":
                    flags = {"z": j > 0, "y": fy, "x": fx}
                    if axis != "z" and flags[axis]:
                        continue
                    if any(flags[a] and rank[a] > rank[axis] for a in "zyx" if a != axis):
                        continue
                    if axis == "z" and j == nz - 1:
                        continue
                    ops[(axis, j, fy, fx)] = source(j, fy, fx)
    return ops

def make_schedule(perms, nz, lag=LAG, window=None):
    ops = {}
    for u, perm in enumerate(perms):
        for key, dep in unit_ops(perm, nz).items():
            ops[(u,) + key] = None if dep is None else (u,) + dep
    children = {}
    for op, dep in ops.items():
        children.setdefault(dep, []).append(op)
    height = {}

    def tall(op):
        if op not in height:
            height[op] = 1 + max([tall(c) for c in children.get(op, [])], default=0)
        return height[op]

    for op in ops:
        tall(op)
    done, slots, left = {}, [], set(ops)
    while left:
        t = len(slots)
        slot = {}
        for axis in "zyx":
            ready = [op for op in left if op[1] == axis and (ops[op] is None or (ops[op] in done and done[ops[op]] + lag <= t))]
            if ready:
                slot[axis] = min(ready, key=lambda op: (op[0] // window if window else 0, -height[op], op[0], op))
        for axis, op in slot.items():
            done[op] = t
            left.discard(op)
        slots.append(slot)
    return slots

def nth_table(nz):
    rows = []
    for z in range(nz):
        offs = sorted((p - z for p in range(nz)), key=lambda o: (abs(o), o if z % 2 else -o))
        rows.append([z + o for o in offs])
    return rows

def pick(values, z):
    out = 0
    for i, v in enumerate(values):
        out = out + v * jnp.where(z == i, 1, 0)
    return out

UP, DOWN, YY, XX, CORE = range(5)
WAYS_OF = dict(z=(UP, DOWN), y=(YY,), x=(XX,))

class Place:
    def __init__(self, nz):
        d, s = lax.axis_index("dp"), lax.axis_index("seq")
        self.nz = nz
        self.z, self.y, self.x, self.c = d // 2, d % 2, s // 2, s % 2
        z, y, x, c = self.z, self.y, self.x, self.c
        self.device = [
            ((z + 1) * 2 + y, x * 2 + c),
            ((z - 1) * 2 + y, x * 2 + c),
            (z * 2 + 1 - y, x * 2 + c),
            (z * 2 + y, (1 - x) * 2 + c),
            (z * 2 + y, x * 2 + 1 - c),
        ]
        self.nth = [[row[j] for row in nth_table(nz)] for j in range(nz)]

    def greet(self):
        barrier = pltpu.get_barrier_semaphore()
        has_up, has_down = self.z + 1 < self.nz, self.z > 0
        for way in range(5):
            def hello(way=way):
                pl.semaphore_signal(barrier, inc=1, device_id=self.device[way], device_id_type=MESH)
            if way < YY:
                pl.when(has_up if way == UP else has_down)(hello)
            else:
                hello()
        edge = jnp.where(self.z == 0, 1, 0) + jnp.where(self.z == self.nz - 1, 1, 0)
        pl.semaphore_wait(barrier, 5 - edge)

    def gather_moves(self, axis, j, fy, fx):
        z, y, x, nz = self.z, self.y, self.x, self.nz
        py, px = (1 - y if fy else y), (1 - x if fx else x)
        if axis == "z":
            out = [(UP, (z - j >= 0) & (z + 1 < nz), (z - j, py, px)), (DOWN, (z + j < nz) & (z > 0), (z + j, py, px))]
            come = [(UP, z - 1 - j >= 0, (z - 1 - j, py, px)), (DOWN, z + 1 + j < nz, (z + 1 + j, py, px))]
        else:
            pz = pick(self.nth[j], z)
            there = (pz, 1 - y, px) if axis == "y" else (pz, py, 1 - x)
            way = YY if axis == "y" else XX
            out = [(way, None, (pz, py, px))]
            come = [(way, None, there)]
        return out, come

def when(cond, fn):
    if cond is None:
        fn()
    else:
        pl.when(cond)(fn)

BACK = (DOWN, UP, YY, XX)


def scatter_steps(here, units, slots, depth, ins, total, twin, landed, send_sem, recv_sem, core_send, core_recv, local_sem, late=()):
    nz = here.nz
    z, y, x, c = here.z, here.y, here.x, here.c
    steps = slots[::-1]
    numbers, order = {}, []
    for t, slot in enumerate(steps):
        for axis, op in slot.items():
            for way in WAYS_OF[axis]:
                numbers[way, t] = len(numbers)
            if op[0] not in order:
                order.append(op[0])

    def plane(u, b, which):
        g, r0, rn, c0, cn = units[u][b]
        return ins[g].at[:, :, :, which, pl.ds(r0, rn), pl.ds(c0, cn)]

    def rows_of(buffer, u, b):
        rn = units[u][b][2]
        return buffer.at[u, :, :, :, pl.ds(b * rn, rn)]

    def local(u, b):
        return pltpu.make_async_copy(plane(u, b, c), rows_of(total, u, b), local_sem.at[u, b])

    def across(u, b):
        return pltpu.make_async_remote_copy(
            src_ref=plane(u, b, 1 - c), dst_ref=rows_of(twin, u, b), send_sem=core_send.at[u, b],
            recv_sem=core_recv.at[u, b], device_id=here.device[CORE], device_id_type=MESH,
        )

    def remote(u, way, t, p):
        i = numbers[way, t]
        return pltpu.make_async_remote_copy(
            src_ref=total.at[u, p[0], p[1], p[2]], dst_ref=landed.at[i], send_sem=send_sem.at[i], recv_sem=recv_sem.at[i],
            device_id=here.device[BACK[way]], device_id_type=MESH,
        )

    ahead = 3
    blocks = range(len(units[0]))
    early = [u for u in order if u not in late]

    def begin_unit(u):
        for b in blocks:
            local(u, b).start()
            across(u, b).start()

    for u in early[:ahead]:
        for b in blocks:
            local(u, b).start()
    here.greet()
    for u in early[:ahead]:
        for b in blocks:
            across(u, b).start()
    if late:
        yield begin_unit

    def join(u):
        later = early.index(u) + ahead if u in early else len(early)
        if later < len(early):
            begin_unit(early[later])
        for b in blocks:
            local(u, b).wait()
            across(u, b).wait_recv()

        @pl.loop(0, nz)
        def _(a):
            for b in range(2):
                for e in range(2):
                    total[u, a, b, e] = (
                        total[u, a, b, e].astype(jnp.float32) + twin[u, a, b, e].astype(jnp.float32)
                    ).astype(jnp.bfloat16)

    joined = set()
    for t in range(len(steps) + depth):
        if t < len(steps):
            for axis, (u, _, j, fy, fx) in steps[t].items():
                if u not in joined:
                    joined.add(u)
                    join(u)
                for way, cond, p in here.gather_moves(axis, j, fy, fx)[1]:
                    when(cond, lambda u=u, way=way, p=p: remote(u, way, t, p).start())
        if t >= depth:
            s = t - depth
            for axis, (u, _, j, fy, fx) in steps[s].items():
                for way, cond, p in here.gather_moves(axis, j, fy, fx)[0]:
                    def add(u=u, way=way, p=p):
                        i = numbers[way, s]
                        pltpu.make_async_copy(landed.at[i], landed.at[i], recv_sem.at[i]).wait()
                        total[u, p[0], p[1], p[2]] = (
                            total[u, p[0], p[1], p[2]].astype(jnp.float32) + landed[i].astype(jnp.float32)
                        ).astype(jnp.bfloat16)
                    when(cond, add)
        yield t
    for t, slot in enumerate(steps):
        for axis, (u, _, j, fy, fx) in slot.items():
            for way, cond, p in here.gather_moves(axis, j, fy, fx)[1]:
                when(cond, lambda u=u, way=way, p=p: remote(u, way, t, p).wait_send())
    for u in order:
        for b in blocks:
            across(u, b).wait_send()


def unit_shape(units):
    return sum(block[2] for block in units[0]), units[0][0][4]


def scatter_scratch(units, slots, nz):
    rows, columns = unit_shape(units)
    count = sum(len(WAYS_OF[axis]) for slot in slots for axis in slot)
    plane = (len(units), nz, 2, 2, rows, columns)
    return [
        pltpu.VMEM(plane, jnp.bfloat16),
        pltpu.VMEM(plane, jnp.bfloat16),
        pltpu.VMEM((count, rows, columns), jnp.bfloat16),
        pltpu.SemaphoreType.DMA((count,)),
        pltpu.SemaphoreType.DMA((count,)),
        pltpu.SemaphoreType.DMA((len(units), len(units[0]))),
        pltpu.SemaphoreType.DMA((len(units), len(units[0]))),
        pltpu.SemaphoreType.DMA((len(units), len(units[0]))),
    ]


def deliver_body(parts, text_rows, n, *refs):
    ins, outs = refs[:n], refs[n:]
    for sums, units in zip(ins, parts):
        for u, unit in enumerate(units):
            for b, (g, r0, rn, c0, cn) in enumerate(unit):
                if g == 8:
                    outs[g][...] = sums[u, :text_rows]
                    outs[-1][...] = sums[u, text_rows:text_rows + 8]
                else:
                    outs[g][r0:r0 + rn, c0:c0 + cn] = sums[u, b * rn:(b + 1) * rn]


def deliver(sums, parts, text_rows, shapes):
    shapes = [(text_rows,) + s[1:] if g == 8 else s for g, s in enumerate(shapes)] + [(8, sums[0].shape[2])]
    return pl.pallas_call(
        functools.partial(deliver_body, parts, text_rows, len(sums)),
        out_shape=[jax.ShapeDtypeStruct(s, jnp.float32) for s in shapes],
        compiler_params=pltpu.CompilerParams(vmem_limit_bytes=16 * 1024 * 1024),
        name="deliver",
    )(*sums)


def pair_scores(bounds_ref, q, k, keep, causal):
    s = lax.dot_general(jnp.where(keep, q, 0), k, (((1,), (1,)), ((), ())), preferred_element_type=jnp.float32)
    col = lax.broadcasted_iota(jnp.int32, s.shape, 1)
    if causal:
        row = lax.broadcasted_iota(jnp.int32, s.shape, 0) + bounds_ref[0]
        seen = (col <= row) & ((col >= bounds_ref[1]) | (col == row))
    else:
        seen = col < bounds_ref[0]
    s = jnp.where(seen, s * 0.125, -1e30)
    e = jnp.exp(s - jnp.max(s, axis=1, keepdims=True))
    return e * (1.0 / jnp.sum(e, axis=1, keepdims=True))


def halves(width):
    lane = lax.broadcasted_iota(jnp.int32, (1, width), 1)
    return [(lane >= 64 * h) & (lane < 64 * h + 64) for h in range(width // 64)]


def attend_body(causal, bounds_ref, q_ref, k_ref, v_ref, out_ref):
    q, k, v = q_ref[...], k_ref[...], v_ref[...]
    out = None
    for keep in halves(q.shape[1]):
        p = pair_scores(bounds_ref, q, k, keep, causal)
        o = jnp.dot(p.astype(jnp.bfloat16), v, preferred_element_type=jnp.float32)
        out = o if out is None else jnp.where(keep, o, out)
    out_ref[...] = out.astype(jnp.bfloat16)


def attend_back_body(causal, bounds_ref, q_ref, k_ref, v_ref, g_ref, dq_ref, dk_ref, dv_ref):
    q, k, v, g = q_ref[...], k_ref[...], v_ref[...], g_ref[...]
    dq = dk = dv = None
    for keep in halves(q.shape[1]):
        p = pair_scores(bounds_ref, q, k, keep, causal)
        dp = lax.dot_general(jnp.where(keep, g, 0), v, (((1,), (1,)), ((), ())), preferred_element_type=jnp.float32)
        ds = (p * (dp - jnp.sum(p * dp, axis=1, keepdims=True))).astype(jnp.bfloat16)
        a = jnp.dot(ds, k, preferred_element_type=jnp.float32)
        b = lax.dot_general(ds, q, (((0,), (0,)), ((), ())), preferred_element_type=jnp.float32)
        e = lax.dot_general(p.astype(jnp.bfloat16), g, (((0,), (0,)), ((), ())), preferred_element_type=jnp.float32)
        if dq is None:
            dq, dk, dv = a, b, e
        else:
            dq, dk, dv = jnp.where(keep, a, dq), jnp.where(keep, b, dk), jnp.where(keep, e, dv)
    dq_ref[...] = (dq * 0.125).astype(jnp.bfloat16)
    dk_ref[...] = (dk * 0.125).astype(jnp.bfloat16)
    dv_ref[...] = dv.astype(jnp.bfloat16)


def attend_call(body, causal, bounds, operands, n_out_rows):
    width = operands[0].shape[1]
    spec = [pl.BlockSpec((a.shape[0], 128), lambda i: (0, i)) for a in operands]
    return pl.pallas_call(
        functools.partial(body, causal),
        grid=(width // 128,),
        out_shape=[jax.ShapeDtypeStruct((r, width), jnp.bfloat16) for r in n_out_rows],
        in_specs=[pl.BlockSpec(memory_space=pltpu.SMEM)] + spec,
        out_specs=[pl.BlockSpec((r, 128), lambda i: (0, i)) for r in n_out_rows],
        compiler_params=pltpu.CompilerParams(vmem_limit_bytes=32 * 1024 * 1024),
        name=("self_" if causal else "cross_") + body.__name__,
    )(bounds, *operands)


def attend(causal, bounds, q, k, v):
    return attend_call(attend_body, causal, bounds, (q, k, v), [q.shape[0]])[0]


def attend_grads(causal, bounds, q, k, v, g):
    return attend_call(attend_back_body, causal, bounds, (q, k, v, g), [q.shape[0], k.shape[0], k.shape[0]])


def dot_tt(a, b):
    return lax.dot_general(a, b, (((0,), (0,)), ((), ())), preferred_element_type=jnp.float32)


def dot_nt(a, b):
    return lax.dot_general(a, b, (((1,), (1,)), ((), ())), preferred_element_type=jnp.float32)


def norm_parts(v):
    centre = v - jnp.mean(v, axis=1, keepdims=True)
    rate = lax.rsqrt(jnp.mean(centre * centre, axis=1, keepdims=True) + eps_norm)
    return centre * rate, rate


def norm_grads(v, gain, h):
    xh, rate = norm_parts(v)
    hg = h * gain
    dv = (hg - jnp.mean(hg, axis=1, keepdims=True) - xh * jnp.mean(hg * xh, axis=1, keepdims=True)) * rate
    return dv, jnp.sum(h * xh, axis=0, keepdims=True), jnp.sum(h, axis=0, keepdims=True)


class Share:
    def __init__(self, here, mine, twins, sums, landed, core_send, core_recv, x_send, x_recv, chunk):
        self.here, self.mine, self.twins, self.sums, self.landed = here, mine, twins, sums, landed
        self.sems, self.chunk = (core_send, core_recv, x_send, x_recv), chunk

    def columns(self, k):
        return pl.ds(k * self.chunk, self.chunk)

    def across(self, g, k, far):
        here, f = self.here, 1 if far else 0
        part = (1 - here.x if far else here.x) * 2 + 1 - here.c
        return pltpu.make_async_remote_copy(
            src_ref=self.mine[g].at[part, :, self.columns(k)], dst_ref=self.twins[g].at[f, :, self.columns(k)],
            send_sem=self.sems[0].at[f, g, k], recv_sem=self.sems[1].at[f, g, k],
            device_id=here.device[CORE], device_id_type=MESH,
        )

    def beyond(self, g, k):
        return pltpu.make_async_remote_copy(
            src_ref=self.sums[g].at[:, self.columns(k)], dst_ref=self.landed[g].at[:, self.columns(k)],
            send_sem=self.sems[2].at[g, k], recv_sem=self.sems[3].at[g, k],
            device_id=self.here.device[XX], device_id_type=MESH,
        )

    def send(self, k):
        for far in (True, False):
            for g in range(len(self.mine)):
                self.across(g, k, far).start()

    def forward(self, k):
        here, cols = self.here, slice(k * self.chunk, (k + 1) * self.chunk)
        for g, mine in enumerate(self.mine):
            self.across(g, k, True).wait_recv()
            part = (1 - here.x) * 2 + here.c
            self.sums[g][:, cols] = (
                mine[part, :, cols].astype(jnp.float32) + self.twins[g][1, :, cols].astype(jnp.float32)
            ).astype(jnp.bfloat16)
            self.beyond(g, k).start()

    def collect(self, g, k):
        here, cols = self.here, slice(k * self.chunk, (k + 1) * self.chunk)
        self.across(g, k, False).wait_recv()
        self.beyond(g, k).wait_recv()
        return (
            self.mine[g][here.x * 2 + here.c, :, cols].astype(jnp.float32) + self.twins[g][0, :, cols].astype(jnp.float32)
            + self.landed[g][:, cols].astype(jnp.float32)
        ).astype(jnp.bfloat16)

    def finish(self, chunks):
        for g in range(len(self.mine)):
            for k in range(chunks):
                self.across(g, k, True).wait_send()
                self.across(g, k, False).wait_send()
                self.beyond(g, k).wait_send()


class Pace:
    def __init__(self, steps, every):
        self.steps, self.every, self.owed = steps, every, 0.0

    def spend(self, time):
        self.owed += time
        while self.owed >= self.every:
            self.owed -= self.every
            next(self.steps, None)


def pair_grads(bounds_ref, causal, q, k, v, g, between):
    dq = dk = dv = None
    for keep in halves(q.shape[1]):
        p = pair_scores(bounds_ref, q, k, keep, causal)
        dp = dot_nt(jnp.where(keep, g, 0), v)
        ds = (p * (dp - jnp.sum(p * dp, axis=1, keepdims=True))).astype(jnp.bfloat16)
        a = jnp.dot(ds, k, preferred_element_type=jnp.float32)
        b = dot_tt(ds, q)
        e = dot_tt(p.astype(jnp.bfloat16), g)
        if dq is None:
            dq, dk, dv = a, b, e
        else:
            dq, dk, dv = jnp.where(keep, a, dq), jnp.where(keep, b, dk), jnp.where(keep, e, dv)
        between()
    return [(r * s).astype(jnp.bfloat16) for r, s in ((dq, 0.125), (dk, 0.125), (dv, 1.0))]


def middle_body(nz, units, slots, depth, *refs):
    (bounds, second_low, grad_second, cross_mix, cross_query, cross_keys, cross_values, two_low, first, text_part,
     proj_part, attended, gain) = refs[:13]
    weights, feed = refs[13:19], refs[19:21]
    placed = refs[21:27]
    text_grad, grad_first, grad_attended, dgain, dbias, sums = refs[27:33]
    held, (weight_sem, mixed, first_low, grad_ck, grad_cv, twin_k, twin_v, sum_k, sum_v, land_k, land_v) = refs[33:39], refs[39:50]
    share_sems, stage, stage_sem, scatter = refs[50:54], refs[54], refs[55], refs[56:]
    here = Place(nz)
    loads = [pltpu.make_async_copy(w, h, weight_sem.at[i]) for i, (w, h) in enumerate(zip(weights, held))]
    for cp in loads:
        cp.start()
    c_out, c_query, c_key, c_value, w_text, w_out = held
    steps = scatter_steps(here, units, slots, depth, feed, *scatter)
    low = jnp.bfloat16
    width = second_low.shape[1]
    rows = text_part.shape[0]
    tiles = [slice(i, i + 256) for i in range(0, width, 256)]
    share = Share(here, (grad_ck, grad_cv), (twin_k, twin_v), (sum_k, sum_v), (land_k, land_v), *share_sems, width // 2)

    pace = Pace(steps, 32.0 / (len(slots) + depth))
    spend = pace.spend

    def stored(i):
        src = stage.at[i % 3, pl.ds(0, placed[i].shape[0])]
        return pltpu.make_async_copy(src, placed[i], stage_sem.at[i])

    next(steps)
    loads[0].wait()
    for n in tiles:
        mixed[:, n] = dot_nt(second_low[...], c_out[n, :]).astype(low)
        spend(0.4)
    for n in tiles:
        stage[0, n, :] = dot_tt(cross_mix[:, n], second_low[...]).astype(low)
        spend(0.55)
    stored(0).start()
    pairs = width // 128
    for i in range(pairs):
        n = slice(i * 128, i * 128 + 128)
        dq, dk, dv = pair_grads(bounds, False, cross_query[:, n], cross_keys[:, n], cross_values[:, n], mixed[:, n], lambda: spend(0.72))
        mixed[:, n] = dq
        grad_ck[:, :, n] = dk.reshape(4, rows, 128)
        grad_cv[:, :, n] = dv.reshape(4, rows, 128)
        if i == pairs // 2 - 1:
            share.send(0)
    share.send(1)
    share.forward(0)
    loads[1].wait()
    for n in tiles:
        grad_first[:, n] = dot_nt(mixed[...], c_query[n, :])
        spend(0.4)
    share.forward(1)
    dv, dg, db = norm_grads(first[...], gain[...], grad_first[...])
    dgain[...] = dg
    dbias[...] = db
    dv = grad_second[...] + dv
    grad_first[...] = dv
    first_low[...] = dv.astype(low)
    spend(2.0)
    loads[5].wait()
    for n in tiles:
        grad_attended[:, n] = dot_nt(first_low[...], w_out[n, :]).astype(low)
        spend(0.4)
    for n in tiles:
        stage[1, n, :] = dot_tt(two_low[:, n], mixed[...]).astype(low)
        spend(0.55)
    stored(1).start()
    for n in tiles:
        stage[2, n, :] = dot_tt(attended[:, n], first_low[...]).astype(low)
        spend(0.55)
    stored(2).start()
    ck = jnp.concatenate([share.collect(0, k) for k in range(2)], axis=1)
    cv = jnp.concatenate([share.collect(1, k) for k in range(2)], axis=1)
    for i in (2, 3, 4):
        loads[i].wait()
    stored(0).wait()
    stored(1).wait()
    for n in tiles:
        stage[0, n, :] = dot_tt(proj_part[:, n], ck).astype(low)
        stage[1, n, :] = dot_tt(proj_part[:, n], cv).astype(low)
        spend(0.7)
    stored(3).start()
    stored(4).start()
    proj = []
    for n in tiles:
        proj.append((dot_nt(ck, c_key[n, :]) + dot_nt(cv, c_value[n, :])).astype(low))
        spend(0.5)
    proj = jnp.concatenate(proj, axis=1)
    stored(2).wait()
    for i in range(0, text_part.shape[1], 256):
        n = slice(i, i + 256)
        stage[2, n, :] = dot_tt(text_part[:, n], proj).astype(low)
        text_grad[:, n] = dot_nt(proj, w_text[n, :])
        spend(0.7)
    stored(5).start()
    for _ in steps:
        pass
    share.finish(2)
    for i in (3, 4, 5):
        stored(i).wait()
    total = scatter[0]
    for u in range(len(units)):
        sums[u] = total[u, here.z, here.y, here.x].astype(jnp.float32)


def middle_back(bounds, near, weights, feed, units, perms, nz, depth=3):
    slots = make_schedule(perms, nz, lag=depth + 1)
    second_low, text_part = near[0], near[8]
    width, rows, text_width = second_low.shape[1], text_part.shape[0], text_part.shape[1]
    low, wide = jnp.bfloat16, jnp.float32
    square = jax.ShapeDtypeStruct((width, width), low)
    outs = [square] * 5 + [jax.ShapeDtypeStruct((text_width, width), low)]
    outs += [jax.ShapeDtypeStruct(text_part.shape, wide), jax.ShapeDtypeStruct(second_low.shape, wide)]
    outs += [jax.ShapeDtypeStruct(second_low.shape, low)] + [jax.ShapeDtypeStruct((1, width), wide)] * 2
    outs += [jax.ShapeDtypeStruct((len(units),) + unit_shape(units), wide)]
    vmem, any_ = pl.BlockSpec(memory_space=pltpu.VMEM), pl.BlockSpec(memory_space=pl.ANY)
    part = pltpu.VMEM((rows, width), low)
    return pl.pallas_call(
        functools.partial(middle_body, nz, units, slots, depth),
        out_shape=outs,
        in_specs=[pl.BlockSpec(memory_space=pltpu.SMEM)] + [vmem] * len(near) + [any_] * 8,
        out_specs=[any_] * 6 + [vmem] * (len(outs) - 6),
        scratch_shapes=[pltpu.VMEM(w.shape, low) for w in weights]
        + [pltpu.SemaphoreType.DMA((6,)), pltpu.VMEM(second_low.shape, low), pltpu.VMEM(second_low.shape, low)]
        + [pltpu.VMEM((4, rows, width), low)] * 2 + [pltpu.VMEM((2, rows, width), low)] * 2 + [part] * 4
        + [pltpu.SemaphoreType.DMA((2, 2, 2))] * 2 + [pltpu.SemaphoreType.DMA((2, 2))] * 2
        + [pltpu.VMEM((3, width, width), low), pltpu.SemaphoreType.DMA((6,))]
        + scatter_scratch(units, slots, nz),
        compiler_params=pltpu.CompilerParams(collective_id=5, has_side_effects=True, vmem_limit_bytes=VMEM_LIMIT),
        name="middle_back",
    )(bounds, *near, *weights, *feed)


class Gather:
    def __init__(self, here, units, slots, depth, given, held, outs, rows_out, sems):
        self.here, self.units, self.slots, self.depth = here, units, slots, depth
        self.outs, self.rows_out = outs, rows_out
        self.ins, self.rows_in = held[:-1], held[-1]
        (self.send_sem, self.recv_sem, self.core_send, self.core_recv, self.local_sem, self.rows_send,
         self.rows_recv) = sems
        self.last = {}
        for t, slot in enumerate(slots):
            for u, axis, j, fy, fx in slot.values():
                self.last[dict(z=(u, fy, fx), y=(u, 1, fx), x=(u, fy, 1))[axis]] = t
        self.done = -1
        self.loads = [pltpu.make_async_copy(given[g], held[g], self.local_sem.at[g]) for g in range(len(held))]
        self.steps = self.run()

    def piece(self, u, p):
        g, r0, rn, c0, cn = self.units[u]
        return self.outs[g].at[p[0], p[1], p[2], self.here.c, pl.ds(r0, rn), pl.ds(c0, cn)]

    def corner(self, u, fy, fx, which):
        g, r0, rn, c0, cn = self.units[u]
        here = self.here
        return self.outs[g].at[
            :, 1 - here.y if fy else here.y, 1 - here.x if fx else here.x, which, pl.ds(r0, rn), pl.ds(c0, cn)
        ]

    def remote(self, u, way, t, p, mine):
        ref = self.piece(u, p)
        g, r0, rn, c0, cn = self.units[u]
        return pltpu.make_async_remote_copy(
            src_ref=self.ins[g].at[pl.ds(r0, rn), pl.ds(c0, cn)] if mine else ref, dst_ref=ref,
            send_sem=self.send_sem.at[way, t], recv_sem=self.recv_sem.at[way, t],
            device_id=self.here.device[way], device_id_type=MESH,
        )

    def across(self, u, fy, fx):
        ref = self.corner(u, fy, fx, self.here.c)
        i = fy * 2 + fx
        return pltpu.make_async_remote_copy(
            src_ref=ref, dst_ref=ref, send_sem=self.core_send.at[u, i], recv_sem=self.core_recv.at[u, i],
            device_id=self.here.device[CORE], device_id_type=MESH,
        )

    def rows_over(self, src, dst, way, i):
        return pltpu.make_async_remote_copy(
            src_ref=src, dst_ref=dst, send_sem=self.rows_send.at[i], recv_sem=self.rows_recv.at[i],
            device_id=self.here.device[way], device_id_type=MESH,
        )

    def run(self):
        here, slots, depth, n = self.here, self.slots, self.depth, len(self.outs)
        z, y, x, c = here.z, here.y, here.x, here.c
        own = [pltpu.make_async_copy(self.ins[g], self.outs[g].at[z, y, x, c], self.local_sem.at[g]) for g in range(n)]
        own.append(pltpu.make_async_copy(self.rows_in, self.rows_out.at[x, c], self.local_sem.at[n]))
        for cp in self.loads:
            cp.start()
        here.greet()
        for cp in self.loads:
            cp.wait()
        for cp in own:
            cp.start()
        beside = self.rows_out.at[1 - x, c]
        self.rows_moves = [
            self.rows_over(self.rows_in, self.rows_out.at[x, c], XX, 0),
            self.rows_over(self.rows_in, self.rows_out.at[x, c], CORE, 1),
            self.rows_over(beside, beside, CORE, 2),
        ]
        self.rows_moves[0].start()
        self.rows_moves[1].start()
        for t in range(len(slots) + depth):
            if t < len(slots):
                for axis, (u, _, j, fy, fx) in slots[t].items():
                    for way, cond, p in here.gather_moves(axis, j, fy, fx)[0]:
                        when(cond, lambda u=u, way=way, p=p: self.remote(u, way, t, p, (j, fy, fx) == (0, 0, 0)).start())
            if t == depth - 1:
                for cp in own:
                    cp.wait()
            if t == 6:
                pltpu.make_async_copy(beside, beside, self.rows_recv.at[0]).wait()
                self.rows_moves[2].start()
            if t >= depth:
                for axis, (u, _, j, fy, fx) in slots[t - depth].items():
                    for way, cond, p in here.gather_moves(axis, j, fy, fx)[1]:
                        def got(u=u, way=way, p=p):
                            ref = self.piece(u, p)
                            pltpu.make_async_copy(ref, ref, self.recv_sem.at[way, t - depth]).wait()
                        when(cond, got)
                for key in sorted(self.last):
                    if self.last[key] == t - depth:
                        self.across(*key).start()
            self.done = t
            yield t
        for t, slot in enumerate(slots):
            for axis, (u, _, j, fy, fx) in slot.items():
                for way, cond, p in here.gather_moves(axis, j, fy, fx)[0]:
                    when(cond, lambda u=u, way=way, p=p: self.remote(u, way, t, p, (j, fy, fx) == (0, 0, 0)).wait_send())
        for u, fy, fx in sorted(self.last):
            self.across(u, fy, fx).wait_send()
        for cp in self.rows_moves:
            cp.wait_send()

    def advance(self, t):
        while self.done < min(t, len(self.slots) + self.depth - 1):
            next(self.steps)

    def frames(self):
        here = self.here
        self.advance(8)
        for i, ref in ((1, self.rows_out.at[here.x, 1 - here.c]), (2, self.rows_out.at[1 - here.x, 1 - here.c])):
            pltpu.make_async_copy(ref, ref, self.rows_recv.at[i]).wait()

    def arrived(self, u):
        self.advance(max(t for key, t in self.last.items() if key[0] == u) + self.depth + 1)
        for fy in range(2):
            for fx in range(2):
                ref = self.corner(u, fy, fx, 1 - self.here.c)
                pltpu.make_async_copy(ref, ref, self.core_recv.at[u, fy * 2 + fx]).wait()


def ahead_body(nz, units, slots, depth, every, *refs):
    bounds, frames, text, cot = refs[:4]
    given = refs[4:16]
    full, rows_out, dw_up, dw_down = refs[16:27], refs[27], refs[28], refs[29]
    (gains, own_low, q_out, k_out, v_out, attended, first, two_low, cross_query, cross_keys, cross_values, cross_mix,
     proj, block_out, grad_second, second_low, dgain, dbias) = refs[30:48]
    held, sems = refs[48:60], refs[60:67]
    (near, near_sem, down, down_sem, up, up_sem, rows_all, rows_sem, normed, grad_act, three_low, second, fed, grad_three,
     stage_down, stage_up, stage_sem) = refs[67:]
    here = Place(nz)
    low, wide = jnp.bfloat16, jnp.float32
    width, count = cot.shape[1], frames.shape[0]
    per = held[0].shape[0]
    gather = Gather(here, units, slots, depth, given, held, full, rows_out, sems)
    pace = Pace(gather.steps, every)
    spend = pace.spend
    tiles = [slice(i, i + 256) for i in range(0, width, 256)]
    depth_slots = near.shape[0]
    loads = {}

    def fetch(u):
        gather.arrived(u)
        slot = u % depth_slots
        loads[u] = pltpu.make_async_copy(full[units[u][0]], near.at[slot], near_sem.at[slot])
        loads[u].start()

    def weight(u, n):
        return near[u % depth_slots, :, :, :, :, :, n].reshape(width, -1)

    def apply(a, u, write, cost):
        if u > 0:
            loads[u].wait()
        for n in tiles:
            write(n, jnp.dot(a[...], weight(u, n), preferred_element_type=wide))
            spend(cost)

    def norm(v, i):
        xh, _ = norm_parts(v)
        return xh * gains[8 + i:9 + i] + gains[9 + i:10 + i]

    def put(ref):
        def write(n, r):
            ref[:, n] = r.astype(low)
        return write

    gather.frames()
    rows_load = pltpu.make_async_copy(rows_out, rows_all, rows_sem)
    rows_load.start()
    fetch(0)
    rows_load.wait()
    loads[0].wait()
    lane = lax.broadcasted_iota(jnp.int32, (128, width), 1)
    spread = jnp.where(lax.broadcasted_iota(jnp.int32, (128, width), 0) == lane % per, 1.0, 0.0).astype(low)
    corner = near[0, :, :, :, :, 16:32, 0:128].astype(wide).reshape(-1, 128).astype(low)
    wider = jnp.dot(corner, spread, preferred_element_type=wide)
    row = lax.broadcasted_iota(jnp.int32, wider.shape, 0)
    wider = jnp.where(row // 16 == lax.broadcasted_iota(jnp.int32, wider.shape, 1) // per, wider, 0.0)
    gains[...] = jnp.sum(wider.reshape(-1, 16, width), axis=0)
    spend(1.5)
    for i in range(2):
        for j in range(2):
            part = i * 2 + j
            normed[part * count:(part + 1) * count] = norm(rows_all[i, j].astype(wide), 0).astype(low)
            spend(0.7)
    own_low[...] = norm(frames[...].astype(wide), 0).astype(low)
    spend(0.7)
    apply(text, 0, put(proj), 0.4)
    fetch(1)
    fetch(2)
    apply(normed, 1, put(k_out), 0.8)
    fetch(3)
    apply(normed, 2, put(v_out), 0.8)
    fetch(4)
    apply(own_low, 3, put(q_out), 0.4)
    fetch(5)
    for i in range(0, width, 128):
        n = slice(i, i + 128)
        out = None
        for keep in halves(128):
            p = pair_scores((bounds[0], bounds[1]), q_out[:, n], k_out[:, n], keep, True).astype(low)
            o = jnp.dot(p, v_out[:, n], preferred_element_type=wide)
            out = o if out is None else jnp.where(keep, o, out)
            spend(0.65)
        attended[:, n] = out.astype(low)
    apply(proj, 4, put(cross_keys), 0.4)
    fetch(6)
    apply(proj, 5, put(cross_values), 0.4)
    fetch(7)

    def add_first(n, r):
        first[:, n] = frames[:, n].astype(wide) + r

    apply(attended, 6, add_first, 0.4)
    two_low[...] = norm(first[...], 2).astype(low)
    spend(0.7)
    fetch(8)
    apply(two_low, 7, put(cross_query), 0.4)
    for i in range(0, width, 128):
        n = slice(i, i + 128)
        out = None
        for keep in halves(128):
            p = pair_scores((bounds[2],), cross_query[:, n], cross_keys[:, n], keep, False).astype(low)
            o = jnp.dot(p, cross_values[:, n], preferred_element_type=wide)
            out = o if out is None else jnp.where(keep, o, out)
            spend(0.35)
        cross_mix[:, n] = out.astype(low)

    def add_second(n, r):
        second[:, n] = first[:, n] + r

    apply(cross_mix, 8, add_second, 0.4)
    three_low[...] = norm(second[...], 4).astype(low)
    grad_three[...] = jnp.zeros_like(grad_three)
    fed[...] = jnp.zeros_like(fed)
    spend(0.7)
    n_near = 9
    n_down = len([u for u in units if u[0] == 10])
    n_up = len(units) - n_near - n_down
    for u in range(n_near, n_near + n_down):
        gather.arrived(u)
    load = pltpu.make_async_copy(full[10], down, down_sem)
    load.start()
    ups = []

    def fetch_up(k):
        gather.arrived(n_near + n_down + k)
        slot = k % 2
        ups.append(pltpu.make_async_copy(
            full[9].at[:, :, :, :, :, pl.ds(k * width, width)], up.at[slot], up_sem.at[slot]))
        ups[k].start()

    fetch_up(0)
    load.wait()

    def down_rows(at):
        s = at // down.shape[4]
        return down[s // 8, s // 4 % 2, s // 2 % 2].reshape(-1, width)

    for at in range(0, n_up * width, 256):
        grad_act[:, at:at + 256] = dot_nt(cot[...], down_rows(at))
        spend(0.4)
    def stored(k):
        slot = k % 2
        rows = pl.ds(k * width, width)
        return [
            pltpu.make_async_copy(stage_down.at[slot], dw_down.at[rows], stage_sem.at[0, slot]),
            pltpu.make_async_copy(stage_up.at[slot], dw_up.at[:, rows], stage_sem.at[1, slot]),
        ]

    for k in range(n_up):
        slot = k % 2
        ups[k].wait()
        if k >= 2:
            for cp in stored(k - 2):
                cp.wait()
        for n in tiles:
            at = slice(k * width + n.start, k * width + n.stop)
            w = up[slot, :, :, :, :, :, n].reshape(width, -1)
            hidden = jnp.dot(three_low[...], w, preferred_element_type=wide)
            phi = 0.5 + 0.5 * lax.erf(hidden * (0.5 ** 0.5))
            act = (hidden * phi).astype(low)
            slope = phi + hidden * jnp.exp(-0.5 * hidden * hidden) * 0.3989422804014327
            grad = (grad_act[:, at] * slope).astype(low)
            spend(0.9)
            fed[...] += jnp.dot(act, down_rows(at.start), preferred_element_type=wide)
            grad_three[...] += dot_nt(grad, w)
            spend(0.8)
            stage_down[slot, n, :] = dot_tt(act, cot[...]).astype(low)
            stage_up[slot, :, n] = dot_tt(three_low[...], grad).astype(low)
            spend(1.1)
            if n.start == 256 and k + 1 < n_up:
                fetch_up(k + 1)
        for cp in stored(k):
            cp.start()
    for _ in gather.steps:
        pass
    block_out[...] = (second[...] + fed[...]).astype(low)
    dv, dgain[...], dbias[...] = norm_grads(second[...], gains[12:13], grad_three[...])
    dv = cot[...].astype(wide) + dv
    grad_second[...] = dv
    second_low[...] = dv.astype(low)
    for k in range(max(n_up - 2, 0), n_up):
        for cp in stored(k):
            cp.wait()


def ahead(bounds, frames, text, cot, arrays, units, perms, nz, depth=3, every=1.3):
    slots = make_schedule(perms, nz, lag=depth + 1)
    low, wide = jnp.bfloat16, jnp.float32
    count, width = frames.shape
    tokens, rows = text.shape[0], arrays[0].shape[0]
    hidden = arrays[9].shape[1]
    any_, vmem = pl.BlockSpec(memory_space=pl.ANY), pl.BlockSpec(memory_space=pltpu.VMEM)

    def like(n, kind):
        return jax.ShapeDtypeStruct((n, width), kind)

    given = [*arrays, frames]
    outs = [jax.ShapeDtypeStruct((nz, 2, 2, 2) + a.shape, a.dtype) for a in arrays]
    outs += [jax.ShapeDtypeStruct((2, 2) + frames.shape, low), jax.ShapeDtypeStruct((width, hidden), low), like(hidden, low)]
    far = len(outs)
    outs += [like(16, wide), like(count, low), like(count, low), like(4 * count, low), like(4 * count, low), like(count, low)]
    outs += [like(count, wide), like(count, low), like(count, low), like(tokens, low), like(tokens, low), like(count, low)]
    outs += [like(tokens, low), like(count, low), like(count, wide), like(count, low), like(1, wide), like(1, wide)]
    block = (nz, 2, 2, 2, rows, width)
    dma = pltpu.SemaphoreType.DMA
    return pl.pallas_call(
        functools.partial(ahead_body, nz, units, slots, depth, every),
        out_shape=outs,
        in_specs=[pl.BlockSpec(memory_space=pltpu.SMEM)] + [vmem] * 3 + [any_] * len(given),
        out_specs=[any_] * far + [vmem] * (len(outs) - far),
        scratch_shapes=[pltpu.VMEM(a.shape, a.dtype) for a in given]
        + [dma((4, len(slots)))] * 2 + [dma((len(units), 4))] * 2 + [dma((len(given),)), dma((3,)), dma((3,))]
        + [pltpu.VMEM((5,) + block, low), dma((5,))]
        + [pltpu.VMEM((nz, 2, 2, 2) + arrays[10].shape, low), dma]
        + [pltpu.VMEM((2,) + block, low), dma((2,))]
        + [pltpu.VMEM((2, 2) + frames.shape, low), dma, pltpu.VMEM((4 * count, width), low)]
        + [pltpu.VMEM((count, hidden), wide), pltpu.VMEM((count, width), low)] + [pltpu.VMEM((count, width), wide)] * 3
        + [pltpu.VMEM((2, width, width), low)] * 2 + [dma((2, 2))],
        compiler_params=pltpu.CompilerParams(collective_id=1, has_side_effects=True, vmem_limit_bytes=VMEM_LIMIT),
        name="ahead",
    )(bounds, frames, text, cot, *given)


def last_body(nz, units, slots, depth, late_first, *refs):
    bounds, query, keys, values, grad_mix, normed, frames, grad_first, gain, others = refs[:10]
    weights, text, early = refs[10:13], refs[13], refs[14:19]
    frames_grad, sums = refs[19:21]
    held, (weight_sem, grad_q, grad_k, grad_v, twin_k, twin_v, sum_k, sum_v, land_k, land_v) = refs[21:24], refs[24:34]
    share_sems, late, grad_norm, scatter = refs[34:38], refs[38], refs[39], refs[40:]
    here = Place(nz)
    low, wide = jnp.bfloat16, jnp.float32
    count, width = normed.shape
    loads = [pltpu.make_async_copy(w, h, weight_sem.at[i]) for i, (w, h) in enumerate(zip(weights, held))]
    loads.append(pltpu.make_async_copy(text, late.at[3], weight_sem.at[3]))
    for cp in loads:
        cp.start()
    ins = [late.at[0], late.at[1], late.at[2], early[0], early[1], early[2], early[3], early[4], late.at[3]]
    late_units = [u for u, unit in enumerate(units) if unit[0][0] in (0, 1, 2, 8)]
    unit_of = {units[u][0][0]: u for u in late_units}
    steps = scatter_steps(here, units, slots, depth, ins, *scatter, late=late_units)
    begin_unit = next(steps)
    done = [-1]

    def spend(time, pace=Pace(None, 30.0 / (late_first + 2))):
        pace.owed += time
        while pace.owed >= pace.every:
            pace.owed -= pace.every
            if done[0] < late_first - 1:
                done[0] += 1
                next(steps)

    share = Share(here, (grad_k, grad_v), (twin_k, twin_v), (sum_k, sum_v), (land_k, land_v), *share_sems, width // 2)
    tiles = [slice(i, i + 256) for i in range(0, width, 256)]
    pairs = width // 128
    next(steps)
    done[0] += 1
    for i in range(pairs):
        n = slice(i * 128, i * 128 + 128)
        dq, dk, dv = pair_grads(bounds, True, query[:, n], keys[:, n], values[:, n], grad_mix[:, n], lambda: spend(1.0))
        grad_q[:, n] = dq
        grad_k[:, :, n] = dk.reshape(4, count, 128)
        grad_v[:, :, n] = dv.reshape(4, count, 128)
        if i == pairs // 2 - 1:
            share.send(0)
        if i == pairs // 2 + 1:
            share.forward(0)
    share.send(1)

    def outer(slot, rows):
        height = width // nz
        for i in range(nz):
            r = dot_tt(normed[:, i * height:(i + 1) * height], rows).astype(low)
            late[slot, i] = r.reshape(late.shape[2:])
            spend(0.55)

    def back(slot, rows, first):
        for n in tiles:
            r = dot_nt(rows, held[slot][n, :])
            grad_norm[:, n] = r if first else grad_norm[:, n] + r
            spend(0.4)

    outer(0, grad_q[...])
    begin_unit(unit_of[0])
    share.forward(1)
    for cp in loads:
        cp.wait()
    back(0, grad_q[...], True)
    for g in range(2):
        rows = jnp.concatenate([share.collect(g, k) for k in range(2)], axis=1)
        outer(1 + g, rows)
        begin_unit(unit_of[1 + g])
        back(1 + g, rows, False)
    dv, dgain, dbias = norm_grads(frames[...].astype(wide), gain[...], grad_norm[...])
    frames_grad[...] = (grad_first[...] + dv).astype(low)
    per = width // (nz * 8)
    both = jnp.concatenate([dgain, dbias, others[...], jnp.zeros((2, width), wide)], axis=0)
    both = jnp.broadcast_to(both[None], (nz * 8, 8, width)).reshape(-1, width)
    row = lax.broadcasted_iota(jnp.int32, both.shape, 0)
    both = jnp.where(row // 8 == lax.broadcasted_iota(jnp.int32, both.shape, 1) // per, both, 0.0).astype(low)
    lane = lax.broadcasted_iota(jnp.int32, (128, width), 1)
    spread = jnp.where(lax.broadcasted_iota(jnp.int32, (128, width), 0) == lane % per, 1.0, 0.0).astype(low)
    block = late[3, :, :, :, :, 16:32, 0:128].astype(wide).reshape(-1, 16, 128)
    tail = dot_nt(both, spread).reshape(-1, 8, 128)
    block = jnp.concatenate([block[:, :8], tail], axis=1)
    late[3, :, :, :, :, 16:32, 0:128] = block.astype(low).reshape(nz, 2, 2, 2, 16, 128)
    begin_unit(unit_of[8])
    for _ in steps:
        pass
    share.finish(2)
    total = scatter[0]
    for u in range(len(units)):
        sums[u] = total[u, here.z, here.y, here.x].astype(wide)


def last_back(bounds, near, weights, text, early, units, perms, nz, depth=3):
    slots = make_schedule(perms, nz, lag=depth + 1, window=3)
    firsts = {}
    for t, slot in enumerate(slots[::-1]):
        for op in slot.values():
            firsts.setdefault(op[0], t)
    late_first = min(firsts[u] for u, unit in enumerate(units) if unit[0][0] in (0, 1, 2, 8))
    count, width = near[4].shape
    low, wide = jnp.bfloat16, jnp.float32
    vmem, any_ = pl.BlockSpec(memory_space=pltpu.VMEM), pl.BlockSpec(memory_space=pl.ANY)
    part = pltpu.VMEM((count, width), low)
    outs = [jax.ShapeDtypeStruct((count, width), low), jax.ShapeDtypeStruct((len(units),) + unit_shape(units), wide)]
    return pl.pallas_call(
        functools.partial(last_body, nz, units, slots, depth, late_first),
        out_shape=outs,
        in_specs=[pl.BlockSpec(memory_space=pltpu.SMEM)] + [vmem] * len(near) + [any_] * 9,
        out_specs=[vmem] * 2,
        scratch_shapes=[pltpu.VMEM(w.shape, low) for w in weights]
        + [pltpu.SemaphoreType.DMA((4,)), part]
        + [pltpu.VMEM((4, count, width), low)] * 2 + [pltpu.VMEM((2, count, width), low)] * 2 + [part] * 4
        + [pltpu.SemaphoreType.DMA((2, 2, 2))] * 2 + [pltpu.SemaphoreType.DMA((2, 2))] * 2
        + [pltpu.VMEM((4,) + text.shape, low), pltpu.VMEM((count, width), wide)]
        + scatter_scratch(units, slots, nz),
        compiler_params=pltpu.CompilerParams(collective_id=2, has_side_effects=True, vmem_limit_bytes=VMEM_LIMIT),
        name="last_back",
    )(bounds, *near, *weights, text, *early)


eps_norm = 1e-05


def layer_norm(values_in, gain_vec, shift_vec):
    centre = values_in - jnp.mean(values_in, axis=-1, keepdims=True)
    spread = jnp.mean(centre * centre, axis=-1, keepdims=True)
    return centre * lax.rsqrt(spread + eps_norm) * gain_vec + shift_vec


def gelu_exact(values_in):
    return jax.nn.gelu(values_in, approximate=False)


def project(left, right):
    return jnp.einsum("gti,ij->gtj", left, right, preferred_element_type=jnp.float32)


def project_back(left, right):
    return jnp.einsum("gtj,ij->gti", left, right, preferred_element_type=jnp.float32)


def outer_sum(left, right):
    return jnp.einsum("gti,gtj->ij", left, right, preferred_element_type=jnp.float32)


class Params(NamedTuple):
    w_query: jax.Array
    w_key: jax.Array
    w_value: jax.Array
    w_out: jax.Array
    c_query: jax.Array
    c_key: jax.Array
    c_value: jax.Array
    c_out: jax.Array
    w_text: jax.Array
    w_up: jax.Array
    w_down: jax.Array
    gain_attn: jax.Array
    bias_attn: jax.Array
    gain_cross: jax.Array
    bias_cross: jax.Array
    gain_feed: jax.Array
    bias_feed: jax.Array


BLOCKS, GAINS = 11, 6


def all_axes():
    return ("dp", "seq")


def fits(own, frames, text):
    rows, width = own.w_query.shape
    return (
        lax.axis_size("seq") == 4 and lax.axis_size("dp") % 2 == 0 and rows == 32 and width % 128 == 0
        and own.w_text.shape[0] % 8 == 0 and own.w_text.shape[0] + 8 == rows
        and own.w_up.shape[0] == rows and own.w_up.shape[1] % width == 0
        and own.w_down.shape == (own.w_up.shape[1] // width * rows, width) and own.w_down.shape[0] == 128
        and width == rows * lax.axis_size("dp") * 4
        and frames.shape[0] == 1 and frames.shape[1] % 32 == 0 and text.shape[0] == 1 and text.shape[1] % 128 == 0
    )


class PlainWires:
    def gather(self, own, frames):
        full = Params(*[lax.all_gather(v, all_axes(), axis=0, tiled=True) for v in own])
        return full, lax.all_gather(frames, "seq", axis=1, tiled=True)

    def scatter(self, grads):
        return Params(*[lax.psum_scatter(v, all_axes(), scatter_dimension=0, tiled=True) for v in grads])

    def share(self, arrays, number):
        return [lax.psum_scatter(a, "seq", scatter_dimension=1, tiled=True) for a in arrays]


def attention(causal, bounds, q, k, v):
    return attend(causal, bounds[0], q[0], k[0], v[0])[None]


def attention_back(causal, bounds, *operands):
    return [r[None] for r in attend_grads(causal, bounds[0], *[a[0] for a in operands])]


def plain_layer(own, frames, cotangent, text_states, frame_start, prompt_len):
    low = jnp.bfloat16
    wires = PlainWires()
    full, all_frames = wires.gather(own, frames)
    wide = [v.astype(jnp.float32) for v in full[BLOCKS:]]
    frames_f = frames.astype(jnp.float32)
    frame_count = frames.shape[1]
    normed, norm_one_back = jax.vjp(layer_norm, frames_f, wide[0], wide[1])
    normed_low = normed.astype(low)
    normed_all = layer_norm(all_frames.astype(jnp.float32), wide[0], wide[1]).astype(low)
    query_rows = project(normed_low, full.w_query).astype(low)
    key_all = project(normed_all, full.w_key).astype(low)
    value_all = project(normed_all, full.w_value).astype(low)
    rank = lax.axis_index("seq")
    self_bounds = jnp.stack([jnp.full_like(frame_start, rank * frame_count), frame_start], axis=1)
    attended = attention(True, self_bounds, query_rows, key_all, value_all)
    first = frames_f + project(attended, full.w_out)
    text_count = text_states.shape[1]
    quarter = text_count // lax.axis_size("seq")
    text_start = rank * quarter
    text_part = lax.dynamic_slice_in_dim(text_states, text_start, quarter, 1)
    proj_all = project(text_states, full.w_text).astype(low)
    cross_keys = project(proj_all, full.c_key).astype(low)
    cross_values = project(proj_all, full.c_value).astype(low)
    proj_part = lax.dynamic_slice_in_dim(proj_all, text_start, quarter, 1)
    normed_two, norm_two_back = jax.vjp(layer_norm, first, wide[2], wide[3])
    normed_two_low = normed_two.astype(low)
    cross_query = project(normed_two_low, full.c_query).astype(low)
    cross_bounds = jnp.stack([prompt_len, prompt_len], axis=1)
    cross_mix = attention(False, cross_bounds, cross_query, cross_keys, cross_values)
    second = first + project(cross_mix, full.c_out)
    normed_three, norm_three_back = jax.vjp(layer_norm, second, wide[4], wide[5])
    three_low = normed_three.astype(low)
    hidden = project(three_low, full.w_up)
    activated, gelu_back = jax.vjp(gelu_exact, hidden)
    act_low = activated.astype(low)
    block_out = (second + project(act_low, full.w_down)).astype(low)
    grad_act = project_back(cotangent, full.w_down)
    dw_down = outer_sum(act_low, cotangent)
    grad_hidden = gelu_back(grad_act)[0].astype(low)
    dw_up = outer_sum(three_low, grad_hidden)
    grad_second_ln, dgain_feed, dbias_feed = norm_three_back(project_back(grad_hidden, full.w_up))
    grad_second = cotangent.astype(jnp.float32) + grad_second_ln
    second_low = grad_second.astype(low)
    dc_out = outer_sum(cross_mix, second_low)
    grad_cross_mix = project_back(second_low, full.c_out).astype(low)
    cq_low, grad_ck, grad_cv = attention_back(
        False, cross_bounds, cross_query, cross_keys, cross_values, grad_cross_mix
    )
    ck_low, cv_low = wires.share([grad_ck, grad_cv], 3)
    dc_key = outer_sum(proj_part, ck_low)
    dc_value = outer_sum(proj_part, cv_low)
    grad_proj = (project_back(ck_low, full.c_key) + project_back(cv_low, full.c_value)).astype(low)
    dw_text = outer_sum(text_part, grad_proj)
    text_grad = project_back(grad_proj, full.w_text)
    dc_query = outer_sum(normed_two_low, cq_low)
    grad_first_ln, dgain_cross, dbias_cross = norm_two_back(project_back(cq_low, full.c_query))
    grad_first = grad_second + grad_first_ln
    first_low = grad_first.astype(low)
    dw_out = outer_sum(attended, first_low)
    grad_attended = project_back(first_low, full.w_out).astype(low)
    q_low, grad_k_all, grad_v_all = attention_back(
        True, self_bounds, query_rows, key_all, value_all, grad_attended
    )
    k_low, v_low = wires.share([grad_k_all, grad_v_all], 4)
    dw_query = outer_sum(normed_low, q_low)
    dw_key = outer_sum(normed_low, k_low)
    dw_value = outer_sum(normed_low, v_low)
    grad_normed = (
        project_back(q_low, full.w_query) + project_back(k_low, full.w_key) + project_back(v_low, full.w_value)
    )
    grad_frames_ln, dgain_attn, dbias_attn = norm_one_back(grad_normed)
    frames_grad = (grad_first + grad_frames_ln).astype(low)
    sums = wires.scatter(
        Params(
            dw_query, dw_key, dw_value, dw_out, dc_query, dc_key, dc_value, dc_out, dw_text, dw_up, dw_down,
            dgain_attn, dbias_attn, dgain_cross, dbias_cross, dgain_feed, dbias_feed,
        )
    )
    return (block_out, frames_grad, text_grad, *sums)


NEAR_ORDERS = ("zyx", "zxy", "zyx", "zxy", "zyx", "zxy", "zyx", "zxy", "zyx")
LATE_ORDERS = ("zxy", "yxz", "zyx", "xyz", "zxy", "zyx", "yxz", "xyz")
LAST_ORDERS = ("zxy", "zxy", "zxy", "yxz", "zyx", "zyx", "yxz", "xzy", "zxy")
FEED_ORDERS = ("zyx", "zxy", "zyx", "yxz", "zxy", "zyx", "xyz", "zxy")


def cycle(orders, n):
    return [orders[i % len(orders)] for i in range(n)]


def fast_layer(own, frames, cotangent, text_states, frame_start, prompt_len):
    low, wide = jnp.bfloat16, jnp.float32
    nz = lax.axis_size("dp") // 2
    shards = nz * 8
    rows, width = own.w_query.shape
    text_rows = own.w_text.shape[0]
    count = frames.shape[1]
    rank = lax.axis_index("seq")
    up, down = own.w_up.shape[1] // width, own.w_down.shape[0] // rows
    near_units = [(g, 0, rows, 0, width) for g in range(9)]
    up_units = [(9, 0, rows, k * width, width) for k in range(up)]
    down_units = [(10, k * rows, rows, 0, width) for k in range(down)]
    units = [near_units[i] for i in (8, 1, 2, 0, 5, 6, 3, 4, 7)] + down_units + up_units
    gains = jnp.stack(own[BLOCKS:])
    gains = jnp.pad(gains, ((0, rows - text_rows - GAINS), (0, width - gains.shape[1])))
    arrays = list(own[:BLOCKS])
    arrays[8] = jnp.concatenate([own.w_text, gains], axis=0)
    tokens = text_states.shape[1]
    text = jnp.pad(text_states.reshape((tokens, shards, text_rows)), ((0, 0), (0, 0), (0, rows - text_rows))).reshape((tokens, width))
    bounds = jnp.concatenate([jnp.full_like(frame_start, rank * count), frame_start, prompt_len])
    cot = cotangent[0]
    orders = cycle(NEAR_ORDERS, 9) + cycle(LATE_ORDERS, up + down)
    outs = ahead(bounds, frames[0], text, cot, arrays, units, orders, nz)
    full, (_, dw_up, dw_down) = [f.reshape((-1, f.shape[-1])) for f in outs[:BLOCKS]], outs[BLOCKS:BLOCKS + 3]
    (gains, normed_low, query_rows, key_all, value_all, attended, first, two_low, cross_query, cross_keys, cross_values,
     cross_mix, proj, block_out, grad_second, second_low, dgain_feed, dbias_feed) = outs[BLOCKS + 3:]
    quarter = tokens // 4
    text_part = lax.dynamic_slice_in_dim(text, rank * quarter, quarter, 0)
    proj_part = lax.dynamic_slice_in_dim(proj, rank * quarter, quarter, 0)
    near = [second_low, grad_second, cross_mix, cross_query, cross_keys, cross_values, two_low, first, text_part, proj_part, attended, gains[10:11]]
    weights = [full[i] for i in (7, 4, 5, 6, 8, 3)]
    lead = (nz, 2, 2, 2)
    feed = [v.reshape(lead + (-1, v.shape[-1])) for v in (dw_up, dw_down)]
    feed_units = [((g - 9, *rest),) for g, *rest in up_units + down_units]
    (dc_out, dc_query, dw_out, dc_key, dc_value, dw_text, text_grad, grad_first, grad_attended, dgain_cross, dbias_cross,
     feed_sums) = middle_back(bounds[2:], near, weights, feed, feed_units, cycle(FEED_ORDERS, up + down), nz)
    others = jnp.concatenate([dgain_cross, dbias_cross, dgain_feed, dbias_feed], axis=0)
    last = [query_rows, key_all, value_all, grad_attended, normed_low, frames[0], grad_first, gains[8:9], others]
    text_block, *early = [v.reshape(lead + (rows, width)) for v in (dw_text, dw_out, dc_query, dc_key, dc_value, dc_out)]
    last_units = [(near_units[i],) for i in (8, 2, 1, 0, 7, 6, 5, 4, 3)]
    frames_grad, sums = last_back(bounds[:2], last, full[:3], text_block, early, last_units, LAST_ORDERS, nz)
    shapes = [(rows, width)] * 9 + [own.w_up.shape, own.w_down.shape]
    feed_units = [((g + 9, *rest),) for ((g, *rest),) in feed_units]
    *blocks, tail = deliver((sums, feed_sums), (last_units, feed_units), text_rows, shapes)
    text_grad = text_grad.reshape((quarter, shards, rows))[:, :, :text_rows].reshape((1, quarter, -1))
    return (block_out[None], frames_grad[None], text_grad, *blocks, *[tail[i, : width // shards] for i in range(GAINS)])


def on_device(frames, cotangent, text_states, frame_start, prompt_len, *params):
    own = Params(*params)
    layer = fast_layer if fits(own, frames, text_states) else plain_layer
    return layer(own, frames, cotangent, text_states, frame_start, prompt_len)


def solution(mesh):
    both = P(all_axes(), None)
    rows, vector = P(*all_axes(), None), P(all_axes())
    item, whole = P("dp"), P("dp", None, None)
    return jax.shard_map(
        on_device,
        mesh=mesh,
        in_specs=(rows, rows, whole, item, item) + (both,) * BLOCKS + (vector,) * GAINS,
        out_specs=(rows,) * 3 + (both,) * BLOCKS + (vector,) * GAINS,
        check_vma=False,
    )
```

```python
import functools
from typing import NamedTuple
import jax
import jax.numpy as jnp
from jax import lax
from jax.experimental import pallas as pl
from jax.experimental.pallas import tpu as pltpu
from jax.sharding import PartitionSpec as P

MESH = pl.DeviceIdType.MESH

LAG = 2
VMEM_LIMIT = 60 * 1024 * 1024

def unit_ops(perm, nz):
    rank = {a: i for i, a in enumerate(perm)}
    ops = {}

    def source(j, fy, fx):
        differs = [a for a, f in (("z", j > 0), ("y", fy), ("x", fx)) if f]
        if not differs:
            return None
        last = max(differs, key=lambda a: rank[a])
        if last == "z":
            return ("z", j - 1, fy, fx)
        if last == "y":
            return ("y", j, 0, fx)
        return ("x", j, fy, 0)

    for j in range(nz):
        for fy in range(2):
            for fx in range(2):
                for axis in "zyx":
                    flags = {"z": j > 0, "y": fy, "x": fx}
                    if axis != "z" and flags[axis]:
                        continue
                    if any(flags[a] and rank[a] > rank[axis] for a in "zyx" if a != axis):
                        continue
                    if axis == "z" and j == nz - 1:
                        continue
                    ops[(axis, j, fy, fx)] = source(j, fy, fx)
    return ops

def make_schedule(perms, nz, lag=LAG, window=None, slope=0.0):
    ops = {}
    for u, perm in enumerate(perms):
        for key, dep in unit_ops(perm, nz).items():
            ops[(u,) + key] = None if dep is None else (u,) + dep
    children = {}
    for op, dep in ops.items():
        children.setdefault(dep, []).append(op)
    height = {}

    def tall(op):
        if op not in height:
            height[op] = 1 + max([tall(c) for c in children.get(op, [])], default=0)
        return height[op]

    for op in ops:
        tall(op)
    done, slots, left = {}, [], set(ops)
    while left:
        t = len(slots)
        slot = {}
        for axis in "zyx":
            ready = [op for op in left if op[1] == axis and (ops[op] is None or (ops[op] in done and done[ops[op]] + lag <= t))]
            if ready:
                slot[axis] = min(ready, key=lambda op: (op[0] // window if window else 0, slope * op[0] - height[op], op[0], op))
        for axis, op in slot.items():
            done[op] = t
            left.discard(op)
        slots.append(slot)
    return slots

def nth_table(nz):
    rows = []
    for z in range(nz):
        offs = sorted((p - z for p in range(nz)), key=lambda o: (abs(o), o if z % 2 else -o))
        rows.append([z + o for o in offs])
    return rows

def pick(values, z):
    out = 0
    for i, v in enumerate(values):
        out = out + v * jnp.where(z == i, 1, 0)
    return out

UP, DOWN, YY, XX, CORE = range(5)
WAYS_OF = dict(z=(UP, DOWN), y=(YY,), x=(XX,))

class Place:
    def __init__(self, nz):
        d, s = lax.axis_index("dp"), lax.axis_index("seq")
        self.nz = nz
        self.z, self.y, self.x, self.c = d // 2, d % 2, s // 2, s % 2
        z, y, x, c = self.z, self.y, self.x, self.c
        self.device = [
            ((z + 1) * 2 + y, x * 2 + c),
            ((z - 1) * 2 + y, x * 2 + c),
            (z * 2 + 1 - y, x * 2 + c),
            (z * 2 + y, (1 - x) * 2 + c),
            (z * 2 + y, x * 2 + 1 - c),
        ]
        self.nth = [[row[j] for row in nth_table(nz)] for j in range(nz)]

    def greet(self):
        barrier = pltpu.get_barrier_semaphore()
        has_up, has_down = self.z + 1 < self.nz, self.z > 0
        for way in range(5):
            def hello(way=way):
                pl.semaphore_signal(barrier, inc=1, device_id=self.device[way], device_id_type=MESH)
            if way < YY:
                pl.when(has_up if way == UP else has_down)(hello)
            else:
                hello()
        edge = jnp.where(self.z == 0, 1, 0) + jnp.where(self.z == self.nz - 1, 1, 0)
        pl.semaphore_wait(barrier, 5 - edge)

    def gather_moves(self, axis, j, fy, fx):
        z, y, x, nz = self.z, self.y, self.x, self.nz
        py, px = (1 - y if fy else y), (1 - x if fx else x)
        if axis == "z":
            out = [(UP, (z - j >= 0) & (z + 1 < nz), (z - j, py, px)), (DOWN, (z + j < nz) & (z > 0), (z + j, py, px))]
            come = [(UP, z - 1 - j >= 0, (z - 1 - j, py, px)), (DOWN, z + 1 + j < nz, (z + 1 + j, py, px))]
        else:
            pz = pick(self.nth[j], z)
            there = (pz, 1 - y, px) if axis == "y" else (pz, py, 1 - x)
            way = YY if axis == "y" else XX
            out = [(way, None, (pz, py, px))]
            come = [(way, None, there)]
        return out, come

def when(cond, fn):
    if cond is None:
        fn()
    else:
        pl.when(cond)(fn)

BACK = (DOWN, UP, YY, XX)


def scatter_steps(here, units, slots, depth, ins, total, twin, landed, send_sem, recv_sem, core_send, core_recv, local_sem, late=()):
    nz = here.nz
    z, y, x, c = here.z, here.y, here.x, here.c
    steps = slots[::-1]
    numbers, order = {}, []
    for t, slot in enumerate(steps):
        for axis, op in slot.items():
            for way in WAYS_OF[axis]:
                numbers[way, t] = len(numbers)
            if op[0] not in order:
                order.append(op[0])

    def plane(u, b, which):
        g, r0, rn, c0, cn = units[u][b]
        return ins[g].at[:, :, :, which, pl.ds(r0, rn), pl.ds(c0, cn)]

    def rows_of(buffer, u, b):
        rn = units[u][b][2]
        return buffer.at[u, :, :, :, pl.ds(b * rn, rn)]

    def local(u, b):
        return pltpu.make_async_copy(plane(u, b, c), rows_of(total, u, b), local_sem.at[u, b])

    def across(u, b):
        return pltpu.make_async_remote_copy(
            src_ref=plane(u, b, 1 - c), dst_ref=rows_of(twin, u, b), send_sem=core_send.at[u, b],
            recv_sem=core_recv.at[u, b], device_id=here.device[CORE], device_id_type=MESH,
        )

    def remote(u, way, t, p):
        i = numbers[way, t]
        return pltpu.make_async_remote_copy(
            src_ref=total.at[u, p[0], p[1], p[2]], dst_ref=landed.at[i], send_sem=send_sem.at[i], recv_sem=recv_sem.at[i],
            device_id=here.device[BACK[way]], device_id_type=MESH,
        )

    ahead = 3
    blocks = range(len(units[0]))
    early = [u for u in order if u not in late]

    def begin_unit(u):
        for b in blocks:
            local(u, b).start()
            across(u, b).start()

    for u in early[:ahead]:
        for b in blocks:
            local(u, b).start()
    here.greet()
    for u in early[:ahead]:
        for b in blocks:
            across(u, b).start()
    if late:
        yield begin_unit

    def join(u):
        later = early.index(u) + ahead if u in early else len(early)
        if later < len(early):
            begin_unit(early[later])
        for b in blocks:
            local(u, b).wait()
            across(u, b).wait_recv()

        @pl.loop(0, nz)
        def _(a):
            for b in range(2):
                for e in range(2):
                    total[u, a, b, e] = (
                        total[u, a, b, e].astype(jnp.float32) + twin[u, a, b, e].astype(jnp.float32)
                    ).astype(jnp.bfloat16)

    joined = set()
    for t in range(len(steps) + depth):
        if t < len(steps):
            for axis, (u, _, j, fy, fx) in steps[t].items():
                if u not in joined:
                    joined.add(u)
                    join(u)
                for way, cond, p in here.gather_moves(axis, j, fy, fx)[1]:
                    when(cond, lambda u=u, way=way, p=p: remote(u, way, t, p).start())
        if t >= depth:
            s = t - depth
            for axis, (u, _, j, fy, fx) in steps[s].items():
                for way, cond, p in here.gather_moves(axis, j, fy, fx)[0]:
                    def add(u=u, way=way, p=p):
                        i = numbers[way, s]
                        pltpu.make_async_copy(landed.at[i], landed.at[i], recv_sem.at[i]).wait()
                        total[u, p[0], p[1], p[2]] = (
                            total[u, p[0], p[1], p[2]].astype(jnp.float32) + landed[i].astype(jnp.float32)
                        ).astype(jnp.bfloat16)
                    when(cond, add)
        yield t
    for t, slot in enumerate(steps):
        for axis, (u, _, j, fy, fx) in slot.items():
            for way, cond, p in here.gather_moves(axis, j, fy, fx)[1]:
                when(cond, lambda u=u, way=way, p=p: remote(u, way, t, p).wait_send())
    for u in order:
        for b in blocks:
            across(u, b).wait_send()


def unit_shape(units):
    return sum(block[2] for block in units[0]), units[0][0][4]


def scatter_scratch(units, slots, nz):
    rows, columns = unit_shape(units)
    count = sum(len(WAYS_OF[axis]) for slot in slots for axis in slot)
    plane = (len(units), nz, 2, 2, rows, columns)
    return [
        pltpu.VMEM(plane, jnp.bfloat16),
        pltpu.VMEM(plane, jnp.bfloat16),
        pltpu.VMEM((count, rows, columns), jnp.bfloat16),
        pltpu.SemaphoreType.DMA((count,)),
        pltpu.SemaphoreType.DMA((count,)),
        pltpu.SemaphoreType.DMA((len(units), len(units[0]))),
        pltpu.SemaphoreType.DMA((len(units), len(units[0]))),
        pltpu.SemaphoreType.DMA((len(units), len(units[0]))),
    ]


def deliver_body(parts, text_rows, n, *refs):
    ins, outs = refs[:n], refs[n:]
    for sums, units in zip(ins, parts):
        for u, unit in enumerate(units):
            for b, (g, r0, rn, c0, cn) in enumerate(unit):
                if g == 8:
                    outs[g][...] = sums[u, :text_rows]
                    outs[-1][...] = sums[u, text_rows:text_rows + 8]
                else:
                    outs[g][r0:r0 + rn, c0:c0 + cn] = sums[u, b * rn:(b + 1) * rn]


def deliver(sums, parts, text_rows, shapes):
    shapes = [(text_rows,) + s[1:] if g == 8 else s for g, s in enumerate(shapes)] + [(8, sums[0].shape[2])]
    return pl.pallas_call(
        functools.partial(deliver_body, parts, text_rows, len(sums)),
        out_shape=[jax.ShapeDtypeStruct(s, jnp.float32) for s in shapes],
        compiler_params=pltpu.CompilerParams(vmem_limit_bytes=16 * 1024 * 1024),
        name="deliver",
    )(*sums)


def pair_scores(bounds_ref, q, k, keep, causal):
    s = lax.dot_general(jnp.where(keep, q, 0), k, (((1,), (1,)), ((), ())), preferred_element_type=jnp.float32)
    col = lax.broadcasted_iota(jnp.int32, s.shape, 1)
    if causal:
        row = lax.broadcasted_iota(jnp.int32, s.shape, 0) + bounds_ref[0]
        seen = (col <= row) & ((col >= bounds_ref[1]) | (col == row))
    else:
        seen = col < bounds_ref[0]
    s = jnp.where(seen, s * 0.125, -1e30)
    e = jnp.exp(s - jnp.max(s, axis=1, keepdims=True))
    return e * (1.0 / jnp.sum(e, axis=1, keepdims=True))


def halves(width):
    lane = lax.broadcasted_iota(jnp.int32, (1, width), 1)
    return [(lane >= 64 * h) & (lane < 64 * h + 64) for h in range(width // 64)]


def attend_body(causal, bounds_ref, q_ref, k_ref, v_ref, out_ref):
    q, k, v = q_ref[...], k_ref[...], v_ref[...]
    out = None
    for keep in halves(q.shape[1]):
        p = pair_scores(bounds_ref, q, k, keep, causal)
        o = jnp.dot(p.astype(jnp.bfloat16), v, preferred_element_type=jnp.float32)
        out = o if out is None else jnp.where(keep, o, out)
    out_ref[...] = out.astype(jnp.bfloat16)


def attend_back_body(causal, bounds_ref, q_ref, k_ref, v_ref, g_ref, dq_ref, dk_ref, dv_ref):
    q, k, v, g = q_ref[...], k_ref[...], v_ref[...], g_ref[...]
    dq = dk = dv = None
    for keep in halves(q.shape[1]):
        p = pair_scores(bounds_ref, q, k, keep, causal)
        dp = lax.dot_general(jnp.where(keep, g, 0), v, (((1,), (1,)), ((), ())), preferred_element_type=jnp.float32)
        ds = (p * (dp - jnp.sum(p * dp, axis=1, keepdims=True))).astype(jnp.bfloat16)
        a = jnp.dot(ds, k, preferred_element_type=jnp.float32)
        b = lax.dot_general(ds, q, (((0,), (0,)), ((), ())), preferred_element_type=jnp.float32)
        e = lax.dot_general(p.astype(jnp.bfloat16), g, (((0,), (0,)), ((), ())), preferred_element_type=jnp.float32)
        if dq is None:
            dq, dk, dv = a, b, e
        else:
            dq, dk, dv = jnp.where(keep, a, dq), jnp.where(keep, b, dk), jnp.where(keep, e, dv)
    dq_ref[...] = (dq * 0.125).astype(jnp.bfloat16)
    dk_ref[...] = (dk * 0.125).astype(jnp.bfloat16)
    dv_ref[...] = dv.astype(jnp.bfloat16)


def attend_call(body, causal, bounds, operands, n_out_rows):
    width = operands[0].shape[1]
    spec = [pl.BlockSpec((a.shape[0], 128), lambda i: (0, i)) for a in operands]
    return pl.pallas_call(
        functools.partial(body, causal),
        grid=(width // 128,),
        out_shape=[jax.ShapeDtypeStruct((r, width), jnp.bfloat16) for r in n_out_rows],
        in_specs=[pl.BlockSpec(memory_space=pltpu.SMEM)] + spec,
        out_specs=[pl.BlockSpec((r, 128), lambda i: (0, i)) for r in n_out_rows],
        compiler_params=pltpu.CompilerParams(vmem_limit_bytes=32 * 1024 * 1024),
        name=("self_" if causal else "cross_") + body.__name__,
    )(bounds, *operands)


def attend(causal, bounds, q, k, v):
    return attend_call(attend_body, causal, bounds, (q, k, v), [q.shape[0]])[0]


def attend_grads(causal, bounds, q, k, v, g):
    return attend_call(attend_back_body, causal, bounds, (q, k, v, g), [q.shape[0], k.shape[0], k.shape[0]])


def dot_tt(a, b):
    return lax.dot_general(a, b, (((0,), (0,)), ((), ())), preferred_element_type=jnp.float32)


def dot_nt(a, b):
    return lax.dot_general(a, b, (((1,), (1,)), ((), ())), preferred_element_type=jnp.float32)


def norm_parts(v):
    centre = v - jnp.mean(v, axis=1, keepdims=True)
    rate = lax.rsqrt(jnp.mean(centre * centre, axis=1, keepdims=True) + eps_norm)
    return centre * rate, rate


def norm_grads(v, gain, h):
    xh, rate = norm_parts(v)
    hg = h * gain
    dv = (hg - jnp.mean(hg, axis=1, keepdims=True) - xh * jnp.mean(hg * xh, axis=1, keepdims=True)) * rate
    return dv, jnp.sum(h * xh, axis=0, keepdims=True), jnp.sum(h, axis=0, keepdims=True)


class Share:
    def __init__(self, here, mine, twins, sums, landed, core_send, core_recv, x_send, x_recv, chunk):
        self.here, self.mine, self.twins, self.sums, self.landed = here, mine, twins, sums, landed
        self.sems, self.chunk = (core_send, core_recv, x_send, x_recv), chunk

    def columns(self, k):
        return pl.ds(k * self.chunk, self.chunk)

    def across(self, g, k, far):
        here, f = self.here, 1 if far else 0
        part = (1 - here.x if far else here.x) * 2 + 1 - here.c
        return pltpu.make_async_remote_copy(
            src_ref=self.mine[g].at[part, :, self.columns(k)], dst_ref=self.twins[g].at[f, :, self.columns(k)],
            send_sem=self.sems[0].at[f, g, k], recv_sem=self.sems[1].at[f, g, k],
            device_id=here.device[CORE], device_id_type=MESH,
        )

    def beyond(self, g, k):
        return pltpu.make_async_remote_copy(
            src_ref=self.sums[g].at[:, self.columns(k)], dst_ref=self.landed[g].at[:, self.columns(k)],
            send_sem=self.sems[2].at[g, k], recv_sem=self.sems[3].at[g, k],
            device_id=self.here.device[XX], device_id_type=MESH,
        )

    def send(self, k):
        for far in (True, False):
            for g in range(len(self.mine)):
                self.across(g, k, far).start()

    def forward(self, k):
        here, cols = self.here, slice(k * self.chunk, (k + 1) * self.chunk)
        for g, mine in enumerate(self.mine):
            self.across(g, k, True).wait_recv()
            part = (1 - here.x) * 2 + here.c
            self.sums[g][:, cols] = (
                mine[part, :, cols].astype(jnp.float32) + self.twins[g][1, :, cols].astype(jnp.float32)
            ).astype(jnp.bfloat16)
            self.beyond(g, k).start()

    def collect(self, g, k):
        here, cols = self.here, slice(k * self.chunk, (k + 1) * self.chunk)
        self.across(g, k, False).wait_recv()
        self.beyond(g, k).wait_recv()
        return (
            self.mine[g][here.x * 2 + here.c, :, cols].astype(jnp.float32) + self.twins[g][0, :, cols].astype(jnp.float32)
            + self.landed[g][:, cols].astype(jnp.float32)
        ).astype(jnp.bfloat16)

    def finish(self, chunks):
        for g in range(len(self.mine)):
            for k in range(chunks):
                self.across(g, k, True).wait_send()
                self.across(g, k, False).wait_send()
                self.beyond(g, k).wait_send()


class Pace:
    def __init__(self, steps, every):
        self.steps, self.every, self.owed = steps, every, 0.0

    def spend(self, time):
        self.owed += time
        while self.owed >= self.every:
            self.owed -= self.every
            next(self.steps, None)


def pair_grads(bounds_ref, causal, q, k, v, g, between):
    dq = dk = dv = None
    for keep in halves(q.shape[1]):
        p = pair_scores(bounds_ref, q, k, keep, causal)
        dp = dot_nt(jnp.where(keep, g, 0), v)
        ds = (p * (dp - jnp.sum(p * dp, axis=1, keepdims=True))).astype(jnp.bfloat16)
        a = jnp.dot(ds, k, preferred_element_type=jnp.float32)
        b = dot_tt(ds, q)
        e = dot_tt(p.astype(jnp.bfloat16), g)
        if dq is None:
            dq, dk, dv = a, b, e
        else:
            dq, dk, dv = jnp.where(keep, a, dq), jnp.where(keep, b, dk), jnp.where(keep, e, dv)
        between()
    return [(r * s).astype(jnp.bfloat16) for r, s in ((dq, 0.125), (dk, 0.125), (dv, 1.0))]


def middle_body(nz, units, slots, depth, *refs):
    (bounds, second_low, grad_second, cross_mix, cross_query, cross_keys, cross_values, two_low, first, text_part,
     proj_part, attended, gain) = refs[:13]
    weights, feed = refs[13:19], refs[19:21]
    placed = refs[21:27]
    text_grad, grad_first, grad_attended, dgain, dbias, sums = refs[27:33]
    held, (weight_sem, mixed, first_low, grad_ck, grad_cv, twin_k, twin_v, sum_k, sum_v, land_k, land_v) = refs[33:39], refs[39:50]
    share_sems, stage, stage_sem, scatter = refs[50:54], refs[54], refs[55], refs[56:]
    here = Place(nz)
    loads = [pltpu.make_async_copy(w, h, weight_sem.at[i]) for i, (w, h) in enumerate(zip(weights, held))]
    for cp in loads:
        cp.start()
    c_out, c_query, c_key, c_value, w_text, w_out = held
    steps = scatter_steps(here, units, slots, depth, feed, *scatter)
    low = jnp.bfloat16
    width = second_low.shape[1]
    rows = text_part.shape[0] // 4
    mine = pl.ds(pl.multiple_of((here.x * 2 + here.c) * rows, rows), rows)
    tiles = [slice(i, i + 256) for i in range(0, width, 256)]
    share = Share(here, (grad_ck, grad_cv), (twin_k, twin_v), (sum_k, sum_v), (land_k, land_v), *share_sems, width // 2)

    pace = Pace(steps, 42.0 / (len(slots) + depth))
    spend = pace.spend

    def stored(i):
        src = stage.at[i % 3, pl.ds(0, placed[i].shape[0])]
        return pltpu.make_async_copy(src, placed[i], stage_sem.at[i])

    next(steps)
    loads[0].wait()
    for n in tiles:
        mixed[:, n] = dot_nt(second_low[...], c_out[n, :]).astype(low)
        spend(0.4)
    for n in tiles:
        stage[0, n, :] = dot_tt(cross_mix[:, n], second_low[...]).astype(low)
        spend(0.55)
    stored(0).start()
    pairs = width // 128
    for i in range(pairs):
        n = slice(i * 128, i * 128 + 128)
        dq, dk, dv = pair_grads(bounds, False, cross_query[:, n], cross_keys[:, n], cross_values[:, n], mixed[:, n], lambda: spend(0.72))
        mixed[:, n] = dq
        grad_ck[:, :, n] = dk.reshape(4, rows, 128)
        grad_cv[:, :, n] = dv.reshape(4, rows, 128)
        if i == pairs // 2 - 1:
            share.send(0)
    share.send(1)
    share.forward(0)
    loads[1].wait()
    for n in tiles:
        grad_first[:, n] = dot_nt(mixed[...], c_query[n, :])
        spend(0.4)
    share.forward(1)
    dv, dg, db = norm_grads(first[...], gain[...], grad_first[...])
    dgain[...] = dg
    dbias[...] = db
    dv = grad_second[...] + dv
    grad_first[...] = dv
    first_low[...] = dv.astype(low)
    spend(2.0)
    loads[5].wait()
    for n in tiles:
        grad_attended[:, n] = dot_nt(first_low[...], w_out[n, :]).astype(low)
        spend(0.4)
    for n in tiles:
        stage[1, n, :] = dot_tt(two_low[:, n], mixed[...]).astype(low)
        spend(0.55)
    stored(1).start()
    for n in tiles:
        stage[2, n, :] = dot_tt(attended[:, n], first_low[...]).astype(low)
        spend(0.55)
    stored(2).start()
    ck = jnp.concatenate([share.collect(0, k) for k in range(2)], axis=1)
    cv = jnp.concatenate([share.collect(1, k) for k in range(2)], axis=1)
    for i in (2, 3, 4):
        loads[i].wait()
    stored(0).wait()
    stored(1).wait()
    for n in tiles:
        stage[0, n, :] = dot_tt(proj_part[mine, n], ck).astype(low)
        stage[1, n, :] = dot_tt(proj_part[mine, n], cv).astype(low)
        spend(0.7)
    stored(3).start()
    stored(4).start()
    proj = []
    for n in tiles:
        proj.append((dot_nt(ck, c_key[n, :]) + dot_nt(cv, c_value[n, :])).astype(low))
        spend(0.5)
    proj = jnp.concatenate(proj, axis=1)
    stored(2).wait()
    for i in range(0, text_part.shape[1], 256):
        n = slice(i, i + 256)
        stage[2, n, :] = dot_tt(text_part[mine, n], proj).astype(low)
        text_grad[:, n] = dot_nt(proj, w_text[n, :])
        spend(0.7)
    stored(5).start()
    for _ in steps:
        pass
    share.finish(2)
    for i in (3, 4, 5):
        stored(i).wait()
    total = scatter[0]
    for u in range(len(units)):
        sums[u] = total[u, here.z, here.y, here.x].astype(jnp.float32)


def middle_back(bounds, near, weights, feed, units, perms, nz, depth=3):
    slots = make_schedule(perms, nz, lag=depth + 1)
    second_low, text_part = near[0], near[8]
    width, rows, text_width = second_low.shape[1], text_part.shape[0] // 4, text_part.shape[1]
    low, wide = jnp.bfloat16, jnp.float32
    square = jax.ShapeDtypeStruct((width, width), low)
    outs = [square] * 5 + [jax.ShapeDtypeStruct((text_width, width), low)]
    outs += [jax.ShapeDtypeStruct((rows, text_width), wide), jax.ShapeDtypeStruct(second_low.shape, wide)]
    outs += [jax.ShapeDtypeStruct(second_low.shape, low)] + [jax.ShapeDtypeStruct((1, width), wide)] * 2
    outs += [jax.ShapeDtypeStruct((len(units),) + unit_shape(units), wide)]
    vmem, any_ = pl.BlockSpec(memory_space=pltpu.VMEM), pl.BlockSpec(memory_space=pl.ANY)
    part = pltpu.VMEM((rows, width), low)
    return pl.pallas_call(
        functools.partial(middle_body, nz, units, slots, depth),
        out_shape=outs,
        in_specs=[pl.BlockSpec(memory_space=pltpu.SMEM)] + [vmem] * len(near) + [any_] * 8,
        out_specs=[any_] * 6 + [vmem] * (len(outs) - 6),
        scratch_shapes=[pltpu.VMEM(w.shape, low) for w in weights]
        + [pltpu.SemaphoreType.DMA((6,)), pltpu.VMEM(second_low.shape, low), pltpu.VMEM(second_low.shape, low)]
        + [pltpu.VMEM((4, rows, width), low)] * 2 + [pltpu.VMEM((2, rows, width), low)] * 2 + [part] * 4
        + [pltpu.SemaphoreType.DMA((2, 2, 2))] * 2 + [pltpu.SemaphoreType.DMA((2, 2))] * 2
        + [pltpu.VMEM((3, width, width), low), pltpu.SemaphoreType.DMA((6,))]
        + scatter_scratch(units, slots, nz),
        compiler_params=pltpu.CompilerParams(collective_id=5, has_side_effects=True, vmem_limit_bytes=VMEM_LIMIT),
        name="middle_back",
    )(bounds, *near, *weights, *feed)


class Gather:
    def __init__(self, here, units, slots, depth, given, held, outs, rows_out, sems):
        self.here, self.units, self.slots, self.depth = here, units, slots, depth
        self.outs, self.rows_out = outs, rows_out
        self.ins, self.rows_in = held[:-1], held[-1]
        (self.send_sem, self.recv_sem, self.core_send, self.core_recv, self.local_sem, self.rows_send,
         self.rows_recv) = sems
        self.last = {}
        for t, slot in enumerate(slots):
            for u, axis, j, fy, fx in slot.values():
                self.last[dict(z=(u, fy, fx), y=(u, 1, fx), x=(u, fy, 1))[axis]] = t
        self.done = -1
        self.loads = [pltpu.make_async_copy(given[g], held[g], self.local_sem.at[g]) for g in range(len(held))]
        self.steps = self.run()

    def piece(self, u, p):
        g, r0, rn, c0, cn = self.units[u]
        return self.outs[g].at[p[0], p[1], p[2], self.here.c, pl.ds(r0, rn), pl.ds(c0, cn)]

    def corner(self, u, fy, fx, which):
        g, r0, rn, c0, cn = self.units[u]
        here = self.here
        return self.outs[g].at[
            :, 1 - here.y if fy else here.y, 1 - here.x if fx else here.x, which, pl.ds(r0, rn), pl.ds(c0, cn)
        ]

    def remote(self, u, way, t, p, mine):
        ref = self.piece(u, p)
        g, r0, rn, c0, cn = self.units[u]
        return pltpu.make_async_remote_copy(
            src_ref=self.ins[g].at[pl.ds(r0, rn), pl.ds(c0, cn)] if mine else ref, dst_ref=ref,
            send_sem=self.send_sem.at[way, t], recv_sem=self.recv_sem.at[way, t],
            device_id=self.here.device[way], device_id_type=MESH,
        )

    def across(self, u, fy, fx):
        ref = self.corner(u, fy, fx, self.here.c)
        i = fy * 2 + fx
        return pltpu.make_async_remote_copy(
            src_ref=ref, dst_ref=ref, send_sem=self.core_send.at[u, i], recv_sem=self.core_recv.at[u, i],
            device_id=self.here.device[CORE], device_id_type=MESH,
        )

    def rows_over(self, src, dst, way, i):
        return pltpu.make_async_remote_copy(
            src_ref=src, dst_ref=dst, send_sem=self.rows_send.at[i], recv_sem=self.rows_recv.at[i],
            device_id=self.here.device[way], device_id_type=MESH,
        )

    def run(self):
        here, slots, depth, n = self.here, self.slots, self.depth, len(self.outs)
        z, y, x, c = here.z, here.y, here.x, here.c
        own = [pltpu.make_async_copy(self.ins[g], self.outs[g].at[z, y, x, c], self.local_sem.at[g]) for g in range(n)]
        own.append(pltpu.make_async_copy(self.rows_in, self.rows_out.at[x, c], self.local_sem.at[n]))
        for cp in self.loads:
            cp.start()
        here.greet()
        for cp in self.loads:
            cp.wait()
        for cp in own:
            cp.start()
        beside = self.rows_out.at[1 - x, c]
        self.rows_moves = [
            self.rows_over(self.rows_in, self.rows_out.at[x, c], XX, 0),
            self.rows_over(self.rows_in, self.rows_out.at[x, c], CORE, 1),
            self.rows_over(beside, beside, CORE, 2),
        ]
        self.rows_moves[0].start()
        self.rows_moves[1].start()
        for t in range(len(slots) + depth):
            if t < len(slots):
                for axis, (u, _, j, fy, fx) in slots[t].items():
                    for way, cond, p in here.gather_moves(axis, j, fy, fx)[0]:
                        when(cond, lambda u=u, way=way, p=p: self.remote(u, way, t, p, (j, fy, fx) == (0, 0, 0)).start())
            if t == depth - 1:
                for cp in own:
                    cp.wait()
            if t == 6:
                pltpu.make_async_copy(beside, beside, self.rows_recv.at[0]).wait()
                self.rows_moves[2].start()
            if t >= depth:
                for axis, (u, _, j, fy, fx) in slots[t - depth].items():
                    for way, cond, p in here.gather_moves(axis, j, fy, fx)[1]:
                        def got(u=u, way=way, p=p):
                            ref = self.piece(u, p)
                            pltpu.make_async_copy(ref, ref, self.recv_sem.at[way, t - depth]).wait()
                        when(cond, got)
                for key in sorted(self.last):
                    if self.last[key] == t - depth:
                        self.across(*key).start()
            self.done = t
            yield t
        for t, slot in enumerate(slots):
            for axis, (u, _, j, fy, fx) in slot.items():
                for way, cond, p in here.gather_moves(axis, j, fy, fx)[0]:
                    when(cond, lambda u=u, way=way, p=p: self.remote(u, way, t, p, (j, fy, fx) == (0, 0, 0)).wait_send())
        for u, fy, fx in sorted(self.last):
            self.across(u, fy, fx).wait_send()
        for cp in self.rows_moves:
            cp.wait_send()

    def advance(self, t):
        while self.done < min(t, len(self.slots) + self.depth - 1):
            next(self.steps)

    def frames(self):
        here = self.here
        self.advance(8)
        for i, ref in ((1, self.rows_out.at[here.x, 1 - here.c]), (2, self.rows_out.at[1 - here.x, 1 - here.c])):
            pltpu.make_async_copy(ref, ref, self.rows_recv.at[i]).wait()

    def arrived(self, u):
        self.advance(max(t for key, t in self.last.items() if key[0] == u) + self.depth + 1)
        for fy in range(2):
            for fx in range(2):
                ref = self.corner(u, fy, fx, 1 - self.here.c)
                pltpu.make_async_copy(ref, ref, self.core_recv.at[u, fy * 2 + fx]).wait()


def ahead_body(nz, units, slots, depth, every, *refs):
    bounds, frames, text, cot = refs[:4]
    given = refs[4:16]
    full, rows_out, dw_up, dw_down = refs[16:27], refs[27], refs[28], refs[29]
    (gains, own_low, q_out, k_out, v_out, attended, first, two_low, cross_query, cross_keys, cross_values, cross_mix,
     proj, block_out, grad_second, second_low, dgain, dbias) = refs[30:48]
    held, sems = refs[48:60], refs[60:67]
    (near, near_sem, down, down_sem, up, up_sem, rows_all, rows_sem, normed, grad_act, three_low, second, fed, grad_three,
     stage_down, stage_up, stage_sem) = refs[67:]
    here = Place(nz)
    low, wide = jnp.bfloat16, jnp.float32
    width, count = cot.shape[1], frames.shape[0]
    per = held[0].shape[0]
    gather = Gather(here, units, slots, depth, given, held, full, rows_out, sems)
    pace = Pace(gather.steps, every)
    spend = pace.spend
    tiles = [slice(i, i + 256) for i in range(0, width, 256)]
    depth_slots = near.shape[0]
    loads = {}

    def fetch(u):
        gather.arrived(u)
        slot = u % depth_slots
        loads[u] = pltpu.make_async_copy(full[units[u][0]], near.at[slot], near_sem.at[slot])
        loads[u].start()

    def weight(u, n):
        return near[u % depth_slots, :, :, :, :, :, n].reshape(width, -1)

    def apply(a, u, write, cost):
        if u > 0:
            loads[u].wait()
        for n in tiles:
            write(n, jnp.dot(a[...], weight(u, n), preferred_element_type=wide))
            spend(cost)

    def norm(v, i):
        xh, _ = norm_parts(v)
        return xh * gains[8 + i:9 + i] + gains[9 + i:10 + i]

    def put(ref):
        def write(n, r):
            ref[:, n] = r.astype(low)
        return write

    gather.frames()
    rows_load = pltpu.make_async_copy(rows_out, rows_all, rows_sem)
    rows_load.start()
    fetch(0)
    rows_load.wait()
    loads[0].wait()
    lane = lax.broadcasted_iota(jnp.int32, (128, width), 1)
    spread = jnp.where(lax.broadcasted_iota(jnp.int32, (128, width), 0) == lane % per, 1.0, 0.0).astype(low)
    corner = near[0, :, :, :, :, 16:32, 0:128].astype(wide).reshape(-1, 128).astype(low)
    wider = jnp.dot(corner, spread, preferred_element_type=wide)
    row = lax.broadcasted_iota(jnp.int32, wider.shape, 0)
    wider = jnp.where(row // 16 == lax.broadcasted_iota(jnp.int32, wider.shape, 1) // per, wider, 0.0)
    gains[...] = jnp.sum(wider.reshape(-1, 16, width), axis=0)
    spend(1.5)
    for i in range(2):
        for j in range(2):
            part = i * 2 + j
            normed[part * count:(part + 1) * count] = norm(rows_all[i, j].astype(wide), 0).astype(low)
            spend(0.7)
    own_low[...] = norm(frames[...].astype(wide), 0).astype(low)
    spend(0.7)
    apply(text, 0, put(proj), 0.4)
    fetch(1)
    fetch(2)
    apply(normed, 1, put(k_out), 0.8)
    fetch(3)
    apply(normed, 2, put(v_out), 0.8)
    fetch(4)
    apply(own_low, 3, put(q_out), 0.4)
    fetch(5)
    for i in range(0, width, 128):
        n = slice(i, i + 128)
        out = None
        for keep in halves(128):
            p = pair_scores((bounds[0], bounds[1]), q_out[:, n], k_out[:, n], keep, True).astype(low)
            o = jnp.dot(p, v_out[:, n], preferred_element_type=wide)
            out = o if out is None else jnp.where(keep, o, out)
            spend(0.65)
        attended[:, n] = out.astype(low)
    apply(proj, 4, put(cross_keys), 0.4)
    fetch(6)
    apply(proj, 5, put(cross_values), 0.4)
    fetch(7)

    def add_first(n, r):
        first[:, n] = frames[:, n].astype(wide) + r

    apply(attended, 6, add_first, 0.4)
    two_low[...] = norm(first[...], 2).astype(low)
    spend(0.7)
    fetch(8)
    apply(two_low, 7, put(cross_query), 0.4)
    for i in range(0, width, 128):
        n = slice(i, i + 128)
        out = None
        for keep in halves(128):
            p = pair_scores((bounds[2],), cross_query[:, n], cross_keys[:, n], keep, False).astype(low)
            o = jnp.dot(p, cross_values[:, n], preferred_element_type=wide)
            out = o if out is None else jnp.where(keep, o, out)
            spend(0.35)
        cross_mix[:, n] = out.astype(low)

    def add_second(n, r):
        second[:, n] = first[:, n] + r

    apply(cross_mix, 8, add_second, 0.4)
    three_low[...] = norm(second[...], 4).astype(low)
    grad_three[...] = jnp.zeros_like(grad_three)
    fed[...] = jnp.zeros_like(fed)
    spend(0.7)
    n_near = 9
    n_down = len([u for u in units if u[0] == 10])
    n_up = len(units) - n_near - n_down
    for u in range(n_near, n_near + n_down):
        gather.arrived(u)
    load = pltpu.make_async_copy(full[10], down, down_sem)
    load.start()
    ups = []

    def fetch_up(k):
        gather.arrived(n_near + n_down + k)
        slot = k % 2
        ups.append(pltpu.make_async_copy(
            full[9].at[:, :, :, :, :, pl.ds(k * width, width)], up.at[slot], up_sem.at[slot]))
        ups[k].start()

    fetch_up(0)
    load.wait()

    def down_rows(at):
        s = at // down.shape[4]
        return down[s // 8, s // 4 % 2, s // 2 % 2].reshape(-1, width)

    for at in range(0, n_up * width, 256):
        grad_act[:, at:at + 256] = dot_nt(cot[...], down_rows(at))
        spend(0.4)
    def stored(k):
        slot = k % 2
        rows = pl.ds(k * width, width)
        return [
            pltpu.make_async_copy(stage_down.at[slot], dw_down.at[rows], stage_sem.at[0, slot]),
            pltpu.make_async_copy(stage_up.at[slot], dw_up.at[:, rows], stage_sem.at[1, slot]),
        ]

    for k in range(n_up):
        slot = k % 2
        ups[k].wait()
        if k >= 2:
            for cp in stored(k - 2):
                cp.wait()
        for n in tiles:
            at = slice(k * width + n.start, k * width + n.stop)
            w = up[slot, :, :, :, :, :, n].reshape(width, -1)
            hidden = jnp.dot(three_low[...], w, preferred_element_type=wide)
            phi = 0.5 + 0.5 * lax.erf(hidden * (0.5 ** 0.5))
            act = (hidden * phi).astype(low)
            slope = phi + hidden * jnp.exp(-0.5 * hidden * hidden) * 0.3989422804014327
            grad = (grad_act[:, at] * slope).astype(low)
            spend(0.9)
            fed[...] += jnp.dot(act, down_rows(at.start), preferred_element_type=wide)
            grad_three[...] += dot_nt(grad, w)
            spend(0.8)
            stage_down[slot, n, :] = dot_tt(act, cot[...]).astype(low)
            stage_up[slot, :, n] = dot_tt(three_low[...], grad).astype(low)
            spend(1.1)
            if n.start == 256 and k + 1 < n_up:
                fetch_up(k + 1)
        for cp in stored(k):
            cp.start()
    for _ in gather.steps:
        pass
    block_out[...] = (second[...] + fed[...]).astype(low)
    dv, dgain[...], dbias[...] = norm_grads(second[...], gains[12:13], grad_three[...])
    dv = cot[...].astype(wide) + dv
    grad_second[...] = dv
    second_low[...] = dv.astype(low)
    for k in range(max(n_up - 2, 0), n_up):
        for cp in stored(k):
            cp.wait()


def ahead(bounds, frames, text, cot, arrays, units, perms, nz, depth=5, every=2.4):
    slots = make_schedule(perms, nz, lag=depth + 1, slope=0.5)
    low, wide = jnp.bfloat16, jnp.float32
    count, width = frames.shape
    tokens, rows = text.shape[0], arrays[0].shape[0]
    hidden = arrays[9].shape[1]
    any_, vmem = pl.BlockSpec(memory_space=pl.ANY), pl.BlockSpec(memory_space=pltpu.VMEM)

    def like(n, kind):
        return jax.ShapeDtypeStruct((n, width), kind)

    given = [*arrays, frames]
    outs = [jax.ShapeDtypeStruct((nz, 2, 2, 2) + a.shape, a.dtype) for a in arrays]
    outs += [jax.ShapeDtypeStruct((2, 2) + frames.shape, low), jax.ShapeDtypeStruct((width, hidden), low), like(hidden, low)]
    far = len(outs)
    outs += [like(16, wide), like(count, low), like(count, low), like(4 * count, low), like(4 * count, low), like(count, low)]
    outs += [like(count, wide), like(count, low), like(count, low), like(tokens, low), like(tokens, low), like(count, low)]
    outs += [like(tokens, low), like(count, low), like(count, wide), like(count, low), like(1, wide), like(1, wide)]
    block = (nz, 2, 2, 2, rows, width)
    dma = pltpu.SemaphoreType.DMA
    return pl.pallas_call(
        functools.partial(ahead_body, nz, units, slots, depth, every),
        out_shape=outs,
        in_specs=[pl.BlockSpec(memory_space=pltpu.SMEM)] + [vmem] * 3 + [any_] * len(given),
        out_specs=[any_] * far + [vmem] * (len(outs) - far),
        scratch_shapes=[pltpu.VMEM(a.shape, a.dtype) for a in given]
        + [dma((4, len(slots)))] * 2 + [dma((len(units), 4))] * 2 + [dma((len(given),)), dma((3,)), dma((3,))]
        + [pltpu.VMEM((5,) + block, low), dma((5,))]
        + [pltpu.VMEM((nz, 2, 2, 2) + arrays[10].shape, low), dma]
        + [pltpu.VMEM((2,) + block, low), dma((2,))]
        + [pltpu.VMEM((2, 2) + frames.shape, low), dma, pltpu.VMEM((4 * count, width), low)]
        + [pltpu.VMEM((count, hidden), wide), pltpu.VMEM((count, width), low)] + [pltpu.VMEM((count, width), wide)] * 3
        + [pltpu.VMEM((2, width, width), low)] * 2 + [dma((2, 2))],
        compiler_params=pltpu.CompilerParams(collective_id=1, has_side_effects=True, vmem_limit_bytes=VMEM_LIMIT),
        name="ahead",
    )(bounds, frames, text, cot, *given)


def last_body(nz, units, slots, depth, firsts, *refs):
    bounds, query, keys, values, grad_mix, normed, frames, grad_first, gain, others = refs[:10]
    weights, text, early = refs[10:13], refs[13], refs[14:19]
    frames_grad, sums = refs[19:21]
    held, (weight_sem, grad_q, grad_k, grad_v, twin_k, twin_v, sum_k, sum_v, land_k, land_v) = refs[21:24], refs[24:34]
    share_sems, late, grad_norm, scatter = refs[34:38], refs[38], refs[39], refs[40:]
    here = Place(nz)
    low, wide = jnp.bfloat16, jnp.float32
    count, width = normed.shape
    loads = [pltpu.make_async_copy(w, h, weight_sem.at[i]) for i, (w, h) in enumerate(zip(weights, held))]
    loads.append(pltpu.make_async_copy(text, late.at[3], weight_sem.at[3]))
    for cp in loads:
        cp.start()
    ins = [late.at[0], late.at[1], late.at[2], early[0], early[1], early[2], early[3], early[4], late.at[3]]
    late_units = [u for u, unit in enumerate(units) if unit[0][0] in (0, 1, 2, 8)]
    unit_of = {units[u][0][0]: u for u in late_units}
    steps = scatter_steps(here, units, slots, depth, ins, *scatter, late=late_units)
    begin_unit = next(steps)
    done = [-1]

    waiting = list(late_units)
    every = 40.0 / max(firsts[u] for u in late_units)

    def spend(time, pace=Pace(None, every)):
        pace.owed += time
        while pace.owed >= pace.every and done[0] + 1 < min(firsts[u] for u in waiting):
            pace.owed -= pace.every
            done[0] += 1
            next(steps)

    def begin(g):
        begin_unit(unit_of[g])
        waiting.remove(unit_of[g])

    share = Share(here, (grad_k, grad_v), (twin_k, twin_v), (sum_k, sum_v), (land_k, land_v), *share_sems, width // 2)
    tiles = [slice(i, i + 256) for i in range(0, width, 256)]
    pairs = width // 128
    next(steps)
    done[0] += 1
    for i in range(pairs):
        n = slice(i * 128, i * 128 + 128)
        dq, dk, dv = pair_grads(bounds, True, query[:, n], keys[:, n], values[:, n], grad_mix[:, n], lambda: spend(1.0))
        grad_q[:, n] = dq
        grad_k[:, :, n] = dk.reshape(4, count, 128)
        grad_v[:, :, n] = dv.reshape(4, count, 128)
        if i == pairs // 2 - 1:
            share.send(0)
        if i == pairs // 2 + 1:
            share.forward(0)
    share.send(1)

    def outer(slot, rows):
        height = width // nz
        for i in range(nz):
            r = dot_tt(normed[:, i * height:(i + 1) * height], rows).astype(low)
            late[slot, i] = r.reshape(late.shape[2:])
            spend(0.55)

    def back(slot, rows, first):
        for n in tiles:
            r = dot_nt(rows, held[slot][n, :])
            grad_norm[:, n] = r if first else grad_norm[:, n] + r
            spend(0.4)

    outer(0, grad_q[...])
    begin(0)
    share.forward(1)
    for cp in loads:
        cp.wait()
    back(0, grad_q[...], True)
    for g in range(2):
        rows = jnp.concatenate([share.collect(g, k) for k in range(2)], axis=1)
        outer(1 + g, rows)
        begin(1 + g)
        back(1 + g, rows, False)
    dv, dgain, dbias = norm_grads(frames[...].astype(wide), gain[...], grad_norm[...])
    frames_grad[...] = (grad_first[...] + dv).astype(low)
    per = width // (nz * 8)
    both = jnp.concatenate([dgain, dbias, others[...], jnp.zeros((2, width), wide)], axis=0)
    both = jnp.broadcast_to(both[None], (nz * 8, 8, width)).reshape(-1, width)
    row = lax.broadcasted_iota(jnp.int32, both.shape, 0)
    both = jnp.where(row // 8 == lax.broadcasted_iota(jnp.int32, both.shape, 1) // per, both, 0.0).astype(low)
    lane = lax.broadcasted_iota(jnp.int32, (128, width), 1)
    spread = jnp.where(lax.broadcasted_iota(jnp.int32, (128, width), 0) == lane % per, 1.0, 0.0).astype(low)
    block = late[3, :, :, :, :, 16:32, 0:128].astype(wide).reshape(-1, 16, 128)
    tail = dot_nt(both, spread).reshape(-1, 8, 128)
    block = jnp.concatenate([block[:, :8], tail], axis=1)
    late[3, :, :, :, :, 16:32, 0:128] = block.astype(low).reshape(nz, 2, 2, 2, 16, 128)
    begin(8)
    for _ in steps:
        pass
    share.finish(2)
    total = scatter[0]
    for u in range(len(units)):
        sums[u] = total[u, here.z, here.y, here.x].astype(wide)


def last_back(bounds, near, weights, text, early, units, perms, nz, depth=5):
    slots = make_schedule(perms, nz, lag=depth + 1, window=3)
    firsts = {}
    for t, slot in enumerate(slots[::-1]):
        for op in slot.values():
            firsts.setdefault(op[0], t)
    count, width = near[4].shape
    low, wide = jnp.bfloat16, jnp.float32
    vmem, any_ = pl.BlockSpec(memory_space=pltpu.VMEM), pl.BlockSpec(memory_space=pl.ANY)
    part = pltpu.VMEM((count, width), low)
    outs = [jax.ShapeDtypeStruct((count, width), low), jax.ShapeDtypeStruct((len(units),) + unit_shape(units), wide)]
    return pl.pallas_call(
        functools.partial(last_body, nz, units, slots, depth, firsts),
        out_shape=outs,
        in_specs=[pl.BlockSpec(memory_space=pltpu.SMEM)] + [vmem] * len(near) + [any_] * 9,
        out_specs=[vmem] * 2,
        scratch_shapes=[pltpu.VMEM(w.shape, low) for w in weights]
        + [pltpu.SemaphoreType.DMA((4,)), part]
        + [pltpu.VMEM((4, count, width), low)] * 2 + [pltpu.VMEM((2, count, width), low)] * 2 + [part] * 4
        + [pltpu.SemaphoreType.DMA((2, 2, 2))] * 2 + [pltpu.SemaphoreType.DMA((2, 2))] * 2
        + [pltpu.VMEM((4,) + text.shape, low), pltpu.VMEM((count, width), wide)]
        + scatter_scratch(units, slots, nz),
        compiler_params=pltpu.CompilerParams(collective_id=2, has_side_effects=True, vmem_limit_bytes=VMEM_LIMIT),
        name="last_back",
    )(bounds, *near, *weights, text, *early)


eps_norm = 1e-05


def layer_norm(values_in, gain_vec, shift_vec):
    centre = values_in - jnp.mean(values_in, axis=-1, keepdims=True)
    spread = jnp.mean(centre * centre, axis=-1, keepdims=True)
    return centre * lax.rsqrt(spread + eps_norm) * gain_vec + shift_vec


def gelu_exact(values_in):
    return jax.nn.gelu(values_in, approximate=False)


def project(left, right):
    return jnp.einsum("gti,ij->gtj", left, right, preferred_element_type=jnp.float32)


def project_back(left, right):
    return jnp.einsum("gtj,ij->gti", left, right, preferred_element_type=jnp.float32)


def outer_sum(left, right):
    return jnp.einsum("gti,gtj->ij", left, right, preferred_element_type=jnp.float32)


class Params(NamedTuple):
    w_query: jax.Array
    w_key: jax.Array
    w_value: jax.Array
    w_out: jax.Array
    c_query: jax.Array
    c_key: jax.Array
    c_value: jax.Array
    c_out: jax.Array
    w_text: jax.Array
    w_up: jax.Array
    w_down: jax.Array
    gain_attn: jax.Array
    bias_attn: jax.Array
    gain_cross: jax.Array
    bias_cross: jax.Array
    gain_feed: jax.Array
    bias_feed: jax.Array


BLOCKS, GAINS = 11, 6


def all_axes():
    return ("dp", "seq")


def fits(own, frames, text):
    rows, width = own.w_query.shape
    return (
        lax.axis_size("seq") == 4 and lax.axis_size("dp") % 2 == 0 and rows == 32 and width % 128 == 0
        and own.w_text.shape[0] % 8 == 0 and own.w_text.shape[0] + 8 == rows
        and own.w_up.shape[0] == rows and own.w_up.shape[1] % width == 0
        and own.w_down.shape == (own.w_up.shape[1] // width * rows, width) and own.w_down.shape[0] == 128
        and width == rows * lax.axis_size("dp") * 4
        and frames.shape[0] == 1 and frames.shape[1] % 32 == 0 and text.shape[0] == 1 and text.shape[1] % 128 == 0
    )


class PlainWires:
    def gather(self, own, frames):
        full = Params(*[lax.all_gather(v, all_axes(), axis=0, tiled=True) for v in own])
        return full, lax.all_gather(frames, "seq", axis=1, tiled=True)

    def scatter(self, grads):
        return Params(*[lax.psum_scatter(v, all_axes(), scatter_dimension=0, tiled=True) for v in grads])

    def share(self, arrays, number):
        return [lax.psum_scatter(a, "seq", scatter_dimension=1, tiled=True) for a in arrays]


def attention(causal, bounds, q, k, v):
    return attend(causal, bounds[0], q[0], k[0], v[0])[None]


def attention_back(causal, bounds, *operands):
    return [r[None] for r in attend_grads(causal, bounds[0], *[a[0] for a in operands])]


def plain_layer(own, frames, cotangent, text_states, frame_start, prompt_len):
    low = jnp.bfloat16
    wires = PlainWires()
    full, all_frames = wires.gather(own, frames)
    wide = [v.astype(jnp.float32) for v in full[BLOCKS:]]
    frames_f = frames.astype(jnp.float32)
    frame_count = frames.shape[1]
    normed, norm_one_back = jax.vjp(layer_norm, frames_f, wide[0], wide[1])
    normed_low = normed.astype(low)
    normed_all = layer_norm(all_frames.astype(jnp.float32), wide[0], wide[1]).astype(low)
    query_rows = project(normed_low, full.w_query).astype(low)
    key_all = project(normed_all, full.w_key).astype(low)
    value_all = project(normed_all, full.w_value).astype(low)
    rank = lax.axis_index("seq")
    self_bounds = jnp.stack([jnp.full_like(frame_start, rank * frame_count), frame_start], axis=1)
    attended = attention(True, self_bounds, query_rows, key_all, value_all)
    first = frames_f + project(attended, full.w_out)
    text_count = text_states.shape[1]
    quarter = text_count // lax.axis_size("seq")
    text_start = rank * quarter
    text_part = lax.dynamic_slice_in_dim(text_states, text_start, quarter, 1)
    proj_all = project(text_states, full.w_text).astype(low)
    cross_keys = project(proj_all, full.c_key).astype(low)
    cross_values = project(proj_all, full.c_value).astype(low)
    proj_part = lax.dynamic_slice_in_dim(proj_all, text_start, quarter, 1)
    normed_two, norm_two_back = jax.vjp(layer_norm, first, wide[2], wide[3])
    normed_two_low = normed_two.astype(low)
    cross_query = project(normed_two_low, full.c_query).astype(low)
    cross_bounds = jnp.stack([prompt_len, prompt_len], axis=1)
    cross_mix = attention(False, cross_bounds, cross_query, cross_keys, cross_values)
    second = first + project(cross_mix, full.c_out)
    normed_three, norm_three_back = jax.vjp(layer_norm, second, wide[4], wide[5])
    three_low = normed_three.astype(low)
    hidden = project(three_low, full.w_up)
    activated, gelu_back = jax.vjp(gelu_exact, hidden)
    act_low = activated.astype(low)
    block_out = (second + project(act_low, full.w_down)).astype(low)
    grad_act = project_back(cotangent, full.w_down)
    dw_down = outer_sum(act_low, cotangent)
    grad_hidden = gelu_back(grad_act)[0].astype(low)
    dw_up = outer_sum(three_low, grad_hidden)
    grad_second_ln, dgain_feed, dbias_feed = norm_three_back(project_back(grad_hidden, full.w_up))
    grad_second = cotangent.astype(jnp.float32) + grad_second_ln
    second_low = grad_second.astype(low)
    dc_out = outer_sum(cross_mix, second_low)
    grad_cross_mix = project_back(second_low, full.c_out).astype(low)
    cq_low, grad_ck, grad_cv = attention_back(
        False, cross_bounds, cross_query, cross_keys, cross_values, grad_cross_mix
    )
    ck_low, cv_low = wires.share([grad_ck, grad_cv], 3)
    dc_key = outer_sum(proj_part, ck_low)
    dc_value = outer_sum(proj_part, cv_low)
    grad_proj = (project_back(ck_low, full.c_key) + project_back(cv_low, full.c_value)).astype(low)
    dw_text = outer_sum(text_part, grad_proj)
    text_grad = project_back(grad_proj, full.w_text)
    dc_query = outer_sum(normed_two_low, cq_low)
    grad_first_ln, dgain_cross, dbias_cross = norm_two_back(project_back(cq_low, full.c_query))
    grad_first = grad_second + grad_first_ln
    first_low = grad_first.astype(low)
    dw_out = outer_sum(attended, first_low)
    grad_attended = project_back(first_low, full.w_out).astype(low)
    q_low, grad_k_all, grad_v_all = attention_back(
        True, self_bounds, query_rows, key_all, value_all, grad_attended
    )
    k_low, v_low = wires.share([grad_k_all, grad_v_all], 4)
    dw_query = outer_sum(normed_low, q_low)
    dw_key = outer_sum(normed_low, k_low)
    dw_value = outer_sum(normed_low, v_low)
    grad_normed = (
        project_back(q_low, full.w_query) + project_back(k_low, full.w_key) + project_back(v_low, full.w_value)
    )
    grad_frames_ln, dgain_attn, dbias_attn = norm_one_back(grad_normed)
    frames_grad = (grad_first + grad_frames_ln).astype(low)
    sums = wires.scatter(
        Params(
            dw_query, dw_key, dw_value, dw_out, dc_query, dc_key, dc_value, dc_out, dw_text, dw_up, dw_down,
            dgain_attn, dbias_attn, dgain_cross, dbias_cross, dgain_feed, dbias_feed,
        )
    )
    return (block_out, frames_grad, text_grad, *sums)


NEAR_ORDERS = ("zxy", "zyx", "zxy", "zxy", "zyx", "zxy", "xyz", "zxy", "zyx")
LATE_ORDERS = ("zyx", "yxz", "yxz", "zyx", "zxy", "zyx", "zyx", "xyz")
LAST_ORDERS = ("zyx", "zxy", "zyx", "xyz", "zxy", "zyx", "xzy", "zxy", "xyz")
FEED_ORDERS = ("zyx", "zxy", "zyx", "yxz", "zxy", "zyx", "xyz", "zxy")


def cycle(orders, n):
    return [orders[i % len(orders)] for i in range(n)]


def fast_layer(own, frames, cotangent, text_states, frame_start, prompt_len):
    low, wide = jnp.bfloat16, jnp.float32
    nz = lax.axis_size("dp") // 2
    shards = nz * 8
    rows, width = own.w_query.shape
    text_rows = own.w_text.shape[0]
    count = frames.shape[1]
    rank = lax.axis_index("seq")
    up, down = own.w_up.shape[1] // width, own.w_down.shape[0] // rows
    near_units = [(g, 0, rows, 0, width) for g in range(9)]
    up_units = [(9, 0, rows, k * width, width) for k in range(up)]
    down_units = [(10, k * rows, rows, 0, width) for k in range(down)]
    units = [near_units[i] for i in (8, 1, 2, 0, 5, 6, 3, 4, 7)] + down_units + up_units
    gains = jnp.stack(own[BLOCKS:])
    gains = jnp.pad(gains, ((0, rows - text_rows - GAINS), (0, width - gains.shape[1])))
    arrays = list(own[:BLOCKS])
    arrays[8] = jnp.concatenate([own.w_text, gains], axis=0)
    tokens = text_states.shape[1]
    text = jnp.pad(text_states.reshape((tokens, shards, text_rows)), ((0, 0), (0, 0), (0, rows - text_rows))).reshape((tokens, width))
    bounds = jnp.concatenate([jnp.full_like(frame_start, rank * count), frame_start, prompt_len])
    cot = cotangent[0]
    orders = cycle(NEAR_ORDERS, 9) + cycle(LATE_ORDERS, up + down)
    outs = ahead(bounds, frames[0], text, cot, arrays, units, orders, nz)
    full, (_, dw_up, dw_down) = [f.reshape((-1, f.shape[-1])) for f in outs[:BLOCKS]], outs[BLOCKS:BLOCKS + 3]
    (gains, normed_low, query_rows, key_all, value_all, attended, first, two_low, cross_query, cross_keys, cross_values,
     cross_mix, proj, block_out, grad_second, second_low, dgain_feed, dbias_feed) = outs[BLOCKS + 3:]
    quarter = tokens // 4
    near = [second_low, grad_second, cross_mix, cross_query, cross_keys, cross_values, two_low, first, text, proj, attended, gains[10:11]]
    weights = [full[i] for i in (7, 4, 5, 6, 8, 3)]
    lead = (nz, 2, 2, 2)
    feed = [v.reshape(lead + (-1, v.shape[-1])) for v in (dw_up, dw_down)]
    feed_units = [((g - 9, *rest),) for g, *rest in up_units + down_units]
    (dc_out, dc_query, dw_out, dc_key, dc_value, dw_text, text_grad, grad_first, grad_attended, dgain_cross, dbias_cross,
     feed_sums) = middle_back(bounds[2:], near, weights, feed, feed_units, cycle(FEED_ORDERS, up + down), nz)
    others = jnp.concatenate([dgain_cross, dbias_cross, dgain_feed, dbias_feed], axis=0)
    last = [query_rows, key_all, value_all, grad_attended, normed_low, frames[0], grad_first, gains[8:9], others]
    text_block, *early = [v.reshape(lead + (rows, width)) for v in (dw_text, dw_out, dc_query, dc_key, dc_value, dc_out)]
    last_units = [(near_units[i],) for i in (8, 2, 1, 0, 7, 6, 5, 4, 3)]
    frames_grad, sums = last_back(bounds[:2], last, full[:3], text_block, early, last_units, LAST_ORDERS, nz)
    shapes = [(rows, width)] * 9 + [own.w_up.shape, own.w_down.shape]
    feed_units = [((g + 9, *rest),) for ((g, *rest),) in feed_units]
    *blocks, tail = deliver((sums, feed_sums), (last_units, feed_units), text_rows, shapes)
    text_grad = text_grad.reshape((quarter, shards, rows))[:, :, :text_rows].reshape((1, quarter, -1))
    return (block_out[None], frames_grad[None], text_grad, *blocks, *[tail[i, : width // shards] for i in range(GAINS)])


def on_device(frames, cotangent, text_states, frame_start, prompt_len, *params):
    own = Params(*params)
    layer = fast_layer if fits(own, frames, text_states) else plain_layer
    return layer(own, frames, cotangent, text_states, frame_start, prompt_len)


def solution(mesh):
    both = P(all_axes(), None)
    rows, vector = P(*all_axes(), None), P(all_axes())
    item, whole = P("dp"), P("dp", None, None)
    return jax.shard_map(
        on_device,
        mesh=mesh,
        in_specs=(rows, rows, whole, item, item) + (both,) * BLOCKS + (vector,) * GAINS,
        out_specs=(rows,) * 3 + (both,) * BLOCKS + (vector,) * GAINS,
        check_vma=False,
    )
```

```python
import functools
from typing import NamedTuple
import jax
import jax.numpy as jnp
from jax import lax
from jax.experimental import pallas as pl
from jax.experimental.pallas import tpu as pltpu
from jax.sharding import PartitionSpec as P

MESH = pl.DeviceIdType.MESH

LAG = 2
VMEM_LIMIT = 60 * 1024 * 1024

def unit_ops(perm, nz):
    rank = {a: i for i, a in enumerate(perm)}
    ops = {}

    def source(j, fy, fx):
        differs = [a for a, f in (("z", j > 0), ("y", fy), ("x", fx)) if f]
        if not differs:
            return None
        last = max(differs, key=lambda a: rank[a])
        if last == "z":
            return ("z", j - 1, fy, fx)
        if last == "y":
            return ("y", j, 0, fx)
        return ("x", j, fy, 0)

    for j in range(nz):
        for fy in range(2):
            for fx in range(2):
                for axis in "zyx":
                    flags = {"z": j > 0, "y": fy, "x": fx}
                    if axis != "z" and flags[axis]:
                        continue
                    if any(flags[a] and rank[a] > rank[axis] for a in "zyx" if a != axis):
                        continue
                    if axis == "z" and j == nz - 1:
                        continue
                    ops[(axis, j, fy, fx)] = source(j, fy, fx)
    return ops

def make_schedule(perms, nz, lag=LAG, window=None, slope=0.0):
    ops = {}
    for u, perm in enumerate(perms):
        for key, dep in unit_ops(perm, nz).items():
            ops[(u,) + key] = None if dep is None else (u,) + dep
    children = {}
    for op, dep in ops.items():
        children.setdefault(dep, []).append(op)
    height = {}

    def tall(op):
        if op not in height:
            height[op] = 1 + max([tall(c) for c in children.get(op, [])], default=0)
        return height[op]

    for op in ops:
        tall(op)
    done, slots, left = {}, [], set(ops)
    while left:
        t = len(slots)
        slot = {}
        for axis in "zyx":
            ready = [op for op in left if op[1] == axis and (ops[op] is None or (ops[op] in done and done[ops[op]] + lag <= t))]
            if ready:
                slot[axis] = min(ready, key=lambda op: (op[0] // window if window else 0, slope * op[0] - height[op], op[0], op))
        for axis, op in slot.items():
            done[op] = t
            left.discard(op)
        slots.append(slot)
    return slots

def nth_table(nz):
    rows = []
    for z in range(nz):
        offs = sorted((p - z for p in range(nz)), key=lambda o: (abs(o), o if z % 2 else -o))
        rows.append([z + o for o in offs])
    return rows

def pick(values, z):
    out = 0
    for i, v in enumerate(values):
        out = out + v * jnp.where(z == i, 1, 0)
    return out

UP, DOWN, YY, XX, CORE = range(5)
WAYS_OF = dict(z=(UP, DOWN), y=(YY,), x=(XX,))

class Place:
    def __init__(self, nz):
        d, s = lax.axis_index("dp"), lax.axis_index("seq")
        self.nz = nz
        self.z, self.y, self.x, self.c = d // 2, d % 2, s // 2, s % 2
        z, y, x, c = self.z, self.y, self.x, self.c
        self.device = [
            ((z + 1) * 2 + y, x * 2 + c),
            ((z - 1) * 2 + y, x * 2 + c),
            (z * 2 + 1 - y, x * 2 + c),
            (z * 2 + y, (1 - x) * 2 + c),
            (z * 2 + y, x * 2 + 1 - c),
        ]
        self.nth = [[row[j] for row in nth_table(nz)] for j in range(nz)]

    def greet(self):
        barrier = pltpu.get_barrier_semaphore()
        has_up, has_down = self.z + 1 < self.nz, self.z > 0
        for way in range(5):
            def hello(way=way):
                pl.semaphore_signal(barrier, inc=1, device_id=self.device[way], device_id_type=MESH)
            if way < YY:
                pl.when(has_up if way == UP else has_down)(hello)
            else:
                hello()
        edge = jnp.where(self.z == 0, 1, 0) + jnp.where(self.z == self.nz - 1, 1, 0)
        pl.semaphore_wait(barrier, 5 - edge)

    def gather_moves(self, axis, j, fy, fx):
        z, y, x, nz = self.z, self.y, self.x, self.nz
        py, px = (1 - y if fy else y), (1 - x if fx else x)
        if axis == "z":
            out = [(UP, (z - j >= 0) & (z + 1 < nz), (z - j, py, px)), (DOWN, (z + j < nz) & (z > 0), (z + j, py, px))]
            come = [(UP, z - 1 - j >= 0, (z - 1 - j, py, px)), (DOWN, z + 1 + j < nz, (z + 1 + j, py, px))]
        else:
            pz = pick(self.nth[j], z)
            there = (pz, 1 - y, px) if axis == "y" else (pz, py, 1 - x)
            way = YY if axis == "y" else XX
            out = [(way, None, (pz, py, px))]
            come = [(way, None, there)]
        return out, come

def when(cond, fn):
    if cond is None:
        fn()
    else:
        pl.when(cond)(fn)

BACK = (DOWN, UP, YY, XX)


def scatter_steps(here, units, slots, depth, ins, total, twin, landed, send_sem, recv_sem, core_send, core_recv, local_sem, late=()):
    nz = here.nz
    z, y, x, c = here.z, here.y, here.x, here.c
    steps = slots[::-1]
    numbers, order = {}, []
    for t, slot in enumerate(steps):
        for axis, op in slot.items():
            for way in WAYS_OF[axis]:
                numbers[way, t] = len(numbers)
            if op[0] not in order:
                order.append(op[0])

    def plane(u, b, which):
        g, r0, rn, c0, cn = units[u][b]
        return ins[g].at[:, :, :, which, pl.ds(r0, rn), pl.ds(c0, cn)]

    def rows_of(buffer, u, b):
        rn = units[u][b][2]
        return buffer.at[u, :, :, :, pl.ds(b * rn, rn)]

    def local(u, b):
        return pltpu.make_async_copy(plane(u, b, c), rows_of(total, u, b), local_sem.at[u, b])

    def across(u, b):
        return pltpu.make_async_remote_copy(
            src_ref=plane(u, b, 1 - c), dst_ref=rows_of(twin, u, b), send_sem=core_send.at[u, b],
            recv_sem=core_recv.at[u, b], device_id=here.device[CORE], device_id_type=MESH,
        )

    def remote(u, way, t, p):
        i = numbers[way, t]
        return pltpu.make_async_remote_copy(
            src_ref=total.at[u, p[0], p[1], p[2]], dst_ref=landed.at[i], send_sem=send_sem.at[i], recv_sem=recv_sem.at[i],
            device_id=here.device[BACK[way]], device_id_type=MESH,
        )

    ahead = 3
    blocks = range(len(units[0]))
    early = [u for u in order if u not in late]

    def begin_unit(u):
        for b in blocks:
            local(u, b).start()
            across(u, b).start()

    for u in early[:ahead]:
        for b in blocks:
            local(u, b).start()
    here.greet()
    for u in early[:ahead]:
        for b in blocks:
            across(u, b).start()
    if late:
        yield begin_unit

    def join(u):
        later = early.index(u) + ahead if u in early else len(early)
        if later < len(early):
            begin_unit(early[later])
        for b in blocks:
            local(u, b).wait()
            across(u, b).wait_recv()

        @pl.loop(0, nz)
        def _(a):
            for b in range(2):
                for e in range(2):
                    total[u, a, b, e] = (
                        total[u, a, b, e].astype(jnp.float32) + twin[u, a, b, e].astype(jnp.float32)
                    ).astype(jnp.bfloat16)

    joined = set()
    for t in range(len(steps) + depth):
        if t < len(steps):
            for axis, (u, _, j, fy, fx) in steps[t].items():
                if u not in joined:
                    joined.add(u)
                    join(u)
                for way, cond, p in here.gather_moves(axis, j, fy, fx)[1]:
                    when(cond, lambda u=u, way=way, p=p: remote(u, way, t, p).start())
        if t >= depth:
            s = t - depth
            for axis, (u, _, j, fy, fx) in steps[s].items():
                for way, cond, p in here.gather_moves(axis, j, fy, fx)[0]:
                    def add(u=u, way=way, p=p):
                        i = numbers[way, s]
                        pltpu.make_async_copy(landed.at[i], landed.at[i], recv_sem.at[i]).wait()
                        total[u, p[0], p[1], p[2]] = (
                            total[u, p[0], p[1], p[2]].astype(jnp.float32) + landed[i].astype(jnp.float32)
                        ).astype(jnp.bfloat16)
                    when(cond, add)
        yield t
    for t, slot in enumerate(steps):
        for axis, (u, _, j, fy, fx) in slot.items():
            for way, cond, p in here.gather_moves(axis, j, fy, fx)[1]:
                when(cond, lambda u=u, way=way, p=p: remote(u, way, t, p).wait_send())
    for u in order:
        for b in blocks:
            across(u, b).wait_send()


def unit_shape(units):
    return sum(block[2] for block in units[0]), units[0][0][4]


def scatter_scratch(units, slots, nz):
    rows, columns = unit_shape(units)
    count = sum(len(WAYS_OF[axis]) for slot in slots for axis in slot)
    plane = (len(units), nz, 2, 2, rows, columns)
    return [
        pltpu.VMEM(plane, jnp.bfloat16),
        pltpu.VMEM(plane, jnp.bfloat16),
        pltpu.VMEM((count, rows, columns), jnp.bfloat16),
        pltpu.SemaphoreType.DMA((count,)),
        pltpu.SemaphoreType.DMA((count,)),
        pltpu.SemaphoreType.DMA((len(units), len(units[0]))),
        pltpu.SemaphoreType.DMA((len(units), len(units[0]))),
        pltpu.SemaphoreType.DMA((len(units), len(units[0]))),
    ]


def deliver_body(parts, text_rows, n, *refs):
    ins, outs = refs[:n], refs[n:]
    for sums, units in zip(ins, parts):
        for u, unit in enumerate(units):
            for b, (g, r0, rn, c0, cn) in enumerate(unit):
                if g == 8:
                    outs[g][...] = sums[u, :text_rows]
                    outs[-1][...] = sums[u, text_rows:text_rows + 8]
                else:
                    outs[g][r0:r0 + rn, c0:c0 + cn] = sums[u, b * rn:(b + 1) * rn]


def deliver(sums, parts, text_rows, shapes):
    shapes = [(text_rows,) + s[1:] if g == 8 else s for g, s in enumerate(shapes)] + [(8, sums[0].shape[2])]
    return pl.pallas_call(
        functools.partial(deliver_body, parts, text_rows, len(sums)),
        out_shape=[jax.ShapeDtypeStruct(s, jnp.float32) for s in shapes],
        compiler_params=pltpu.CompilerParams(vmem_limit_bytes=16 * 1024 * 1024),
        name="deliver",
    )(*sums)


def pair_scores(bounds_ref, q, k, keep, causal):
    s = lax.dot_general(jnp.where(keep, q, 0), k, (((1,), (1,)), ((), ())), preferred_element_type=jnp.float32)
    col = lax.broadcasted_iota(jnp.int32, s.shape, 1)
    if causal:
        row = lax.broadcasted_iota(jnp.int32, s.shape, 0) + bounds_ref[0]
        seen = (col <= row) & ((col >= bounds_ref[1]) | (col == row))
    else:
        seen = col < bounds_ref[0]
    s = jnp.where(seen, s * 0.125, -1e30)
    e = jnp.exp(s - jnp.max(s, axis=1, keepdims=True))
    return e * (1.0 / jnp.sum(e, axis=1, keepdims=True))


def halves(width):
    lane = lax.broadcasted_iota(jnp.int32, (1, width), 1)
    return [(lane >= 64 * h) & (lane < 64 * h + 64) for h in range(width // 64)]


def attend_body(causal, bounds_ref, q_ref, k_ref, v_ref, out_ref):
    q, k, v = q_ref[...], k_ref[...], v_ref[...]
    out = None
    for keep in halves(q.shape[1]):
        p = pair_scores(bounds_ref, q, k, keep, causal)
        o = jnp.dot(p.astype(jnp.bfloat16), v, preferred_element_type=jnp.float32)
        out = o if out is None else jnp.where(keep, o, out)
    out_ref[...] = out.astype(jnp.bfloat16)


def attend_back_body(causal, bounds_ref, q_ref, k_ref, v_ref, g_ref, dq_ref, dk_ref, dv_ref):
    q, k, v, g = q_ref[...], k_ref[...], v_ref[...], g_ref[...]
    dq = dk = dv = None
    for keep in halves(q.shape[1]):
        p = pair_scores(bounds_ref, q, k, keep, causal)
        dp = lax.dot_general(jnp.where(keep, g, 0), v, (((1,), (1,)), ((), ())), preferred_element_type=jnp.float32)
        ds = (p * (dp - jnp.sum(p * dp, axis=1, keepdims=True))).astype(jnp.bfloat16)
        a = jnp.dot(ds, k, preferred_element_type=jnp.float32)
        b = lax.dot_general(ds, q, (((0,), (0,)), ((), ())), preferred_element_type=jnp.float32)
        e = lax.dot_general(p.astype(jnp.bfloat16), g, (((0,), (0,)), ((), ())), preferred_element_type=jnp.float32)
        if dq is None:
            dq, dk, dv = a, b, e
        else:
            dq, dk, dv = jnp.where(keep, a, dq), jnp.where(keep, b, dk), jnp.where(keep, e, dv)
    dq_ref[...] = (dq * 0.125).astype(jnp.bfloat16)
    dk_ref[...] = (dk * 0.125).astype(jnp.bfloat16)
    dv_ref[...] = dv.astype(jnp.bfloat16)


def attend_call(body, causal, bounds, operands, n_out_rows):
    width = operands[0].shape[1]
    spec = [pl.BlockSpec((a.shape[0], 128), lambda i: (0, i)) for a in operands]
    return pl.pallas_call(
        functools.partial(body, causal),
        grid=(width // 128,),
        out_shape=[jax.ShapeDtypeStruct((r, width), jnp.bfloat16) for r in n_out_rows],
        in_specs=[pl.BlockSpec(memory_space=pltpu.SMEM)] + spec,
        out_specs=[pl.BlockSpec((r, 128), lambda i: (0, i)) for r in n_out_rows],
        compiler_params=pltpu.CompilerParams(vmem_limit_bytes=32 * 1024 * 1024),
        name=("self_" if causal else "cross_") + body.__name__,
    )(bounds, *operands)


def attend(causal, bounds, q, k, v):
    return attend_call(attend_body, causal, bounds, (q, k, v), [q.shape[0]])[0]


def attend_grads(causal, bounds, q, k, v, g):
    return attend_call(attend_back_body, causal, bounds, (q, k, v, g), [q.shape[0], k.shape[0], k.shape[0]])


def dot_tt(a, b):
    return lax.dot_general(a, b, (((0,), (0,)), ((), ())), preferred_element_type=jnp.float32)


def dot_nt(a, b):
    return lax.dot_general(a, b, (((1,), (1,)), ((), ())), preferred_element_type=jnp.float32)


def norm_parts(v):
    centre = v - jnp.mean(v, axis=1, keepdims=True)
    rate = lax.rsqrt(jnp.mean(centre * centre, axis=1, keepdims=True) + eps_norm)
    return centre * rate, rate


def norm_grads(v, gain, h):
    xh, rate = norm_parts(v)
    hg = h * gain
    dv = (hg - jnp.mean(hg, axis=1, keepdims=True) - xh * jnp.mean(hg * xh, axis=1, keepdims=True)) * rate
    return dv, jnp.sum(h * xh, axis=0, keepdims=True), jnp.sum(h, axis=0, keepdims=True)


class Share:
    def __init__(self, here, mine, twins, sums, landed, core_send, core_recv, x_send, x_recv, chunk):
        self.here, self.mine, self.twins, self.sums, self.landed = here, mine, twins, sums, landed
        self.sems, self.chunk = (core_send, core_recv, x_send, x_recv), chunk

    def columns(self, k):
        return pl.ds(k * self.chunk, self.chunk)

    def across(self, g, k, far):
        here, f = self.here, 1 if far else 0
        part = (1 - here.x if far else here.x) * 2 + 1 - here.c
        return pltpu.make_async_remote_copy(
            src_ref=self.mine[g].at[part, :, self.columns(k)], dst_ref=self.twins[g].at[f, :, self.columns(k)],
            send_sem=self.sems[0].at[f, g, k], recv_sem=self.sems[1].at[f, g, k],
            device_id=here.device[CORE], device_id_type=MESH,
        )

    def beyond(self, g, k):
        return pltpu.make_async_remote_copy(
            src_ref=self.sums[g].at[:, self.columns(k)], dst_ref=self.landed[g].at[:, self.columns(k)],
            send_sem=self.sems[2].at[g, k], recv_sem=self.sems[3].at[g, k],
            device_id=self.here.device[XX], device_id_type=MESH,
        )

    def send(self, k):
        for far in (True, False):
            for g in range(len(self.mine)):
                self.across(g, k, far).start()

    def forward(self, k):
        here, cols = self.here, slice(k * self.chunk, (k + 1) * self.chunk)
        for g, mine in enumerate(self.mine):
            self.across(g, k, True).wait_recv()
            part = (1 - here.x) * 2 + here.c
            self.sums[g][:, cols] = (
                mine[part, :, cols].astype(jnp.float32) + self.twins[g][1, :, cols].astype(jnp.float32)
            ).astype(jnp.bfloat16)
            self.beyond(g, k).start()

    def collect(self, g, k):
        here, cols = self.here, slice(k * self.chunk, (k + 1) * self.chunk)
        self.across(g, k, False).wait_recv()
        self.beyond(g, k).wait_recv()
        return (
            self.mine[g][here.x * 2 + here.c, :, cols].astype(jnp.float32) + self.twins[g][0, :, cols].astype(jnp.float32)
            + self.landed[g][:, cols].astype(jnp.float32)
        ).astype(jnp.bfloat16)

    def finish(self, chunks):
        for g in range(len(self.mine)):
            for k in range(chunks):
                self.across(g, k, True).wait_send()
                self.across(g, k, False).wait_send()
                self.beyond(g, k).wait_send()


class Pace:
    def __init__(self, steps, every):
        self.steps, self.every, self.owed = steps, every, 0.0

    def spend(self, time):
        self.owed += time
        while self.owed >= self.every:
            self.owed -= self.every
            next(self.steps, None)


def pair_grads(bounds_ref, causal, q, k, v, g, between):
    dq = dk = dv = None
    for keep in halves(q.shape[1]):
        p = pair_scores(bounds_ref, q, k, keep, causal)
        dp = dot_nt(jnp.where(keep, g, 0), v)
        ds = (p * (dp - jnp.sum(p * dp, axis=1, keepdims=True))).astype(jnp.bfloat16)
        a = jnp.dot(ds, k, preferred_element_type=jnp.float32)
        b = dot_tt(ds, q)
        e = dot_tt(p.astype(jnp.bfloat16), g)
        if dq is None:
            dq, dk, dv = a, b, e
        else:
            dq, dk, dv = jnp.where(keep, a, dq), jnp.where(keep, b, dk), jnp.where(keep, e, dv)
        between()
    return [(r * s).astype(jnp.bfloat16) for r, s in ((dq, 0.125), (dk, 0.125), (dv, 1.0))]


def middle_body(nz, units, slots, depth, *refs):
    (bounds, second_low, grad_second, cross_mix, cross_query, cross_keys, cross_values, two_low, first, text_part,
     proj_part, attended, gain) = refs[:13]
    weights, feed = refs[13:19], refs[19:21]
    placed = refs[21:27]
    text_grad, grad_first, grad_attended, dgain, dbias, sums = refs[27:33]
    held, (weight_sem, mixed, first_low, grad_ck, grad_cv, twin_k, twin_v, sum_k, sum_v, land_k, land_v) = refs[33:39], refs[39:50]
    share_sems, stage, stage_sem, scatter = refs[50:54], refs[54], refs[55], refs[56:]
    here = Place(nz)
    loads = [pltpu.make_async_copy(w, h, weight_sem.at[i]) for i, (w, h) in enumerate(zip(weights, held))]
    for cp in loads:
        cp.start()
    c_out, c_query, c_key, c_value, w_text, w_out = held
    steps = scatter_steps(here, units, slots, depth, feed, *scatter)
    low = jnp.bfloat16
    width = second_low.shape[1]
    rows = text_part.shape[0] // 4
    mine = pl.ds(pl.multiple_of((here.x * 2 + here.c) * rows, rows), rows)
    tiles = [slice(i, i + 256) for i in range(0, width, 256)]
    share = Share(here, (grad_ck, grad_cv), (twin_k, twin_v), (sum_k, sum_v), (land_k, land_v), *share_sems, width // 2)

    pace = Pace(steps, 42.0 / (len(slots) + depth))
    spend = pace.spend

    def stored(i):
        src = stage.at[i % 3, pl.ds(0, placed[i].shape[0])]
        return pltpu.make_async_copy(src, placed[i], stage_sem.at[i])

    next(steps)
    loads[0].wait()
    for n in tiles:
        mixed[:, n] = dot_nt(second_low[...], c_out[n, :]).astype(low)
        spend(0.4)
    for n in tiles:
        stage[0, n, :] = dot_tt(cross_mix[:, n], second_low[...]).astype(low)
        spend(0.55)
    stored(0).start()
    pairs = width // 128
    for i in range(pairs):
        n = slice(i * 128, i * 128 + 128)
        dq, dk, dv = pair_grads(bounds, False, cross_query[:, n], cross_keys[:, n], cross_values[:, n], mixed[:, n], lambda: spend(0.72))
        mixed[:, n] = dq
        grad_ck[:, :, n] = dk.reshape(4, rows, 128)
        grad_cv[:, :, n] = dv.reshape(4, rows, 128)
        if i == pairs // 2 - 1:
            share.send(0)
    share.send(1)
    share.forward(0)
    loads[1].wait()
    for n in tiles:
        grad_first[:, n] = dot_nt(mixed[...], c_query[n, :])
        spend(0.4)
    share.forward(1)
    dv, dg, db = norm_grads(first[...], gain[...], grad_first[...])
    dgain[...] = dg
    dbias[...] = db
    dv = grad_second[...] + dv
    grad_first[...] = dv
    first_low[...] = dv.astype(low)
    spend(2.0)
    loads[5].wait()
    for n in tiles:
        grad_attended[:, n] = dot_nt(first_low[...], w_out[n, :]).astype(low)
        spend(0.4)
    for n in tiles:
        stage[1, n, :] = dot_tt(two_low[:, n], mixed[...]).astype(low)
        spend(0.55)
    stored(1).start()
    for n in tiles:
        stage[2, n, :] = dot_tt(attended[:, n], first_low[...]).astype(low)
        spend(0.55)
    stored(2).start()
    ck = jnp.concatenate([share.collect(0, k) for k in range(2)], axis=1)
    cv = jnp.concatenate([share.collect(1, k) for k in range(2)], axis=1)
    for i in (2, 3, 4):
        loads[i].wait()
    stored(0).wait()
    stored(1).wait()
    for n in tiles:
        stage[0, n, :] = dot_tt(proj_part[mine, n], ck).astype(low)
        stage[1, n, :] = dot_tt(proj_part[mine, n], cv).astype(low)
        spend(0.7)
    stored(3).start()
    stored(4).start()
    proj = []
    for n in tiles:
        proj.append((dot_nt(ck, c_key[n, :]) + dot_nt(cv, c_value[n, :])).astype(low))
        spend(0.5)
    proj = jnp.concatenate(proj, axis=1)
    stored(2).wait()
    for i in range(0, text_part.shape[1], 256):
        n = slice(i, i + 256)
        stage[2, n, :] = dot_tt(text_part[mine, n], proj).astype(low)
        text_grad[:, n] = dot_nt(proj, w_text[n, :])
        spend(0.7)
    stored(5).start()
    for _ in steps:
        pass
    share.finish(2)
    for i in (3, 4, 5):
        stored(i).wait()
    total = scatter[0]
    for u in range(len(units)):
        sums[u] = total[u, here.z, here.y, here.x].astype(jnp.float32)


def middle_back(bounds, near, weights, feed, units, perms, nz, depth=3):
    slots = make_schedule(perms, nz, lag=depth + 1)
    second_low, text_part = near[0], near[8]
    width, rows, text_width = second_low.shape[1], text_part.shape[0] // 4, text_part.shape[1]
    low, wide = jnp.bfloat16, jnp.float32
    square = jax.ShapeDtypeStruct((width, width), low)
    outs = [square] * 5 + [jax.ShapeDtypeStruct((text_width, width), low)]
    outs += [jax.ShapeDtypeStruct((rows, text_width), wide), jax.ShapeDtypeStruct(second_low.shape, wide)]
    outs += [jax.ShapeDtypeStruct(second_low.shape, low)] + [jax.ShapeDtypeStruct((1, width), wide)] * 2
    outs += [jax.ShapeDtypeStruct((len(units),) + unit_shape(units), wide)]
    vmem, any_ = pl.BlockSpec(memory_space=pltpu.VMEM), pl.BlockSpec(memory_space=pl.ANY)
    part = pltpu.VMEM((rows, width), low)
    return pl.pallas_call(
        functools.partial(middle_body, nz, units, slots, depth),
        out_shape=outs,
        in_specs=[pl.BlockSpec(memory_space=pltpu.SMEM)] + [vmem] * len(near) + [any_] * 8,
        out_specs=[any_] * 6 + [vmem] * (len(outs) - 6),
        scratch_shapes=[pltpu.VMEM(w.shape, low) for w in weights]
        + [pltpu.SemaphoreType.DMA((6,)), pltpu.VMEM(second_low.shape, low), pltpu.VMEM(second_low.shape, low)]
        + [pltpu.VMEM((4, rows, width), low)] * 2 + [pltpu.VMEM((2, rows, width), low)] * 2 + [part] * 4
        + [pltpu.SemaphoreType.DMA((2, 2, 2))] * 2 + [pltpu.SemaphoreType.DMA((2, 2))] * 2
        + [pltpu.VMEM((3, width, width), low), pltpu.SemaphoreType.DMA((6,))]
        + scatter_scratch(units, slots, nz),
        compiler_params=pltpu.CompilerParams(collective_id=5, has_side_effects=True, vmem_limit_bytes=VMEM_LIMIT),
        name="middle_back",
    )(bounds, *near, *weights, *feed)


class Gather:
    def __init__(self, here, units, slots, depth, given, held, outs, rows_out, sems):
        self.here, self.units, self.slots, self.depth = here, units, slots, depth
        self.outs, self.rows_out = outs, rows_out
        self.ins, self.rows_in = held[:-1], held[-1]
        (self.send_sem, self.recv_sem, self.core_send, self.core_recv, self.local_sem, self.rows_send,
         self.rows_recv) = sems
        self.last = {}
        for t, slot in enumerate(slots):
            for u, axis, j, fy, fx in slot.values():
                self.last[dict(z=(u, fy, fx), y=(u, 1, fx), x=(u, fy, 1))[axis]] = t
        self.done = -1
        self.loads = [pltpu.make_async_copy(given[g], held[g], self.local_sem.at[g]) for g in range(len(held))]
        self.steps = self.run()

    def piece(self, u, p):
        g, r0, rn, c0, cn = self.units[u]
        return self.outs[g].at[p[0], p[1], p[2], self.here.c, pl.ds(r0, rn), pl.ds(c0, cn)]

    def corner(self, u, fy, fx, which):
        g, r0, rn, c0, cn = self.units[u]
        here = self.here
        return self.outs[g].at[
            :, 1 - here.y if fy else here.y, 1 - here.x if fx else here.x, which, pl.ds(r0, rn), pl.ds(c0, cn)
        ]

    def remote(self, u, way, t, p, mine):
        ref = self.piece(u, p)
        g, r0, rn, c0, cn = self.units[u]
        return pltpu.make_async_remote_copy(
            src_ref=self.ins[g].at[pl.ds(r0, rn), pl.ds(c0, cn)] if mine else ref, dst_ref=ref,
            send_sem=self.send_sem.at[way, t], recv_sem=self.recv_sem.at[way, t],
            device_id=self.here.device[way], device_id_type=MESH,
        )

    def across(self, u, fy, fx):
        ref = self.corner(u, fy, fx, self.here.c)
        i = fy * 2 + fx
        return pltpu.make_async_remote_copy(
            src_ref=ref, dst_ref=ref, send_sem=self.core_send.at[u, i], recv_sem=self.core_recv.at[u, i],
            device_id=self.here.device[CORE], device_id_type=MESH,
        )

    def rows_over(self, src, dst, way, i):
        return pltpu.make_async_remote_copy(
            src_ref=src, dst_ref=dst, send_sem=self.rows_send.at[i], recv_sem=self.rows_recv.at[i],
            device_id=self.here.device[way], device_id_type=MESH,
        )

    def run(self):
        here, slots, depth, n = self.here, self.slots, self.depth, len(self.outs)
        z, y, x, c = here.z, here.y, here.x, here.c
        own = [pltpu.make_async_copy(self.ins[g], self.outs[g].at[z, y, x, c], self.local_sem.at[g]) for g in range(n)]
        own.append(pltpu.make_async_copy(self.rows_in, self.rows_out.at[x, c], self.local_sem.at[n]))
        for cp in self.loads:
            cp.start()
        here.greet()
        for cp in self.loads:
            cp.wait()
        for cp in own:
            cp.start()
        beside = self.rows_out.at[1 - x, c]
        self.rows_moves = [
            self.rows_over(self.rows_in, self.rows_out.at[x, c], XX, 0),
            self.rows_over(self.rows_in, self.rows_out.at[x, c], CORE, 1),
            self.rows_over(beside, beside, CORE, 2),
        ]
        self.rows_moves[0].start()
        self.rows_moves[1].start()
        for t in range(len(slots) + depth):
            if t < len(slots):
                for axis, (u, _, j, fy, fx) in slots[t].items():
                    for way, cond, p in here.gather_moves(axis, j, fy, fx)[0]:
                        when(cond, lambda u=u, way=way, p=p: self.remote(u, way, t, p, (j, fy, fx) == (0, 0, 0)).start())
            if t == depth - 1:
                for cp in own:
                    cp.wait()
            if t == 6:
                pltpu.make_async_copy(beside, beside, self.rows_recv.at[0]).wait()
                self.rows_moves[2].start()
            if t >= depth:
                for axis, (u, _, j, fy, fx) in slots[t - depth].items():
                    for way, cond, p in here.gather_moves(axis, j, fy, fx)[1]:
                        def got(u=u, way=way, p=p):
                            ref = self.piece(u, p)
                            pltpu.make_async_copy(ref, ref, self.recv_sem.at[way, t - depth]).wait()
                        when(cond, got)
                for key in sorted(self.last):
                    if self.last[key] == t - depth:
                        self.across(*key).start()
            self.done = t
            yield t
        for t, slot in enumerate(slots):
            for axis, (u, _, j, fy, fx) in slot.items():
                for way, cond, p in here.gather_moves(axis, j, fy, fx)[0]:
                    when(cond, lambda u=u, way=way, p=p: self.remote(u, way, t, p, (j, fy, fx) == (0, 0, 0)).wait_send())
        for u, fy, fx in sorted(self.last):
            self.across(u, fy, fx).wait_send()
        for cp in self.rows_moves:
            cp.wait_send()

    def advance(self, t):
        while self.done < min(t, len(self.slots) + self.depth - 1):
            next(self.steps)

    def frames(self):
        here = self.here
        self.advance(8)
        for i, ref in ((1, self.rows_out.at[here.x, 1 - here.c]), (2, self.rows_out.at[1 - here.x, 1 - here.c])):
            pltpu.make_async_copy(ref, ref, self.rows_recv.at[i]).wait()

    def arrived(self, u):
        self.advance(max(t for key, t in self.last.items() if key[0] == u) + self.depth + 1)
        for fy in range(2):
            for fx in range(2):
                ref = self.corner(u, fy, fx, 1 - self.here.c)
                pltpu.make_async_copy(ref, ref, self.core_recv.at[u, fy * 2 + fx]).wait()


def ahead_body(nz, units, slots, depth, every, *refs):
    bounds, frames, text, cot = refs[:4]
    given = refs[4:16]
    full, rows_out, dw_up, dw_down = refs[16:27], refs[27], refs[28], refs[29]
    (gains, own_low, q_out, k_out, v_out, attended, first, two_low, cross_query, cross_keys, cross_values, cross_mix,
     proj, block_out, grad_second, second_low, dgain, dbias) = refs[30:48]
    held, sems = refs[48:60], refs[60:67]
    (near, near_sem, down, down_sem, up, up_sem, rows_all, rows_sem, normed, grad_act, three_low, second, fed, grad_three,
     stage_down, stage_up, stage_sem) = refs[67:]
    here = Place(nz)
    low, wide = jnp.bfloat16, jnp.float32
    width, count = cot.shape[1], frames.shape[0]
    per = held[0].shape[0]
    gather = Gather(here, units, slots, depth, given, held, full, rows_out, sems)
    pace = Pace(gather.steps, every)
    spend = pace.spend
    tiles = [slice(i, i + 256) for i in range(0, width, 256)]
    depth_slots = near.shape[0]
    loads = {}

    def fetch(u):
        gather.arrived(u)
        slot = u % depth_slots
        loads[u] = pltpu.make_async_copy(full[units[u][0]], near.at[slot], near_sem.at[slot])
        loads[u].start()

    def weight(u, n):
        return near[u % depth_slots, :, :, :, :, :, n].reshape(width, -1)

    def apply(a, u, write, cost):
        if u > 0:
            loads[u].wait()
        for n in tiles:
            write(n, jnp.dot(a[...], weight(u, n), preferred_element_type=wide))
            spend(cost)

    def norm(v, i):
        xh, _ = norm_parts(v)
        return xh * gains[8 + i:9 + i] + gains[9 + i:10 + i]

    def put(ref):
        def write(n, r):
            ref[:, n] = r.astype(low)
        return write

    gather.frames()
    rows_load = pltpu.make_async_copy(rows_out, rows_all, rows_sem)
    rows_load.start()
    fetch(0)
    rows_load.wait()
    loads[0].wait()
    lane = lax.broadcasted_iota(jnp.int32, (128, width), 1)
    spread = jnp.where(lax.broadcasted_iota(jnp.int32, (128, width), 0) == lane % per, 1.0, 0.0).astype(low)
    corner = near[0, :, :, :, :, 16:32, 0:128].astype(wide).reshape(-1, 128).astype(low)
    wider = jnp.dot(corner, spread, preferred_element_type=wide)
    row = lax.broadcasted_iota(jnp.int32, wider.shape, 0)
    wider = jnp.where(row // 16 == lax.broadcasted_iota(jnp.int32, wider.shape, 1) // per, wider, 0.0)
    gains[...] = jnp.sum(wider.reshape(-1, 16, width), axis=0)
    spend(1.5)
    for i in range(2):
        for j in range(2):
            part = i * 2 + j
            normed[part * count:(part + 1) * count] = norm(rows_all[i, j].astype(wide), 0).astype(low)
            spend(0.7)
    own_low[...] = norm(frames[...].astype(wide), 0).astype(low)
    spend(0.7)
    apply(text, 0, put(proj), 0.4)
    fetch(1)
    fetch(2)
    apply(normed, 1, put(k_out), 0.8)
    fetch(3)
    apply(normed, 2, put(v_out), 0.8)
    fetch(4)
    apply(own_low, 3, put(q_out), 0.4)
    fetch(5)
    for i in range(0, width, 128):
        n = slice(i, i + 128)
        out = None
        for keep in halves(128):
            p = pair_scores((bounds[0], bounds[1]), q_out[:, n], k_out[:, n], keep, True).astype(low)
            o = jnp.dot(p, v_out[:, n], preferred_element_type=wide)
            out = o if out is None else jnp.where(keep, o, out)
            spend(0.65)
        attended[:, n] = out.astype(low)
    apply(proj, 4, put(cross_keys), 0.4)
    fetch(6)
    apply(proj, 5, put(cross_values), 0.4)
    fetch(7)

    def add_first(n, r):
        first[:, n] = frames[:, n].astype(wide) + r

    apply(attended, 6, add_first, 0.4)
    two_low[...] = norm(first[...], 2).astype(low)
    spend(0.7)
    fetch(8)
    apply(two_low, 7, put(cross_query), 0.4)
    for i in range(0, width, 128):
        n = slice(i, i + 128)
        out = None
        for keep in halves(128):
            p = pair_scores((bounds[2],), cross_query[:, n], cross_keys[:, n], keep, False).astype(low)
            o = jnp.dot(p, cross_values[:, n], preferred_element_type=wide)
            out = o if out is None else jnp.where(keep, o, out)
            spend(0.35)
        cross_mix[:, n] = out.astype(low)

    def add_second(n, r):
        second[:, n] = first[:, n] + r

    apply(cross_mix, 8, add_second, 0.4)
    three_low[...] = norm(second[...], 4).astype(low)
    grad_three[...] = jnp.zeros_like(grad_three)
    fed[...] = jnp.zeros_like(fed)
    spend(0.7)
    n_near = 9
    n_down = len([u for u in units if u[0] == 10])
    n_up = len(units) - n_near - n_down
    for u in range(n_near, n_near + n_down):
        gather.arrived(u)
    load = pltpu.make_async_copy(full[10], down, down_sem)
    load.start()
    ups = []

    def fetch_up(k):
        gather.arrived(n_near + n_down + k)
        slot = k % 2
        ups.append(pltpu.make_async_copy(
            full[9].at[:, :, :, :, :, pl.ds(k * width, width)], up.at[slot], up_sem.at[slot]))
        ups[k].start()

    fetch_up(0)
    load.wait()

    def down_rows(at, n):
        s = at // down.shape[4]
        if n == 4 * down.shape[4]:
            return down[s // 8, s // 4 % 2].reshape(-1, width)
        return down[s // 8, s // 4 % 2, s // 2 % 2].reshape(-1, width)

    for at in range(0, n_up * width, 256):
        grad_act[:, at:at + 256] = dot_nt(cot[...], down_rows(at, 256))
        spend(0.4)
    def stored(k):
        slot = k % 2
        rows = pl.ds(k * width, width)
        return [
            pltpu.make_async_copy(stage_down.at[slot], dw_down.at[rows], stage_sem.at[0, slot]),
            pltpu.make_async_copy(stage_up.at[slot], dw_up.at[:, rows], stage_sem.at[1, slot]),
        ]

    half = width // 2
    for k in range(n_up):
        slot = k % 2
        ups[k].wait()
        if k >= 2:
            for cp in stored(k - 2):
                cp.wait()
        for n in (slice(0, half), slice(half, width)):
            at = slice(k * width + n.start, k * width + n.stop)
            w = up[slot, :, :, :, :, :, n].reshape(width, -1)
            hidden = jnp.dot(three_low[...], w, preferred_element_type=wide)
            phi = 0.5 + 0.5 * lax.erf(hidden * (0.5 ** 0.5))
            act = (hidden * phi).astype(low)
            slope = phi + hidden * jnp.exp(-0.5 * hidden * hidden) * 0.3989422804014327
            grad = (grad_act[:, at] * slope).astype(low)
            spend(1.8)
            fed[...] += jnp.dot(act, down_rows(at.start, half), preferred_element_type=wide)
            grad_three[...] += dot_nt(grad, w)
            spend(1.6)
            stage_down[slot, n, :] = dot_tt(act, cot[...]).astype(low)
            stage_up[slot, :, n] = dot_tt(three_low[...], grad).astype(low)
            spend(2.2)
            if n.start == 0 and k + 1 < n_up:
                fetch_up(k + 1)
        for cp in stored(k):
            cp.start()
    for _ in gather.steps:
        pass
    block_out[...] = (second[...] + fed[...]).astype(low)
    dv, dgain[...], dbias[...] = norm_grads(second[...], gains[12:13], grad_three[...])
    dv = cot[...].astype(wide) + dv
    grad_second[...] = dv
    second_low[...] = dv.astype(low)
    for k in range(max(n_up - 2, 0), n_up):
        for cp in stored(k):
            cp.wait()


def ahead(bounds, frames, text, cot, arrays, units, perms, nz, depth=5, every=2.4):
    slots = make_schedule(perms, nz, lag=depth + 1, slope=0.5)
    low, wide = jnp.bfloat16, jnp.float32
    count, width = frames.shape
    tokens, rows = text.shape[0], arrays[0].shape[0]
    hidden = arrays[9].shape[1]
    any_, vmem = pl.BlockSpec(memory_space=pl.ANY), pl.BlockSpec(memory_space=pltpu.VMEM)

    def like(n, kind):
        return jax.ShapeDtypeStruct((n, width), kind)

    given = [*arrays, frames]
    outs = [jax.ShapeDtypeStruct((nz, 2, 2, 2) + a.shape, a.dtype) for a in arrays]
    outs += [jax.ShapeDtypeStruct((2, 2) + frames.shape, low), jax.ShapeDtypeStruct((width, hidden), low), like(hidden, low)]
    far = len(outs)
    outs += [like(16, wide), like(count, low), like(count, low), like(4 * count, low), like(4 * count, low), like(count, low)]
    outs += [like(count, wide), like(count, low), like(count, low), like(tokens, low), like(tokens, low), like(count, low)]
    outs += [like(tokens, low), like(count, low), like(count, wide), like(count, low), like(1, wide), like(1, wide)]
    block = (nz, 2, 2, 2, rows, width)
    dma = pltpu.SemaphoreType.DMA
    return pl.pallas_call(
        functools.partial(ahead_body, nz, units, slots, depth, every),
        out_shape=outs,
        in_specs=[pl.BlockSpec(memory_space=pltpu.SMEM)] + [vmem] * 3 + [any_] * len(given),
        out_specs=[any_] * far + [vmem] * (len(outs) - far),
        scratch_shapes=[pltpu.VMEM(a.shape, a.dtype) for a in given]
        + [dma((4, len(slots)))] * 2 + [dma((len(units), 4))] * 2 + [dma((len(given),)), dma((3,)), dma((3,))]
        + [pltpu.VMEM((5,) + block, low), dma((5,))]
        + [pltpu.VMEM((nz, 2, 2, 2) + arrays[10].shape, low), dma]
        + [pltpu.VMEM((2,) + block, low), dma((2,))]
        + [pltpu.VMEM((2, 2) + frames.shape, low), dma, pltpu.VMEM((4 * count, width), low)]
        + [pltpu.VMEM((count, hidden), wide), pltpu.VMEM((count, width), low)] + [pltpu.VMEM((count, width), wide)] * 3
        + [pltpu.VMEM((2, width, width), low)] * 2 + [dma((2, 2))],
        compiler_params=pltpu.CompilerParams(collective_id=1, has_side_effects=True, vmem_limit_bytes=VMEM_LIMIT),
        name="ahead",
    )(bounds, frames, text, cot, *given)


def last_body(nz, units, slots, depth, firsts, *refs):
    bounds, query, keys, values, grad_mix, normed, frames, grad_first, gain, others = refs[:10]
    weights, text, early = refs[10:13], refs[13], refs[14:19]
    frames_grad, sums = refs[19:21]
    held, (weight_sem, grad_q, grad_k, grad_v, twin_k, twin_v, sum_k, sum_v, land_k, land_v) = refs[21:24], refs[24:34]
    share_sems, late, grad_norm, scatter = refs[34:38], refs[38], refs[39], refs[40:]
    here = Place(nz)
    low, wide = jnp.bfloat16, jnp.float32
    count, width = normed.shape
    loads = [pltpu.make_async_copy(w, h, weight_sem.at[i]) for i, (w, h) in enumerate(zip(weights, held))]
    loads.append(pltpu.make_async_copy(text, late.at[3], weight_sem.at[3]))
    for cp in loads:
        cp.start()
    ins = [late.at[0], late.at[1], late.at[2], early[0], early[1], early[2], early[3], early[4], late.at[3]]
    late_units = [u for u, unit in enumerate(units) if unit[0][0] in (0, 1, 2, 8)]
    unit_of = {units[u][0][0]: u for u in late_units}
    steps = scatter_steps(here, units, slots, depth, ins, *scatter, late=late_units)
    begin_unit = next(steps)
    done = [-1]

    waiting = list(late_units)
    every = 40.0 / max(firsts[u] for u in late_units)

    def spend(time, pace=Pace(None, every)):
        pace.owed += time
        while pace.owed >= pace.every and done[0] + 1 < min(firsts[u] for u in waiting):
            pace.owed -= pace.every
            done[0] += 1
            next(steps)

    def begin(g):
        begin_unit(unit_of[g])
        waiting.remove(unit_of[g])

    share = Share(here, (grad_k, grad_v), (twin_k, twin_v), (sum_k, sum_v), (land_k, land_v), *share_sems, width // 2)
    tiles = [slice(i, i + 256) for i in range(0, width, 256)]
    pairs = width // 128
    next(steps)
    done[0] += 1
    for i in range(pairs):
        n = slice(i * 128, i * 128 + 128)
        dq, dk, dv = pair_grads(bounds, True, query[:, n], keys[:, n], values[:, n], grad_mix[:, n], lambda: spend(1.0))
        grad_q[:, n] = dq
        grad_k[:, :, n] = dk.reshape(4, count, 128)
        grad_v[:, :, n] = dv.reshape(4, count, 128)
        if i == pairs // 2 - 1:
            share.send(0)
        if i == pairs // 2 + 1:
            share.forward(0)
    share.send(1)

    def outer(slot, rows):
        height = width // nz
        for i in range(nz):
            r = dot_tt(normed[:, i * height:(i + 1) * height], rows).astype(low)
            late[slot, i] = r.reshape(late.shape[2:])
            spend(0.55)

    def back(slot, rows, first):
        for n in tiles:
            r = dot_nt(rows, held[slot][n, :])
            grad_norm[:, n] = r if first else grad_norm[:, n] + r
            spend(0.4)

    outer(0, grad_q[...])
    begin(0)
    share.forward(1)
    for cp in loads:
        cp.wait()
    back(0, grad_q[...], True)
    for g in range(2):
        rows = jnp.concatenate([share.collect(g, k) for k in range(2)], axis=1)
        outer(1 + g, rows)
        begin(1 + g)
        back(1 + g, rows, False)
    dv, dgain, dbias = norm_grads(frames[...].astype(wide), gain[...], grad_norm[...])
    frames_grad[...] = (grad_first[...] + dv).astype(low)
    per = width // (nz * 8)
    both = jnp.concatenate([dgain, dbias, others[...], jnp.zeros((2, width), wide)], axis=0)
    both = jnp.broadcast_to(both[None], (nz * 8, 8, width)).reshape(-1, width)
    row = lax.broadcasted_iota(jnp.int32, both.shape, 0)
    both = jnp.where(row // 8 == lax.broadcasted_iota(jnp.int32, both.shape, 1) // per, both, 0.0).astype(low)
    lane = lax.broadcasted_iota(jnp.int32, (128, width), 1)
    spread = jnp.where(lax.broadcasted_iota(jnp.int32, (128, width), 0) == lane % per, 1.0, 0.0).astype(low)
    block = late[3, :, :, :, :, 16:32, 0:128].astype(wide).reshape(-1, 16, 128)
    tail = dot_nt(both, spread).reshape(-1, 8, 128)
    block = jnp.concatenate([block[:, :8], tail], axis=1)
    late[3, :, :, :, :, 16:32, 0:128] = block.astype(low).reshape(nz, 2, 2, 2, 16, 128)
    begin(8)
    for _ in steps:
        pass
    share.finish(2)
    total = scatter[0]
    for u in range(len(units)):
        sums[u] = total[u, here.z, here.y, here.x].astype(wide)


def last_back(bounds, near, weights, text, early, units, perms, nz, depth=5):
    slots = make_schedule(perms, nz, lag=depth + 1, window=3)
    firsts = {}
    for t, slot in enumerate(slots[::-1]):
        for op in slot.values():
            firsts.setdefault(op[0], t)
    count, width = near[4].shape
    low, wide = jnp.bfloat16, jnp.float32
    vmem, any_ = pl.BlockSpec(memory_space=pltpu.VMEM), pl.BlockSpec(memory_space=pl.ANY)
    part = pltpu.VMEM((count, width), low)
    outs = [jax.ShapeDtypeStruct((count, width), low), jax.ShapeDtypeStruct((len(units),) + unit_shape(units), wide)]
    return pl.pallas_call(
        functools.partial(last_body, nz, units, slots, depth, firsts),
        out_shape=outs,
        in_specs=[pl.BlockSpec(memory_space=pltpu.SMEM)] + [vmem] * len(near) + [any_] * 9,
        out_specs=[vmem] * 2,
        scratch_shapes=[pltpu.VMEM(w.shape, low) for w in weights]
        + [pltpu.SemaphoreType.DMA((4,)), part]
        + [pltpu.VMEM((4, count, width), low)] * 2 + [pltpu.VMEM((2, count, width), low)] * 2 + [part] * 4
        + [pltpu.SemaphoreType.DMA((2, 2, 2))] * 2 + [pltpu.SemaphoreType.DMA((2, 2))] * 2
        + [pltpu.VMEM((4,) + text.shape, low), pltpu.VMEM((count, width), wide)]
        + scatter_scratch(units, slots, nz),
        compiler_params=pltpu.CompilerParams(collective_id=2, has_side_effects=True, vmem_limit_bytes=VMEM_LIMIT),
        name="last_back",
    )(bounds, *near, *weights, text, *early)


eps_norm = 1e-05


def layer_norm(values_in, gain_vec, shift_vec):
    centre = values_in - jnp.mean(values_in, axis=-1, keepdims=True)
    spread = jnp.mean(centre * centre, axis=-1, keepdims=True)
    return centre * lax.rsqrt(spread + eps_norm) * gain_vec + shift_vec


def gelu_exact(values_in):
    return jax.nn.gelu(values_in, approximate=False)


def project(left, right):
    return jnp.einsum("gti,ij->gtj", left, right, preferred_element_type=jnp.float32)


def project_back(left, right):
    return jnp.einsum("gtj,ij->gti", left, right, preferred_element_type=jnp.float32)


def outer_sum(left, right):
    return jnp.einsum("gti,gtj->ij", left, right, preferred_element_type=jnp.float32)


class Params(NamedTuple):
    w_query: jax.Array
    w_key: jax.Array
    w_value: jax.Array
    w_out: jax.Array
    c_query: jax.Array
    c_key: jax.Array
    c_value: jax.Array
    c_out: jax.Array
    w_text: jax.Array
    w_up: jax.Array
    w_down: jax.Array
    gain_attn: jax.Array
    bias_attn: jax.Array
    gain_cross: jax.Array
    bias_cross: jax.Array
    gain_feed: jax.Array
    bias_feed: jax.Array


BLOCKS, GAINS = 11, 6


def all_axes():
    return ("dp", "seq")


def fits(own, frames, text):
    rows, width = own.w_query.shape
    return (
        lax.axis_size("seq") == 4 and lax.axis_size("dp") % 2 == 0 and rows == 32 and width % 128 == 0
        and own.w_text.shape[0] % 8 == 0 and own.w_text.shape[0] + 8 == rows
        and own.w_up.shape[0] == rows and own.w_up.shape[1] % width == 0
        and own.w_down.shape == (own.w_up.shape[1] // width * rows, width) and own.w_down.shape[0] == 128
        and width == rows * lax.axis_size("dp") * 4
        and frames.shape[0] == 1 and frames.shape[1] % 32 == 0 and text.shape[0] == 1 and text.shape[1] % 128 == 0
    )


class PlainWires:
    def gather(self, own, frames):
        full = Params(*[lax.all_gather(v, all_axes(), axis=0, tiled=True) for v in own])
        return full, lax.all_gather(frames, "seq", axis=1, tiled=True)

    def scatter(self, grads):
        return Params(*[lax.psum_scatter(v, all_axes(), scatter_dimension=0, tiled=True) for v in grads])

    def share(self, arrays, number):
        return [lax.psum_scatter(a, "seq", scatter_dimension=1, tiled=True) for a in arrays]


def attention(causal, bounds, q, k, v):
    return attend(causal, bounds[0], q[0], k[0], v[0])[None]


def attention_back(causal, bounds, *operands):
    return [r[None] for r in attend_grads(causal, bounds[0], *[a[0] for a in operands])]


def plain_layer(own, frames, cotangent, text_states, frame_start, prompt_len):
    low = jnp.bfloat16
    wires = PlainWires()
    full, all_frames = wires.gather(own, frames)
    wide = [v.astype(jnp.float32) for v in full[BLOCKS:]]
    frames_f = frames.astype(jnp.float32)
    frame_count = frames.shape[1]
    normed, norm_one_back = jax.vjp(layer_norm, frames_f, wide[0], wide[1])
    normed_low = normed.astype(low)
    normed_all = layer_norm(all_frames.astype(jnp.float32), wide[0], wide[1]).astype(low)
    query_rows = project(normed_low, full.w_query).astype(low)
    key_all = project(normed_all, full.w_key).astype(low)
    value_all = project(normed_all, full.w_value).astype(low)
    rank = lax.axis_index("seq")
    self_bounds = jnp.stack([jnp.full_like(frame_start, rank * frame_count), frame_start], axis=1)
    attended = attention(True, self_bounds, query_rows, key_all, value_all)
    first = frames_f + project(attended, full.w_out)
    text_count = text_states.shape[1]
    quarter = text_count // lax.axis_size("seq")
    text_start = rank * quarter
    text_part = lax.dynamic_slice_in_dim(text_states, text_start, quarter, 1)
    proj_all = project(text_states, full.w_text).astype(low)
    cross_keys = project(proj_all, full.c_key).astype(low)
    cross_values = project(proj_all, full.c_value).astype(low)
    proj_part = lax.dynamic_slice_in_dim(proj_all, text_start, quarter, 1)
    normed_two, norm_two_back = jax.vjp(layer_norm, first, wide[2], wide[3])
    normed_two_low = normed_two.astype(low)
    cross_query = project(normed_two_low, full.c_query).astype(low)
    cross_bounds = jnp.stack([prompt_len, prompt_len], axis=1)
    cross_mix = attention(False, cross_bounds, cross_query, cross_keys, cross_values)
    second = first + project(cross_mix, full.c_out)
    normed_three, norm_three_back = jax.vjp(layer_norm, second, wide[4], wide[5])
    three_low = normed_three.astype(low)
    hidden = project(three_low, full.w_up)
    activated, gelu_back = jax.vjp(gelu_exact, hidden)
    act_low = activated.astype(low)
    block_out = (second + project(act_low, full.w_down)).astype(low)
    grad_act = project_back(cotangent, full.w_down)
    dw_down = outer_sum(act_low, cotangent)
    grad_hidden = gelu_back(grad_act)[0].astype(low)
    dw_up = outer_sum(three_low, grad_hidden)
    grad_second_ln, dgain_feed, dbias_feed = norm_three_back(project_back(grad_hidden, full.w_up))
    grad_second = cotangent.astype(jnp.float32) + grad_second_ln
    second_low = grad_second.astype(low)
    dc_out = outer_sum(cross_mix, second_low)
    grad_cross_mix = project_back(second_low, full.c_out).astype(low)
    cq_low, grad_ck, grad_cv = attention_back(
        False, cross_bounds, cross_query, cross_keys, cross_values, grad_cross_mix
    )
    ck_low, cv_low = wires.share([grad_ck, grad_cv], 3)
    dc_key = outer_sum(proj_part, ck_low)
    dc_value = outer_sum(proj_part, cv_low)
    grad_proj = (project_back(ck_low, full.c_key) + project_back(cv_low, full.c_value)).astype(low)
    dw_text = outer_sum(text_part, grad_proj)
    text_grad = project_back(grad_proj, full.w_text)
    dc_query = outer_sum(normed_two_low, cq_low)
    grad_first_ln, dgain_cross, dbias_cross = norm_two_back(project_back(cq_low, full.c_query))
    grad_first = grad_second + grad_first_ln
    first_low = grad_first.astype(low)
    dw_out = outer_sum(attended, first_low)
    grad_attended = project_back(first_low, full.w_out).astype(low)
    q_low, grad_k_all, grad_v_all = attention_back(
        True, self_bounds, query_rows, key_all, value_all, grad_attended
    )
    k_low, v_low = wires.share([grad_k_all, grad_v_all], 4)
    dw_query = outer_sum(normed_low, q_low)
    dw_key = outer_sum(normed_low, k_low)
    dw_value = outer_sum(normed_low, v_low)
    grad_normed = (
        project_back(q_low, full.w_query) + project_back(k_low, full.w_key) + project_back(v_low, full.w_value)
    )
    grad_frames_ln, dgain_attn, dbias_attn = norm_one_back(grad_normed)
    frames_grad = (grad_first + grad_frames_ln).astype(low)
    sums = wires.scatter(
        Params(
            dw_query, dw_key, dw_value, dw_out, dc_query, dc_key, dc_value, dc_out, dw_text, dw_up, dw_down,
            dgain_attn, dbias_attn, dgain_cross, dbias_cross, dgain_feed, dbias_feed,
        )
    )
    return (block_out, frames_grad, text_grad, *sums)


NEAR_ORDERS = ("zxy", "zyx", "zxy", "zxy", "zyx", "zxy", "xyz", "zxy", "zyx")
LATE_ORDERS = ("zyx", "yxz", "yxz", "zyx", "zxy", "zyx", "zyx", "xyz")
LAST_ORDERS = ("zyx", "zxy", "zyx", "xyz", "zxy", "zyx", "xzy", "zxy", "xyz")
FEED_ORDERS = ("zyx", "zxy", "zyx", "yxz", "zxy", "zyx", "xyz", "zxy")


def cycle(orders, n):
    return [orders[i % len(orders)] for i in range(n)]


def fast_layer(own, frames, cotangent, text_states, frame_start, prompt_len):
    low, wide = jnp.bfloat16, jnp.float32
    nz = lax.axis_size("dp") // 2
    shards = nz * 8
    rows, width = own.w_query.shape
    text_rows = own.w_text.shape[0]
    count = frames.shape[1]
    rank = lax.axis_index("seq")
    up, down = own.w_up.shape[1] // width, own.w_down.shape[0] // rows
    near_units = [(g, 0, rows, 0, width) for g in range(9)]
    up_units = [(9, 0, rows, k * width, width) for k in range(up)]
    down_units = [(10, k * rows, rows, 0, width) for k in range(down)]
    units = [near_units[i] for i in (8, 1, 2, 0, 5, 6, 3, 4, 7)] + down_units + up_units
    gains = jnp.stack(own[BLOCKS:])
    gains = jnp.pad(gains, ((0, rows - text_rows - GAINS), (0, width - gains.shape[1])))
    arrays = list(own[:BLOCKS])
    arrays[8] = jnp.concatenate([own.w_text, gains], axis=0)
    tokens = text_states.shape[1]
    text = jnp.pad(text_states.reshape((tokens, shards, text_rows)), ((0, 0), (0, 0), (0, rows - text_rows))).reshape((tokens, width))
    bounds = jnp.concatenate([jnp.full_like(frame_start, rank * count), frame_start, prompt_len])
    cot = cotangent[0]
    orders = cycle(NEAR_ORDERS, 9) + cycle(LATE_ORDERS, up + down)
    outs = ahead(bounds, frames[0], text, cot, arrays, units, orders, nz)
    full, (_, dw_up, dw_down) = [f.reshape((-1, f.shape[-1])) for f in outs[:BLOCKS]], outs[BLOCKS:BLOCKS + 3]
    (gains, normed_low, query_rows, key_all, value_all, attended, first, two_low, cross_query, cross_keys, cross_values,
     cross_mix, proj, block_out, grad_second, second_low, dgain_feed, dbias_feed) = outs[BLOCKS + 3:]
    quarter = tokens // 4
    near = [second_low, grad_second, cross_mix, cross_query, cross_keys, cross_values, two_low, first, text, proj, attended, gains[10:11]]
    weights = [full[i] for i in (7, 4, 5, 6, 8, 3)]
    lead = (nz, 2, 2, 2)
    feed = [v.reshape(lead + (-1, v.shape[-1])) for v in (dw_up, dw_down)]
    feed_units = [((g - 9, *rest),) for g, *rest in up_units + down_units]
    (dc_out, dc_query, dw_out, dc_key, dc_value, dw_text, text_grad, grad_first, grad_attended, dgain_cross, dbias_cross,
     feed_sums) = middle_back(bounds[2:], near, weights, feed, feed_units, cycle(FEED_ORDERS, up + down), nz)
    others = jnp.concatenate([dgain_cross, dbias_cross, dgain_feed, dbias_feed], axis=0)
    last = [query_rows, key_all, value_all, grad_attended, normed_low, frames[0], grad_first, gains[8:9], others]
    text_block, *early = [v.reshape(lead + (rows, width)) for v in (dw_text, dw_out, dc_query, dc_key, dc_value, dc_out)]
    last_units = [(near_units[i],) for i in (8, 2, 1, 0, 7, 6, 5, 4, 3)]
    frames_grad, sums = last_back(bounds[:2], last, full[:3], text_block, early, last_units, LAST_ORDERS, nz)
    shapes = [(rows, width)] * 9 + [own.w_up.shape, own.w_down.shape]
    feed_units = [((g + 9, *rest),) for ((g, *rest),) in feed_units]
    *blocks, tail = deliver((sums, feed_sums), (last_units, feed_units), text_rows, shapes)
    text_grad = text_grad.reshape((quarter, shards, rows))[:, :, :text_rows].reshape((1, quarter, -1))
    return (block_out[None], frames_grad[None], text_grad, *blocks, *[tail[i, : width // shards] for i in range(GAINS)])


def on_device(frames, cotangent, text_states, frame_start, prompt_len, *params):
    own = Params(*params)
    layer = fast_layer if fits(own, frames, text_states) else plain_layer
    return layer(own, frames, cotangent, text_states, frame_start, prompt_len)


def solution(mesh):
    both = P(all_axes(), None)
    rows, vector = P(*all_axes(), None), P(all_axes())
    item, whole = P("dp"), P("dp", None, None)
    return jax.shard_map(
        on_device,
        mesh=mesh,
        in_specs=(rows, rows, whole, item, item) + (both,) * BLOCKS + (vector,) * GAINS,
        out_specs=(rows,) * 3 + (both,) * BLOCKS + (vector,) * GAINS,
        check_vma=False,
    )
```
